32 devices in a mesh: dp: 4 (over y, x), grp: 8 (over z, core).
Axes of the slice: x: 2, y: 2, z: 4, core: 2. Of those that a mesh axis runs over, the one named last changes fastest.
Arguments:
- layer_input: bfloat16 [4, 2048, 2048], P('dp', 'grp'), may hold values from -6 to 6
- out_cotangent: bfloat16 [4, 2048, 2048], P('dp', 'grp'), may hold values from -6 to 6
- seq_lengths: int32 [4], P('dp'), may hold values from 1024 to 2048, as said below
- block_owner: int32 [168], replicated, may hold values from 0 to 7, as said below
- weight_master: float32 [192, 128, 2048], P('grp'), as said below
- weight_first: float32 [192, 128, 2048], P('grp')
- weight_second: float32 [192, 128, 2048], P('grp')
- gain_master: float32 [2, 2048], P(None, 'grp'), may hold values from 0.5 to 1.5
- gain_first: float32 [2, 2048], P(None, 'grp')
- gain_second: float32 [2, 2048], P(None, 'grp')
Outputs:
- layer_output: bfloat16 [4, 2048, 2048], P('dp', 'grp')
- input_grad: bfloat16 [4, 2048, 2048], P('dp', 'grp')
- new_master: float32 [192, 128, 2048], P('grp')
- new_first: float32 [192, 128, 2048], P('grp')
- new_second: float32 [192, 128, 2048], P('grp')
- weight_copy: bfloat16 [192, 128, 2048], P('grp')
- new_gain: float32 [2, 2048], P(None, 'grp')
- new_gain_first: float32 [2, 2048], P(None, 'grp')
- new_gain_second: float32 [2, 2048], P(None, 'grp')
The draws below stay inside these ranges and needn't reach their ends.
Inputs may be any that keep to these rules, and one draw needn't show every extreme that they name: `seq_lengths`: each index of dp holds 1 sequence; one of them, drawn from the seed, has length exactly 2048. `block_owner`: each index of grp owns at most 24 blocks, and one owns exactly 24. `weight_master`: slots that hold no block carry values as well.
All inputs are finite; a program needn't handle non-finite values.
Results may differ from the reference program's by a relative error of at most 0.023.
Values may be sent and summed in bfloat16 or wider, within the bound.
No kernel may reach another device: no remote copies, remote signals or barrier semaphores. Data moves between devices by JAX's collectives and lax.ppermute only.
A program may use at most 640 MiB of HBM per device.

```python
import math
import jax
import jax.numpy as jnp
from jax import lax

D = 2048
QUERY_HEADS = 32
KEY_VALUE_HEADS = 4
HEAD_WIDTH = 64
FF = 5632
ROW_LENGTH = 2048
LMIN = 1024
R = 128
STEP = 7
KEY_VALUE_WIDTH = 256
SEQ_DEV = 1
SEQS = 4
BLOCKS = 168
SLOTS = 24
N_GRP = 8


def owner_table(key):
    key = jax.random.fold_in(key, 101)
    key_busy, key_spots, key_order = jax.random.split(key, 3)
    busiest = jax.random.randint(key_busy, (), 0, N_GRP).astype(jnp.int32)
    spots = jax.random.permutation(key_spots, (N_GRP - 1) * SLOTS)[:BLOCKS - SLOTS].astype(jnp.int32)
    others = spots // SLOTS
    others = others + (others >= busiest).astype(jnp.int32)
    listing = jnp.concatenate([jnp.zeros((SLOTS,), jnp.int32) + busiest, others])
    shuffle = jax.random.permutation(key_order, BLOCKS).astype(jnp.int32)
    return listing[shuffle].astype(jnp.int32)


def slot_kinds(key):
    owners = owner_table(key)
    block_order = jnp.arange(BLOCKS, dtype=jnp.int32)
    same_owner = owners[:, None] == owners[None, :]
    earlier = block_order[None, :] < block_order[:, None]
    ranking = jnp.sum((same_owner & earlier).astype(jnp.int32), axis=1)
    placing = owners * SLOTS + ranking
    model_blocks = D // R
    kv_blocks = KEY_VALUE_WIDTH // R
    ff_blocks = FF // R
    edges = [model_blocks, model_blocks + kv_blocks, model_blocks + 2 * kv_blocks, 2 * model_blocks + 2 * kv_blocks, 2 * model_blocks + 2 * kv_blocks + ff_blocks, 2 * model_blocks + 2 * kv_blocks + 2 * ff_blocks]
    kind_block = jnp.zeros((BLOCKS,), jnp.int32)
    for edge in edges:
        kind_block = kind_block + (block_order >= edge).astype(jnp.int32)
    return jnp.full((SLOTS * N_GRP,), 7, jnp.int32).at[placing].set(kind_block)


def weight_scales():
    model_scale = D ** (-0.5)
    return [model_scale, model_scale, model_scale, math.sqrt(ROW_LENGTH / (32.0 * D)), model_scale, model_scale, FF ** (-0.5), model_scale]


def gradient_scales():
    rooted = math.sqrt(SEQS * (LMIN + ROW_LENGTH) / 2.0)
    return [rooted * factor for factor in [0.9, 2.5, 2.5, 1.27 * math.sqrt(16.0 / ROW_LENGTH), 0.3, 0.36, 0.6, 0.5]]


def draw_seq_lengths(key, part):
    key = jax.random.fold_in(key, 13)
    key_lengths, key_pick = jax.random.split(key)
    lengths = jax.random.randint(key_lengths, (SEQS,), LMIN, ROW_LENGTH + 1)
    picked = jax.random.randint(key_pick, (SEQS // SEQ_DEV,), 0, SEQ_DEV)
    order = jnp.arange(SEQS, dtype=jnp.int32)
    longest = order % SEQ_DEV == picked[order // SEQ_DEV]
    return jnp.where(longest, ROW_LENGTH, lengths).astype(jnp.int32)


def draw_block_owner(key, part):
    return owner_table(key)


def draw_weight_master(key, part):
    slot_kind = slot_kinds(key)
    key = jax.random.fold_in(key, 3)
    scaling = jnp.array(weight_scales(), jnp.float32)[slot_kind][:, None, None]
    base = jnp.clip(jax.random.normal(key, (SLOTS * N_GRP, R, D), jnp.float32), -4.0, 4.0)
    return base * scaling


def draw_weight_first(key, part):
    slot_kind = slot_kinds(key)
    key = jax.random.fold_in(key, 5)
    scaling = jnp.array(gradient_scales(), jnp.float32)[slot_kind][:, None, None] / 9.0
    base = jnp.clip(jax.random.normal(key, (SLOTS * N_GRP, R, D), jnp.float32), -4.0, 4.0)
    return base * scaling


def draw_weight_second(key, part):
    slot_kind = slot_kinds(key)
    key = jax.random.fold_in(key, 7)
    sizes_grad = jnp.array(gradient_scales(), jnp.float32)[slot_kind][:, None, None]
    factor = jnp.exp(jax.random.uniform(key, (SLOTS * N_GRP, R, D), jnp.float32, 0.0, math.log(4.0)))
    return sizes_grad * sizes_grad * factor / 19.0


def gain_scales():
    rooted = math.sqrt(SEQS * (LMIN + ROW_LENGTH) / 2.0)
    return jnp.array([[1.5 * rooted], [0.8 * rooted]], jnp.float32)


def draw_gain_first(key, part):
    key = jax.random.fold_in(key, 17)
    base = jnp.clip(jax.random.normal(key, (2, D), jnp.float32), -4.0, 4.0)
    return base * gain_scales() / 9.0


def draw_gain_second(key, part):
    key = jax.random.fold_in(key, 19)
    scaling = gain_scales()
    factor = jnp.exp(jax.random.uniform(key, (2, D), jnp.float32, 0.0, math.log(4.0)))
    return scaling * scaling * factor / 19.0


def levels(stream_key, extent, shards, smallest, high):
    def one(dim, blocks):
        steps = jax.random.uniform(jax.random.fold_in(jax.random.fold_in(stream_key, 6), dim), (blocks,), jnp.float32, smallest / len(shards), high / len(shards))
        return jnp.repeat(jnp.exp(steps), extent[dim] // blocks).reshape((-1,) + (1,) * (len(extent) - dim - 1))

    level = one(*shards[0])
    for cut in shards[1:]:
        level = level * one(*cut)
    return level


def noise(rng, dims, scale, reach, cuts=(), kind=jnp.bfloat16):
    values = jax.random.normal(rng, dims, jnp.float32) * scale
    if len(cuts) > 0:
        values = levels(rng, dims, cuts, -0.22, 0.18) * values
    return jnp.clip(values, min=-reach, max=reach).astype(kind)


def setup_inputs(seed: int = 0) -> dict:
    arg_keys = jax.random.split(jax.random.key(seed), 11)
    return {
        "layer_input": noise(arg_keys[0], (SEQS, ROW_LENGTH, D), 1.0, 6.0, ((0, 4), (1, 8))),
        "out_cotangent": noise(arg_keys[1], (SEQS, ROW_LENGTH, D), 1.0, 6.0, ((0, 4), (1, 8))),
        "seq_lengths": draw_seq_lengths(jax.random.fold_in(arg_keys[10], 71), 0),
        "block_owner": draw_block_owner(jax.random.fold_in(arg_keys[10], 71), 0),
        "weight_master": draw_weight_master(jax.random.fold_in(arg_keys[10], 71), 0),
        "weight_first": draw_weight_first(jax.random.fold_in(arg_keys[10], 71), 0),
        "weight_second": draw_weight_second(jax.random.fold_in(arg_keys[10], 71), 0),
        "gain_master": jnp.clip(1.0 + 0.1 * jax.random.normal(arg_keys[7], (2, D), jnp.float32), 0.5, 1.5),
        "gain_first": draw_gain_first(jax.random.fold_in(arg_keys[10], 71), 0),
        "gain_second": draw_gain_second(jax.random.fold_in(arg_keys[10], 71), 0),
    }


NORM_EPS = 1e-05
BETA_ONE = 0.9
BETA_TWO = 0.95
ADAM_EPS = 1e-08
WEIGHT_RATE = 0.1
GAIN_RATE = 0.5
WEIGHT_DECAY = 0.1
MASKED = -1e+30
HIGH = lax.Precision.HIGHEST

@jax.custom_vjp
def reduced_precision(v):
    return lax.optimization_barrier(v.astype(jnp.bfloat16)).astype(jnp.float32)

@jax.custom_vjp
def low_back(v):
    return v

def low_keep(v):
    return (reduced_precision(v), None)

def low_pass(kept, grad):
    return (grad,)

def back_keep(v):
    return (v, None)

def back_low(kept, grad):
    return (reduced_precision(grad),)
reduced_precision.defvjp(low_keep, low_pass)
low_back.defvjp(back_keep, back_low)

def owner_slots(block_owner):
    block_order = jnp.arange(block_owner.shape[0], dtype=jnp.int32)
    same_owner = block_owner[:, None] == block_owner[None, :]
    earlier = block_order[None, :] < block_order[:, None]
    ranking = lax.optimization_barrier(jnp.sum((same_owner & earlier).astype(jnp.int32), axis=1))
    return (block_owner * SLOTS + ranking).astype(jnp.int32)

def split_weights(blocks):
    model_blocks = D // R
    kv_blocks = KEY_VALUE_WIDTH // R
    ff_blocks = FF // R
    counts_list = [model_blocks, kv_blocks, kv_blocks, model_blocks, ff_blocks, ff_blocks, ff_blocks]
    shapes_list = [(D, D), (KEY_VALUE_WIDTH, D), (KEY_VALUE_WIDTH, D), (D, D), (FF, D), (FF, D), (FF, D)]
    pieces = []
    offset = 0
    for amount, target in zip(counts_list, shapes_list):
        pieces.append(blocks[offset:offset + amount].reshape(target))
        offset = offset + amount
    return pieces

def rotary_tables(positions, head_size):
    halfway = head_size // 2
    spacing = jnp.arange(halfway, dtype=jnp.float32) * (-2.0 * math.log(10000.0) / head_size)
    angles = positions.astype(jnp.float32)[:, None] * jnp.exp(spacing)[None, :]
    return (jnp.cos(angles), jnp.sin(angles))

def apply_rotation(values, cosine_rows, sine_rows):
    halfway = values.shape[-1] // 2
    leading = values[..., :halfway]
    trailing = values[..., halfway:]
    cos_rows = cosine_rows[:, None, :]
    sin_rows = sine_rows[:, None, :]
    return jnp.concatenate([leading * cos_rows - trailing * sin_rows, trailing * cos_rows + leading * sin_rows], axis=-1)

def attend(queries, rotated_keys, reduced_values, length):
    heads_per_group = QUERY_HEADS // KEY_VALUE_HEADS
    key_head_rows = jnp.repeat(rotated_keys, heads_per_group, axis=1)
    value_head_rows = jnp.repeat(reduced_values, heads_per_group, axis=1)
    block_rows = min(512, ROW_LENGTH)
    key_slots = jnp.arange(ROW_LENGTH, dtype=jnp.int32)
    score_scale = 1.0 / math.sqrt(HEAD_WIDTH)

    @jax.checkpoint
    def one_block(packed):
        query_block, first_row = packed
        row_slots = first_row + jnp.arange(block_rows, dtype=jnp.int32)
        raw_scores = low_back(jnp.einsum('qhd,khd->hqk', query_block, key_head_rows, precision=HIGH))
        allowed = (key_slots[None, :] <= row_slots[:, None]) & (key_slots[None, :] < length)
        scores = jnp.where(allowed[None], raw_scores * score_scale, MASKED)
        row_peak = lax.optimization_barrier(jnp.max(scores, axis=-1, keepdims=True))
        exponent = jnp.exp(scores - row_peak)
        soft_weights = exponent / lax.optimization_barrier(jnp.sum(exponent, axis=-1, keepdims=True))
        return jnp.einsum('hqk,khd->qhd', reduced_precision(soft_weights), value_head_rows, precision=HIGH)
    starts = jnp.arange(ROW_LENGTH // block_rows, dtype=jnp.int32) * block_rows
    mixture = lax.map(one_block, (queries.reshape(ROW_LENGTH // block_rows, block_rows, QUERY_HEADS, HEAD_WIDTH), starts))
    return mixture.reshape(ROW_LENGTH, QUERY_HEADS, HEAD_WIDTH)

def forward(master, gains, inputs, lengths, slot_of_block):
    w_query, w_key, w_value, w_out, w_gate, w_up, w_down = split_weights(reduced_precision(master)[slot_of_block])
    gain_low = reduced_precision(gains)
    paired_halves = inputs.shape[0]
    positions = jnp.arange(ROW_LENGTH, dtype=jnp.int32)
    valid_rows = positions[None, :] < lengths[:, None]
    cosine_rows, sine_rows = rotary_tables(positions, HEAD_WIDTH)
    root_one = lax.rsqrt(lax.optimization_barrier(jnp.mean(inputs * inputs, axis=-1, keepdims=True)) + NORM_EPS)
    normed_one = inputs * root_one
    hidden_one = reduced_precision(normed_one * gain_low[0])
    query_proj = low_back(jnp.einsum('spd,de->spe', hidden_one, w_query, precision=HIGH))
    key_projection = low_back(jnp.einsum('spd,ed->spe', hidden_one, w_key, precision=HIGH))
    value_projection = low_back(jnp.einsum('spd,ed->spe', hidden_one, w_value, precision=HIGH))
    queries = reduced_precision(apply_rotation(query_proj.reshape(paired_halves, ROW_LENGTH, QUERY_HEADS, HEAD_WIDTH), cosine_rows, sine_rows))
    rotated_keys = reduced_precision(apply_rotation(key_projection.reshape(paired_halves, ROW_LENGTH, KEY_VALUE_HEADS, HEAD_WIDTH), cosine_rows, sine_rows))
    reduced_values = reduced_precision(value_projection.reshape(paired_halves, ROW_LENGTH, KEY_VALUE_HEADS, HEAD_WIDTH))
    attended = jnp.stack([attend(queries[index], rotated_keys[index], reduced_values[index], lengths[index]) for index in range(paired_halves)])
    attended = reduced_precision(low_back(attended.reshape(paired_halves, ROW_LENGTH, D)))
    residual = inputs + low_back(jnp.einsum('spd,de->spe', attended, w_out, precision=HIGH))
    root_two = lax.rsqrt(lax.optimization_barrier(jnp.mean(residual * residual, axis=-1, keepdims=True)) + NORM_EPS)
    normed_two = residual * root_two
    hidden_two = reduced_precision(normed_two * gain_low[1])
    gate_pre = low_back(jnp.einsum('spd,fd->spf', hidden_two, w_gate, precision=HIGH))
    up_pre = low_back(jnp.einsum('spd,fd->spf', hidden_two, w_up, precision=HIGH))
    inner = reduced_precision(gate_pre * jax.nn.sigmoid(gate_pre) * up_pre)
    output = residual + jnp.einsum('spf,fd->spd', inner, w_down, precision=HIGH)
    return jnp.where(valid_rows[:, :, None], output, 0.0)

def adamw(master, first, second, gradient, rate, decay):
    first_new = BETA_ONE * first + (1.0 - BETA_ONE) * gradient
    second_new = BETA_TWO * second + (1.0 - BETA_TWO) * gradient * gradient
    first_fix = 1.0 - BETA_ONE ** STEP
    second_fix = 1.0 - BETA_TWO ** STEP
    stepped = first_new / first_fix / (jnp.sqrt(second_new / second_fix) + ADAM_EPS)
    return (master - rate * (stepped + decay * master), first_new, second_new)

def reference(layer_input, out_cotangent, seq_lengths, block_owner, weight_master, weight_first, weight_second, gain_master, gain_first, gain_second):
    slot_of_block = owner_slots(block_owner)
    pair_count = SEQS // 2
    inputs_all = layer_input.astype(jnp.float32).reshape(pair_count, 2, ROW_LENGTH, D)
    cotangents = out_cotangent.astype(jnp.float32).reshape(pair_count, 2, ROW_LENGTH, D)
    lengths_all = seq_lengths.reshape(pair_count, 2)

    def one_pair(totals, batch):
        pair_input, pair_cotangent, pair_lengths = batch

        def apply_layer(master, gains, values_in):
            return forward(master, gains, values_in, pair_lengths, slot_of_block)
        output, pullback = jax.vjp(apply_layer, weight_master, gain_master, pair_input)
        grad_master, grad_gain, grad_input = pullback(pair_cotangent)
        return ((totals[0] + grad_master, totals[1] + grad_gain), (output, grad_input))
    initial = (jnp.zeros_like(weight_master), jnp.zeros_like(gain_master))
    (slot_grad, gain_grad), (outputs, input_grads) = lax.scan(one_pair, initial, (inputs_all, cotangents, lengths_all))
    new_master, new_first, new_second = adamw(weight_master, weight_first, weight_second, slot_grad, WEIGHT_RATE, WEIGHT_DECAY)
    new_gain, new_gain_first, new_gain_second = adamw(gain_master, gain_first, gain_second, gain_grad, GAIN_RATE, 0.0)
    layer_output = outputs.reshape(SEQS, ROW_LENGTH, D).astype(jnp.bfloat16)
    input_grad = input_grads.reshape(SEQS, ROW_LENGTH, D).astype(jnp.bfloat16)
    return (layer_output, input_grad, new_master, new_first, new_second, new_master.astype(jnp.bfloat16), new_gain, new_gain_first, new_gain_second)
```

```python
import functools
import math

import jax
import jax.numpy as jnp
from jax import lax
from jax.experimental import pallas as pl
from jax.experimental.pallas import tpu as pltpu
from jax.sharding import PartitionSpec as P

D = 2048
QUERY_HEADS = 32
KEY_VALUE_HEADS = 4
HEAD_WIDTH = 64
FF = 5632
ROW_LENGTH = 2048
R = 128
STEP = 7
KEY_VALUE_WIDTH = 256
MODEL_BLOCKS = D // R
KV_BLOCKS = KEY_VALUE_WIDTH // R
FF_BLOCKS = FF // R
KEY_AT = MODEL_BLOCKS
OUT_AT = MODEL_BLOCKS + 2 * KV_BLOCKS
GATE_AT = OUT_AT + MODEL_BLOCKS
UP_AT = GATE_AT + FF_BLOCKS
DOWN_AT = UP_AT + FF_BLOCKS
BLOCKS = DOWN_AT + FF_BLOCKS

NORM_EPS = 1e-05
BETA_ONE = 0.9
BETA_TWO = 0.95
ADAM_EPS = 1e-08
WEIGHT_RATE = 0.1
GAIN_RATE = 0.5
WEIGHT_DECAY = 0.1
MASKED = -1e30
LOW = jnp.bfloat16
FULL = jnp.float32


def rotary_tables(positions, head_size):
    halfway = head_size // 2
    spacing = jnp.arange(halfway, dtype=FULL) * (-2.0 * math.log(10000.0) / head_size)
    angles = positions.astype(FULL)[:, None] * jnp.exp(spacing)[None, :]
    return (jnp.cos(angles), jnp.sin(angles))


def apply_rotation(values, cosine_rows, sine_rows):
    halfway = values.shape[-1] // 2
    leading = values[..., :halfway]
    trailing = values[..., halfway:]
    cos_rows = cosine_rows[:, None, :]
    sin_rows = sine_rows[:, None, :]
    return jnp.concatenate(
        [leading * cos_rows - trailing * sin_rows, trailing * cos_rows + leading * sin_rows],
        axis=-1,
    )


def contract_rows(left, right):
    return lax.dot_general(left, right, (((1,), (1,)), ((), ())), preferred_element_type=FULL)


def contract_first(left, right):
    return lax.dot_general(left, right, (((0,), (0,)), ((), ())), preferred_element_type=FULL)


def plain_dot(left, right):
    return jnp.dot(left, right, preferred_element_type=FULL)


def adamw(master, first, second, gradient, rate, decay):
    first_new = BETA_ONE * first + (1.0 - BETA_ONE) * gradient
    second_new = BETA_TWO * second + (1.0 - BETA_TWO) * gradient * gradient
    first_fix = 1.0 - BETA_ONE**STEP
    second_fix = 1.0 - BETA_TWO**STEP
    stepped = first_new / first_fix / (jnp.sqrt(second_new / second_fix) + ADAM_EPS)
    return (master - rate * (stepped + decay * master), first_new, second_new)


KEY_CHUNK = 256
GROUP_WIDTH = D // KEY_VALUE_HEADS
PAIRS = GROUP_WIDTH // 128
EXP_SCALE = math.log2(math.e) / math.sqrt(HEAD_WIDTH)


def lanes_of(shape):
    return lax.broadcasted_iota(jnp.int32, shape, len(shape) - 1)


def swap_halves(values):
    first = (lanes_of(values.shape) % HEAD_WIDTH) < HEAD_WIDTH // 2
    return jnp.where(first, pltpu.roll(values, 96, 1), pltpu.roll(values, 32, 1))


def turn(values, cosine, sine):
    return values * cosine + swap_halves(values) * sine


def chunk_bounds(where_ref):
    start, rows, length = where_ref[0], where_ref[1], where_ref[2 + pl.program_id(0)]
    free = jnp.minimum(start // KEY_CHUNK, length // KEY_CHUNK)
    last = jnp.minimum(start + rows, length)
    return free, (last + KEY_CHUNK - 1) // KEY_CHUNK, start, length


def chunk_rows(spots_ref, chunk):
    return pl.ds(pl.multiple_of(spots_ref[chunk] * KEY_CHUNK, KEY_CHUNK), KEY_CHUNK)


def stacked(block, odd):
    wide = block.astype(FULL)
    wide = jnp.where(odd, pltpu.roll(wide, 64, 1), wide)
    low = jnp.where(lanes_of(wide.shape) < HEAD_WIDTH, wide, 0.0)
    return jnp.concatenate([low, pltpu.roll(low, 64, 1)], axis=0)


def mask_of(chunk, start, length, queries):
    keys = chunk * KEY_CHUNK + lax.broadcasted_iota(jnp.int32, (KEY_CHUNK, queries), 0)
    places = start + lax.broadcasted_iota(jnp.int32, (KEY_CHUNK, queries), 1)
    allowed = (keys <= places) & (keys < length)
    return jnp.concatenate([allowed, allowed], axis=0)


def across(left, right):
    return lax.dot_general(left, right, (((1,), (1,)), ((), ())), preferred_element_type=FULL)


def attend_forward_kernel(
    where_ref, spots_ref, cos_ref, sin_ref, q_ref, k_ref, v_ref, out_ref, log_ref, turned, peaks, sums, totals
):
    queries = q_ref.shape[1]
    odd = (pl.program_id(1) % 2) == 1
    free, end, start, length = chunk_bounds(where_ref)
    for pair in range(PAIRS):
        lanes = slice(128 * pair, 128 * pair + 128)
        turned[:, lanes] = turn(q_ref[0, :, lanes].astype(FULL), cos_ref[...], sin_ref[...]).astype(LOW)
    peaks[...] = jnp.full(peaks.shape, MASKED, FULL)
    sums[...] = jnp.zeros(sums.shape, FULL)
    totals[...] = jnp.zeros(totals.shape, FULL)

    def step(chunk, masked):
        rows = chunk_rows(spots_ref, chunk)
        keys = stacked(k_ref[0, rows, :], odd).astype(LOW)
        values = stacked(v_ref[0, rows, :], odd).T.astype(LOW)
        allowed = mask_of(chunk, start, length, queries) if masked else None
        for pair in range(PAIRS):
            scores = across(keys, turned[:, 128 * pair : 128 * pair + 128]) * EXP_SCALE
            if masked:
                scores = jnp.where(allowed, scores, MASKED)
            weights, fades = [], []
            for side in range(2):
                head = slice(2 * pair + side, 2 * pair + side + 1)
                part = scores[side * KEY_CHUNK : (side + 1) * KEY_CHUNK]
                old = peaks[head, :]
                new = jnp.maximum(old, jnp.max(part, axis=0, keepdims=True))
                weight = jnp.exp2(part - new)
                fade = jnp.exp2(old - new)
                peaks[head, :] = new
                sums[head, :] = sums[head, :] * fade + jnp.sum(weight, axis=0, keepdims=True)
                weights.append(weight.astype(LOW))
                fades.append(jnp.broadcast_to(fade, (HEAD_WIDTH, queries)))
            mixed = jnp.dot(values, jnp.concatenate(weights, axis=0), preferred_element_type=FULL)
            totals[pair] = totals[pair] * jnp.concatenate(fades, axis=0) + mixed

    @pl.loop(0, free)
    def _(chunk):
        step(chunk, False)

    @pl.loop(free, end)
    def _(chunk):
        step(chunk, True)

    for pair in range(PAIRS):
        shares = [
            jnp.broadcast_to(1.0 / sums[2 * pair + side : 2 * pair + side + 1, :], (HEAD_WIDTH, queries))
            for side in range(2)
        ]
        mixed = totals[pair] * jnp.concatenate(shares, axis=0)
        out_ref[0, :, 128 * pair : 128 * pair + 128] = mixed.T.astype(LOW)
    log_ref[0] = peaks[...] + jnp.log2(sums[...])


def attend_backward_kernel(
    where_ref, spots_ref, cos_ref, sin_ref, q_ref, k_ref, v_ref, out_ref, grad_ref, log_ref,
    dq_ref, dkv_ref, turned, dots, turning, key_sums, value_sums,
):
    queries = q_ref.shape[1]
    group = pl.program_id(1)
    odd = (group % 2) == 1
    free, end, start, length = chunk_bounds(where_ref)
    for pair in range(PAIRS):
        lanes = slice(128 * pair, 128 * pair + 128)
        turned[:, lanes] = turn(q_ref[0, :, lanes].astype(FULL), cos_ref[...], sin_ref[...]).astype(LOW)
        products = (out_ref[0, :, lanes].astype(FULL) * grad_ref[0, :, lanes].astype(FULL)).T
        dots[2 * pair : 2 * pair + 1, :] = jnp.sum(products[:HEAD_WIDTH], axis=0, keepdims=True)
        dots[2 * pair + 1 : 2 * pair + 2, :] = jnp.sum(products[HEAD_WIDTH:], axis=0, keepdims=True)
    turning[...] = jnp.zeros(turning.shape, FULL)

    @pl.when(group == 0)
    def _():
        dkv_ref[...] = jnp.zeros(dkv_ref.shape, LOW)

    key_lanes = pl.ds(pl.multiple_of((group // 2) * 128, 128), 128)
    value_lanes = pl.ds(pl.multiple_of(KEY_VALUE_WIDTH + (group // 2) * 128, 128), 128)

    def step(chunk, masked):
        rows = chunk_rows(spots_ref, chunk)
        wide_keys = stacked(k_ref[0, rows, :], odd)
        keys = wide_keys.astype(LOW)
        keys_down = wide_keys.T.astype(LOW)
        values = stacked(v_ref[0, rows, :], odd).astype(LOW)
        allowed = mask_of(chunk, start, length, queries) if masked else None
        for pair in range(PAIRS):
            lanes = slice(128 * pair, 128 * pair + 128)
            asked = turned[:, lanes]
            given = grad_ref[0, :, lanes]
            scores = across(keys, asked) * EXP_SCALE
            if masked:
                scores = jnp.where(allowed, scores, MASKED)
            slopes = across(values, given)
            weights, moves = [], []
            for side in range(2):
                head = slice(2 * pair + side, 2 * pair + side + 1)
                part = slice(side * KEY_CHUNK, (side + 1) * KEY_CHUNK)
                weight = jnp.exp2(scores[part] - log_ref[0, head, :])
                weights.append(weight.astype(LOW))
                moves.append((weight * (slopes[part] - dots[head, :])).astype(LOW))
            weights = jnp.concatenate(weights, axis=0)
            moves = jnp.concatenate(moves, axis=0)
            value_part = jnp.dot(weights, given, preferred_element_type=FULL)
            key_part = jnp.dot(moves, asked, preferred_element_type=FULL)
            if pair == 0:
                value_sums[...] = value_part
                key_sums[...] = key_part
            else:
                value_sums[...] += value_part
                key_sums[...] += key_part
            turning[pair] += jnp.dot(keys_down, moves, preferred_element_type=FULL)
        for sums, lanes, scale in (
            (key_sums, key_lanes, 1.0 / math.sqrt(HEAD_WIDTH)),
            (value_sums, value_lanes, 1.0),
        ):
            both = (sums[:KEY_CHUNK] + pltpu.roll(sums[KEY_CHUNK:], 64, 1)) * scale
            low_side = lanes_of(both.shape) < HEAD_WIDTH
            kept = dkv_ref[0, rows, lanes].astype(FULL)
            mine = jnp.where(odd, pltpu.roll(both, 64, 1), both)
            dkv_ref[0, rows, lanes] = jnp.where(low_side != odd, mine, kept).astype(LOW)

    @pl.loop(0, free)
    def _(chunk):
        step(chunk, False)

    @pl.loop(free, end)
    def _(chunk):
        step(chunk, True)

    for pair in range(PAIRS):
        back = turning[pair].T * (1.0 / math.sqrt(HEAD_WIDTH))
        dq_ref[0, :, 128 * pair : 128 * pair + 128] = turn(back, cos_ref[...], -sin_ref[...]).astype(LOW)


def attention_specs(sequences, rows, row_length):
    q_spec = pl.BlockSpec((1, rows, GROUP_WIDTH), lambda s, g, w, t: (s, 0, g))
    k_spec = pl.BlockSpec((1, row_length, 128), lambda s, g, w, t: (s, 0, g // 2))
    v_spec = pl.BlockSpec((1, row_length, 128), lambda s, g, w, t: (s, 0, 2 + g // 2))
    table_spec = pl.BlockSpec((rows, 128), lambda s, g, w, t: (0, 0))
    log_spec = pl.BlockSpec((1, 2 * PAIRS, rows), lambda s, g, w, t: (s, g, 0))
    return q_spec, k_spec, v_spec, table_spec, log_spec


def attend_forward(places, spots, cosine, sine, query_proj, kv_all):
    sequences, rows, _ = query_proj.shape
    row_length = kv_all.shape[1]
    q_spec, k_spec, v_spec, table_spec, log_spec = attention_specs(sequences, rows, row_length)
    pairs = sequences * QUERY_HEADS * rows * row_length
    return pl.pallas_call(
        attend_forward_kernel,
        grid_spec=pltpu.PrefetchScalarGridSpec(
            num_scalar_prefetch=2,
            grid=(sequences, KEY_VALUE_HEADS),
            in_specs=[table_spec, table_spec, q_spec, k_spec, v_spec],
            out_specs=[q_spec, log_spec],
            scratch_shapes=[
                pltpu.VMEM((rows, GROUP_WIDTH), LOW),
                pltpu.VMEM((2 * PAIRS, rows), FULL),
                pltpu.VMEM((2 * PAIRS, rows), FULL),
                pltpu.VMEM((PAIRS, 128, rows), FULL),
            ],
        ),
        out_shape=[
            jax.ShapeDtypeStruct(query_proj.shape, LOW),
            jax.ShapeDtypeStruct((sequences, QUERY_HEADS, rows), FULL),
        ],
        compiler_params=pltpu.CompilerParams(vmem_limit_bytes=40 * 1024 * 1024),
        cost_estimate=pl.CostEstimate(
            flops=4 * HEAD_WIDTH * pairs, bytes_accessed=8 * 1024 * 1024, transcendentals=pairs
        ),
        name="attend_forward",
    )(places, spots, cosine, sine, query_proj, kv_all, kv_all)


def attend_backward(places, spots, cosine, sine, query_proj, kv_all, attended, grad_attended, logs):
    sequences, rows, _ = query_proj.shape
    row_length = kv_all.shape[1]
    q_spec, k_spec, v_spec, table_spec, log_spec = attention_specs(sequences, rows, row_length)
    pairs = sequences * QUERY_HEADS * rows * row_length
    return pl.pallas_call(
        attend_backward_kernel,
        grid_spec=pltpu.PrefetchScalarGridSpec(
            num_scalar_prefetch=2,
            grid=(sequences, KEY_VALUE_HEADS),
            in_specs=[table_spec, table_spec, q_spec, k_spec, v_spec, q_spec, q_spec, log_spec],
            out_specs=[
                q_spec,
                pl.BlockSpec((1, row_length, 2 * KEY_VALUE_WIDTH), lambda s, g, w, t: (s, 0, 0)),
            ],
            scratch_shapes=[
                pltpu.VMEM((rows, GROUP_WIDTH), LOW),
                pltpu.VMEM((2 * PAIRS, rows), FULL),
                pltpu.VMEM((PAIRS, 128, rows), FULL),
                pltpu.VMEM((2 * KEY_CHUNK, 128), FULL),
                pltpu.VMEM((2 * KEY_CHUNK, 128), FULL),
            ],
        ),
        out_shape=[
            jax.ShapeDtypeStruct(query_proj.shape, LOW),
            jax.ShapeDtypeStruct((sequences, row_length, 2 * KEY_VALUE_WIDTH), LOW),
        ],
        compiler_params=pltpu.CompilerParams(vmem_limit_bytes=40 * 1024 * 1024),
        cost_estimate=pl.CostEstimate(
            flops=10 * HEAD_WIDTH * pairs, bytes_accessed=12 * 1024 * 1024, transcendentals=pairs
        ),
        name="attend_backward",
    )(places, spots, cosine, sine, query_proj, kv_all, kv_all, attended, grad_attended, logs)


def swap_dp(value, distance):
    size = lax.axis_size("dp")
    return lax.ppermute(value, "dp", [(a, a ^ distance) for a in range(size)])


def part_members():
    size = lax.axis_size("dp")
    rank = lax.axis_index("dp")
    return [rank ^ d if size == 4 else jnp.int32(d) for d in range(size)]


def gather_parts(value):
    size = lax.axis_size("dp")
    if size != 4:
        whole = lax.all_gather(value, "dp", axis=0)
        return [whole[d] for d in range(size)]
    near = swap_dp(value, 1)
    far = swap_dp(value, 2)
    half = value.shape[0] // 2
    cross = jnp.concatenate([swap_dp(far[:half], 1), swap_dp(near[half:], 2)], axis=0)
    return [value, near, far, cross]


def gather_dp(value):
    return jnp.concatenate(gather_parts(value), axis=0)


def exchange_parts(parts):
    size = lax.axis_size("dp")
    if size != 4:
        whole = lax.all_to_all(jnp.stack(parts), "dp", 0, 0)
        return [whole[d] for d in range(size)]
    return [parts[0]] + [swap_dp(parts[d], d) for d in range(1, size)]


def split_parts(value):
    size = lax.axis_size("dp")
    rows = value.shape[0] // size
    return [value[d * rows : (d + 1) * rows] for d in range(size)]


def scatter_dp(value):
    size = lax.axis_size("dp")
    if size != 4:
        return lax.psum_scatter(
            value.astype(LOW), "dp", scatter_dimension=0, tiled=True
        ).astype(FULL)
    parts = split_parts(value)
    total = parts[0]
    for distance in range(size - 1, 0, -1):
        total = total + swap_dp(parts[distance].astype(LOW), distance).astype(FULL)
    return total


def line_up(parts, width):
    rows = parts[0].shape[0]
    whole = jnp.zeros((rows, len(parts) * width), parts[0].dtype)
    for part, who in zip(parts, part_members()):
        whole = lax.dynamic_update_slice_in_dim(whole, part, who * width, 1)
    return whole


def cut_up(value, width):
    return [lax.dynamic_slice_in_dim(value, who * width, width, 1) for who in part_members()]


def is_line():
    return lax.axis_size("grp") == 8


def chip_shift(value, steps):
    pairs = []
    for chip in range(4):
        if 0 <= chip + steps < 4:
            pairs += [(2 * chip + core, 2 * (chip + steps) + core) for core in range(2)]
    return lax.ppermute(value, "grp", pairs)


def core_swap(value):
    return lax.ppermute(value, "grp", [(a, a ^ 1) for a in range(8)])


def gather_earlier(value):
    sequences, rows, width = value.shape
    member = lax.axis_index("grp")
    chunks = ROW_LENGTH // KEY_CHUNK
    if not is_line() or rows != KEY_CHUNK:
        whole = lax.all_gather(value, "grp", axis=1, tiled=True)
        return whole, jnp.arange(chunks, dtype=jnp.int32)
    first_core = member % 2 == 0
    pieces = []
    for steps in range(4):
        mine = value if steps == 0 else chip_shift(value, steps)
        other = core_swap(mine)
        pieces += [jnp.where(first_core, mine, other), jnp.where(first_core, other, mine)]
    order = jnp.arange(chunks, dtype=jnp.int32)
    spots = jnp.maximum(2 * (member // 2 - order // 2) + order % 2, 0)
    return jnp.concatenate(pieces, axis=1), spots


def scatter_earlier(terms):
    sequences, row_length, width = terms.shape
    if not is_line() or ROW_LENGTH // 8 != KEY_CHUNK:
        return lax.psum_scatter(terms, "grp", scatter_dimension=1, tiled=True).astype(FULL)
    first_core = lax.axis_index("grp") % 2 == 0
    terms = terms.reshape(sequences, 4, 2, KEY_CHUNK, width)
    kept = jnp.where(first_core, terms[:, :, 0], terms[:, :, 1])
    given = jnp.where(first_core, terms[:, :, 1], terms[:, :, 0])
    chip_sums = kept.astype(FULL) + core_swap(given).astype(FULL)
    total = chip_sums[:, 0]
    for steps in range(3, 0, -1):
        total = total + chip_shift(chip_sums[:, steps].astype(LOW), -steps).astype(FULL)
    return total


def sum_everywhere(value):
    if lax.axis_size("dp") != 4 or not is_line():
        return lax.psum(value, ("dp", "grp"))
    value = value + swap_dp(value, 1)
    value = value + swap_dp(value, 2)
    value = value + core_swap(value)
    total = value
    for steps in range(1, 4):
        pairs = [(a, (a + 2 * steps) % 8) for a in range(8)]
        total = total + lax.ppermute(value, "grp", pairs)
    return total


ANY_SPEC = pl.BlockSpec(memory_space=pl.ANY)
LANES = 8


def copy_blocks(count, read, write, used, hold, read_sems, write_sem):
    size = -(-count // LANES)
    groups = [(g * size, min((g + 1) * size, count)) for g in range(LANES) if g * size < count]

    def each(low, high, act):
        @pl.loop(low, high)
        def _(block):
            @pl.when(used(block))
            def _():
                act(block)

    for group, (low, high) in enumerate(groups):
        each(low, high, lambda block: read(block, hold.at[block], read_sems.at[group], True))
    for group, (low, high) in enumerate(groups):
        each(low, high, lambda block: read(block, hold.at[block], read_sems.at[group], False))
        each(low, high, lambda block: write(block, hold.at[block], write_sem, True))
    each(0, count, lambda block: write(block, hold.at[block], write_sem, False))


def move(source, target, sem, start):
    copy = pltpu.make_async_copy(source, target, sem)
    if start:
        copy.start()
    else:
        copy.wait()


def block_call(kernel, name, table, inputs, outputs, count, piece, aliases=None):
    hold = pltpu.VMEM((count, piece, D), LOW)
    return pl.pallas_call(
        kernel,
        grid_spec=pltpu.PrefetchScalarGridSpec(
            num_scalar_prefetch=1,
            grid=(1,),
            in_specs=[ANY_SPEC] * len(inputs),
            out_specs=[ANY_SPEC] * len(outputs),
            scratch_shapes=[hold, pltpu.SemaphoreType.DMA((LANES,)), pltpu.SemaphoreType.DMA],
        ),
        out_shape=outputs,
        input_output_aliases=aliases or {},
        compiler_params=pltpu.CompilerParams(
            vmem_limit_bytes=2 * count * piece * D + 4 * 1024 * 1024
        ),
        cost_estimate=pl.CostEstimate(
            flops=0, bytes_accessed=4 * count * piece * D, transcendentals=0
        ),
        name=name,
    )(table, *inputs)


def pick_kernel(at_ref, early_ref, late_ref, out_ref, hold, read_sems, write_sem):
    count = out_ref.shape[0]
    early_slots, late_slots = at_ref[2 * count], at_ref[2 * count + 1]

    def read(block, target, sem, start):
        owner, slot = at_ref[block], at_ref[count + block]

        @pl.when(slot < early_slots)
        def _():
            move(early_ref.at[owner * early_slots + slot], target, sem, start)

        @pl.when(slot >= early_slots)
        def _():
            move(late_ref.at[owner * late_slots + slot - early_slots], target, sem, start)

    def write(block, source, sem, start):
        move(source, out_ref.at[block], sem, start)

    copy_blocks(count, read, write, lambda block: True, hold, read_sems, write_sem)


def pick_blocks(owners, slots, early, late, early_slots, late_slots):
    count = owners.shape[0]
    table = jnp.concatenate([owners, slots, jnp.array([early_slots, late_slots], jnp.int32)])
    piece = early.shape[1]
    out = jax.ShapeDtypeStruct((count, piece, D), LOW)
    return block_call(pick_kernel, "pick_blocks", table, (early, late), [out], count, piece)[0]


def pick_early_kernel(
    team, at_ref, early_ref, query_ref, kv_ref, out_ref, hold, read_sems, write_sem
):
    early_slots = at_ref[2 * GATE_AT]
    share = D // team

    def read(block, target, sem, start):
        source = early_ref.at[at_ref[block] * early_slots + at_ref[GATE_AT + block]]
        move(source, target, sem, start)

    def write(block, source, sem, start):
        def columns(target, place):
            for band in range(team):
                move(source.at[:, pl.ds(band * share, share)], target.at[place, band], sem, start)

        @pl.when(block < KEY_AT)
        def _():
            columns(query_ref, block)

        @pl.when((block >= KEY_AT) & (block < OUT_AT))
        def _():
            move(source, kv_ref.at[block - KEY_AT], sem, start)

        @pl.when(block >= OUT_AT)
        def _():
            columns(out_ref, block - OUT_AT)

    copy_blocks(GATE_AT, read, write, lambda block: True, hold, read_sems, write_sem)


def pick_early(owners, slots, early, early_slots, team):
    piece = early.shape[1]
    columns = jax.ShapeDtypeStruct((MODEL_BLOCKS, team, piece, D // team), LOW)
    rows = jax.ShapeDtypeStruct((2 * KV_BLOCKS, piece, D), LOW)
    return block_call(
        functools.partial(pick_early_kernel, team),
        "pick_early",
        jnp.concatenate([owners, slots, jnp.array([early_slots], jnp.int32)]),
        (early,),
        [columns, rows, columns],
        GATE_AT,
        piece,
    )


def assemble_kernel(order_ref, *refs):
    count = len(refs) - 4
    parts, whole, hold, read_sems, write_sem = refs[:count], refs[-4], refs[-3], refs[-2], refs[-1]
    rows, width = parts[0].shape
    band = rows // 4
    for start in (True, False):
        for group in range(4):
            some = pl.ds(group * band, band)
            for index, part in enumerate(parts):
                lanes = pl.ds(pl.multiple_of(order_ref[index] * width, width), width)
                move(part.at[some], hold.at[some, lanes], read_sems.at[group], start)
            if not start:
                move(hold.at[some], whole.at[some], write_sem, True)
    move(hold, whole, write_sem, False)


def assemble_columns(parts):
    rows, width = parts[0].shape
    wide = width * len(parts)
    return pl.pallas_call(
        assemble_kernel,
        grid_spec=pltpu.PrefetchScalarGridSpec(
            num_scalar_prefetch=1,
            grid=(1,),
            in_specs=[ANY_SPEC] * len(parts),
            out_specs=ANY_SPEC,
            scratch_shapes=[
                pltpu.VMEM((rows, wide), LOW),
                pltpu.SemaphoreType.DMA((4,)),
                pltpu.SemaphoreType.DMA,
            ],
        ),
        out_shape=jax.ShapeDtypeStruct((rows, wide), LOW),
        compiler_params=pltpu.CompilerParams(vmem_limit_bytes=2 * rows * wide + 4 * 1024 * 1024),
        cost_estimate=pl.CostEstimate(
            flops=0, bytes_accessed=4 * rows * wide, transcendentals=0
        ),
        name="assemble_columns",
    )(jnp.stack(part_members()), *parts)


def place_ff_kernel(at_ref, *refs):
    terms, early_ref, late_ref, hold, read_sems, write_sem = (
        refs[:3], refs[3], refs[4], refs[5], refs[6], refs[7]
    )
    count = 3 * FF_BLOCKS
    early_slots, late_slots = at_ref[2 * count], at_ref[2 * count + 1]

    def read(block, target, sem, start):
        for index, term in enumerate(terms):

            @pl.when((block >= index * FF_BLOCKS) & (block < (index + 1) * FF_BLOCKS))
            def _():
                move(term.at[block - index * FF_BLOCKS], target, sem, start)

    def write(block, source, sem, start):
        owner, slot = at_ref[block], at_ref[count + block]

        @pl.when(slot < early_slots)
        def _():
            move(source, early_ref.at[owner * early_slots + slot], sem, start)

        @pl.when(slot >= early_slots)
        def _():
            move(source, late_ref.at[owner * late_slots + slot - early_slots], sem, start)

    copy_blocks(count, read, write, lambda block: True, hold, read_sems, write_sem)


def place_ff(owners, slots, terms, early_slots, late_slots):
    devices = lax.axis_size("grp")
    piece = terms[0].shape[1]
    table = jnp.concatenate([owners, slots, jnp.array([early_slots, late_slots], jnp.int32)])
    outs = [
        jax.ShapeDtypeStruct((devices * count, piece, D), LOW)
        for count in (early_slots, late_slots)
    ]
    return block_call(place_ff_kernel, "place_ff", table, terms, outs, 3 * FF_BLOCKS, piece)


def place_attention_kernel(
    team, at_ref, query_ref, kv_ref, out_ref, early_in, early_ref, hold, read_sems, write_sem
):
    early_slots = at_ref[2 * GATE_AT]
    share = D // team

    def read(block, target, sem, start):
        def columns(source, place):
            for band in range(team):
                move(source.at[place, band], target.at[:, pl.ds(band * share, share)], sem, start)

        @pl.when(block < KEY_AT)
        def _():
            columns(query_ref, block)

        @pl.when((block >= KEY_AT) & (block < OUT_AT))
        def _():
            move(kv_ref.at[block - KEY_AT], target, sem, start)

        @pl.when(block >= OUT_AT)
        def _():
            columns(out_ref, block - OUT_AT)

    def write(block, source, sem, start):
        target = early_ref.at[at_ref[block] * early_slots + at_ref[GATE_AT + block]]
        move(source, target, sem, start)

    def used(block):
        return at_ref[GATE_AT + block] < early_slots

    copy_blocks(GATE_AT, read, write, used, hold, read_sems, write_sem)


def place_attention(owners, slots, terms, early, early_slots, team):
    piece = early.shape[1]
    return block_call(
        functools.partial(place_attention_kernel, team),
        "place_attention",
        jnp.concatenate([owners, slots, jnp.array([early_slots], jnp.int32)]),
        (*terms, early),
        [jax.ShapeDtypeStruct(early.shape, LOW)],
        GATE_AT,
        piece,
        {4: 0},
    )[0]


def adamw_kernel(team, first_slot, at_ref, master, first, second, *refs):
    parts = refs[:team]
    new_master, new_first, new_second, copy, shares = refs[-5:]
    kind = at_ref[team + first_slot + pl.program_id(0)]
    piece, share = R // team, D // team
    for index in range(team):
        shares[at_ref[index]] = parts[index][0]

    def update(rows, lanes, gradient):
        results = adamw(
            master[0, rows, lanes], first[0, rows, lanes], second[0, rows, lanes],
            gradient, WEIGHT_RATE, WEIGHT_DECAY,
        )
        for target, value in zip((new_master, new_first, new_second), results):
            target[0, rows, lanes] = value
        copy[0, rows, lanes] = results[0].astype(LOW)

    for band in range(team):
        rows = slice(band * piece, (band + 1) * piece)

        @pl.when(kind == 1)
        def _():
            update(rows, slice(0, D), shares[band].astype(FULL))

        @pl.when(kind == 2)
        def _():
            for index in range(team):
                lanes = slice(index * share, (index + 1) * share)
                update(rows, lanes, shares[index, :, band * share : (band + 1) * share].astype(FULL))

        @pl.when(kind == 0)
        def _():
            update(rows, slice(0, D), jnp.zeros((piece, D), FULL))


def adamw_slots(kinds, master, first, second, parts, first_slot, so_far):
    team = len(parts)
    count = parts[0].shape[0]
    slot_spec = pl.BlockSpec((1, R, D), lambda i, a: (first_slot + i, 0, 0))
    part_spec = pl.BlockSpec((1, R // team, D), lambda i, a: (i, 0, 0))
    whole = jax.ShapeDtypeStruct(master.shape, FULL)
    extra = [] if so_far is None else list(so_far)
    return pl.pallas_call(
        functools.partial(adamw_kernel, team, first_slot),
        grid_spec=pltpu.PrefetchScalarGridSpec(
            num_scalar_prefetch=1,
            grid=(count,),
            in_specs=[slot_spec] * 3 + [part_spec] * team + [ANY_SPEC] * len(extra),
            out_specs=[slot_spec] * 4,
            scratch_shapes=[pltpu.VMEM((team, R // team, D), LOW)],
        ),
        out_shape=[whole, whole, whole, jax.ShapeDtypeStruct(master.shape, LOW)],
        input_output_aliases={4 + team + k: k for k in range(len(extra))},
        compiler_params=pltpu.CompilerParams(vmem_limit_bytes=40 * 1024 * 1024),
        cost_estimate=pl.CostEstimate(
            flops=20 * count * R * D, bytes_accessed=28 * count * R * D, transcendentals=0
        ),
        name="adamw_slots",
    )(jnp.concatenate([jnp.stack(part_members()), kinds]), master, first, second, *parts, *extra)


def after(value, *others):
    return lax.optimization_barrier((value,) + others)[0]


def per_device(
    layer_input,
    out_cotangent,
    seq_lengths,
    block_owner,
    weight_master,
    weight_first,
    weight_second,
    gain_master,
    gain_first,
    gain_second,
):
    slot_count = weight_master.shape[0]
    team = lax.axis_size("dp")
    rank = lax.axis_index("dp")
    member = lax.axis_index("grp")
    piece = R // team
    sequence_count = layer_input.shape[0]
    segment_rows = layer_input.shape[1]
    token_count = sequence_count * segment_rows
    model_share = D // team
    kv_share = KEY_VALUE_WIDTH // team
    early_slots = slot_count * 5 // 12
    late_slots = slot_count - early_slots

    block_order = jnp.arange(BLOCKS, dtype=jnp.int32)
    same_owner = block_owner[:, None] == block_owner[None, :]
    earlier = block_order[None, :] < block_order[:, None]
    slots = jnp.sum((same_owner & earlier).astype(jnp.int32), axis=1)
    whole_columns = (block_order < KEY_AT) | ((block_order >= OUT_AT) & (block_order < GATE_AT))
    block_kind = jnp.where(whole_columns, 2, 1)
    mine = (block_owner == member)[None, :] & (
        slots[None, :] == jnp.arange(slot_count, dtype=jnp.int32)[:, None]
    )
    kinds = jnp.sum(jnp.where(mine, block_kind[None, :], 0), axis=1)
    my_attention = jnp.any(mine & (block_order < GATE_AT)[None, :], axis=1)
    spills = jnp.any(slots[:GATE_AT] >= early_slots)

    def shares_of(low, high):
        count = high - low
        by_rows = lax.dynamic_slice(weight_master, (low, rank * piece, 0), (count, piece, D))
        by_columns = lax.dynamic_slice(
            weight_master, (low, 0, rank * model_share), (count, R, model_share)
        ).astype(LOW)
        by_columns = jnp.concatenate(
            [by_columns[:, j * piece : (j + 1) * piece] for j in range(team)], axis=-1
        )
        return jnp.where((kinds[low:high] == 2)[:, None, None], by_columns, by_rows.astype(LOW))

    shares_early = shares_of(0, early_slots)
    shares_late = shares_of(early_slots, slot_count)
    gathered_early = lax.all_gather(shares_early, "grp", axis=0, tiled=True)
    gathered_late = lax.all_gather(shares_late, "grp", axis=0, tiled=True)
    gains_all = lax.all_gather(gain_master.astype(LOW), "grp", axis=1, tiled=True)

    positions = member * segment_rows + jnp.arange(segment_rows, dtype=jnp.int32)
    valid_rows = (positions[None, :] < seq_lengths[:, None]).reshape(token_count, 1)
    cosine_rows, sine_rows = rotary_tables(positions, HEAD_WIDTH)
    wide_cosine = jnp.concatenate([cosine_rows] * 4, axis=1)
    wide_sine = jnp.concatenate([-sine_rows, sine_rows] * 2, axis=1)
    places = jnp.concatenate(
        [jnp.stack([member * segment_rows, jnp.int32(segment_rows)]), seq_lengths]
    ).astype(jnp.int32)
    inputs = layer_input.reshape(token_count, D).astype(FULL)
    root_one = lax.rsqrt(jnp.mean(inputs * inputs, axis=-1, keepdims=True) + NORM_EPS)
    normed_one = inputs * root_one
    gain_one = gains_all[0].astype(FULL)
    gain_two = gains_all[1].astype(FULL)
    hidden_one = (normed_one * gain_one).astype(LOW)
    hidden_one_all = gather_dp(hidden_one)
    grad_out = jnp.where(valid_rows, out_cotangent.reshape(token_count, D), jnp.zeros((), LOW))
    grad_out_all = gather_dp(after(grad_out, hidden_one_all))
    gathered_early = after(gathered_early, hidden_one_all, grad_out_all)

    def attention_early():
        return tuple(
            pick_early(block_owner[:GATE_AT], slots[:GATE_AT], gathered_early, early_slots, team)
        )

    def attention_spilled():
        everything = lax.all_gather(
            jnp.concatenate([shares_early, shares_late]), "grp", axis=0, tiled=True
        )
        found = jnp.take(
            everything, (block_owner * slot_count + slots)[:GATE_AT], axis=0, mode="clip"
        )

        def columns(first):
            chosen = found[first : first + MODEL_BLOCKS]
            return chosen.reshape(MODEL_BLOCKS, piece, team, model_share).transpose(0, 2, 1, 3)

        return columns(0), found[KEY_AT:OUT_AT], columns(OUT_AT)

    query_share, kv_rows, out_share = lax.cond(spills, attention_spilled, attention_early)
    query_share = query_share.reshape(D, model_share)
    kv_rows = kv_rows.reshape(2 * kv_share, D)
    out_share = out_share.reshape(D, model_share)


    kv_parts = exchange_parts(split_parts(contract_rows(hidden_one_all, kv_rows).astype(LOW)))
    query_parts = exchange_parts(split_parts(plain_dot(hidden_one_all, query_share).astype(LOW)))
    kv_proj = (
        line_up(kv_parts, 2 * kv_share)
        .reshape(token_count, team, 2 * KV_BLOCKS, piece)
        .transpose(0, 2, 1, 3)
        .reshape(token_count, 2 * KEY_VALUE_WIDTH)
    )
    keys_local = apply_rotation(
        kv_proj[:, :KEY_VALUE_WIDTH]
        .astype(FULL)
        .reshape(sequence_count, segment_rows, KEY_VALUE_HEADS, HEAD_WIDTH),
        cosine_rows,
        sine_rows,
    ).astype(LOW)
    kv_local = jnp.concatenate(
        [
            keys_local.reshape(sequence_count, segment_rows, KEY_VALUE_WIDTH),
            kv_proj[:, KEY_VALUE_WIDTH:].reshape(sequence_count, segment_rows, KEY_VALUE_WIDTH),
        ],
        axis=-1,
    )
    kv_all, spots = gather_earlier(kv_local)
    query_proj = line_up(query_parts, model_share).reshape(sequence_count, segment_rows, D)
    w_out = assemble_columns(gather_parts(after(out_share, query_proj)))

    attended, logs = attend_forward(places, spots, wide_cosine, wide_sine, query_proj, kv_all)
    attended_flat = attended.reshape(token_count, D)
    residual = inputs + plain_dot(attended_flat, w_out)
    root_two = lax.rsqrt(jnp.mean(residual * residual, axis=-1, keepdims=True) + NORM_EPS)
    normed_two = residual * root_two
    hidden_two = (normed_two * gain_two).astype(LOW)
    hidden_two_all = gather_dp(hidden_two)
    attended_all = gather_dp(after(attended_flat, hidden_two_all))

    ff_blocks = pick_blocks(
        block_owner[GATE_AT:], slots[GATE_AT:], gathered_early, gathered_late, early_slots, late_slots
    )
    w_gate = ff_blocks[:FF_BLOCKS].reshape(FF // team, D)
    w_up = ff_blocks[FF_BLOCKS : 2 * FF_BLOCKS].reshape(FF // team, D)
    w_down = ff_blocks[2 * FF_BLOCKS :].reshape(FF // team, D)
    gate_pre = contract_rows(hidden_two_all, w_gate)
    up_pre = contract_rows(hidden_two_all, w_up)
    sigmoid_gate = jax.nn.sigmoid(gate_pre)
    activated = gate_pre * sigmoid_gate
    inner = (activated * up_pre).astype(LOW)
    grad_inner = contract_rows(grad_out_all, w_down)
    grad_gate = (
        grad_inner * up_pre * (sigmoid_gate * (1.0 + gate_pre * (1.0 - sigmoid_gate)))
    ).astype(LOW)
    grad_up = (grad_inner * activated).astype(LOW)
    grad_htwo = scatter_dp(plain_dot(grad_gate, w_gate) + plain_dot(grad_up, w_up))
    output = residual + scatter_dp(plain_dot(inner, w_down))
    layer_output = (
        jnp.where(valid_rows, output, 0.0)
        .astype(LOW)
        .reshape(sequence_count, segment_rows, D)
    )
    ff_terms = [
        contract_first(left, right).astype(LOW).reshape(FF_BLOCKS, piece, D)
        for left, right in (
            (grad_gate, hidden_two_all),
            (grad_up, hidden_two_all),
            (inner, grad_out_all),
        )
    ]
    early_terms, late_terms = place_ff(
        block_owner[GATE_AT:], slots[GATE_AT:], ff_terms, early_slots, late_slots
    )
    late_sums = lax.psum_scatter(late_terms, "grp", scatter_dimension=0, tiled=True)

    scaled_two = grad_htwo * gain_two
    grad_resid = grad_out.astype(FULL) + root_two * (
        scaled_two - normed_two * jnp.mean(scaled_two * normed_two, axis=-1, keepdims=True)
    )
    resid_low = grad_resid.astype(LOW)
    grad_attended = contract_rows(resid_low, w_out).astype(LOW)
    resid_share = jnp.concatenate(exchange_parts(cut_up(resid_low, model_share)), axis=0)
    out_terms = contract_first(attended_all, resid_share)
    grad_query, kv_terms = attend_backward(
        places,
        spots,
        wide_cosine,
        wide_sine,
        query_proj,
        kv_all,
        attended,
        grad_attended.reshape(sequence_count, segment_rows, D),
        logs,
    )
    query_share_parts = exchange_parts(cut_up(grad_query.reshape(token_count, D), model_share))
    key_value_sums = scatter_earlier(kv_terms)
    grad_keys = apply_rotation(
        key_value_sums[:, :, :KEY_VALUE_WIDTH].reshape(
            sequence_count, segment_rows, KEY_VALUE_HEADS, HEAD_WIDTH
        ),
        cosine_rows,
        -sine_rows,
    ).reshape(token_count, KEY_VALUE_WIDTH)
    grad_values = key_value_sums[:, :, KEY_VALUE_WIDTH:].reshape(token_count, KEY_VALUE_WIDTH)
    grad_kv = (
        jnp.concatenate([grad_keys, grad_values], axis=1)
        .astype(LOW)
        .reshape(token_count, 2 * KV_BLOCKS, team, piece)
        .transpose(0, 2, 1, 3)
        .reshape(token_count, 2 * KEY_VALUE_WIDTH)
    )
    grad_kv_share = jnp.concatenate(exchange_parts(cut_up(grad_kv, 2 * kv_share)), axis=0)
    grad_query_share = jnp.concatenate(query_share_parts, axis=0)

    query_terms = contract_first(hidden_one_all, grad_query_share)
    kv_weight_terms = contract_first(grad_kv_share, hidden_one_all)
    column_shape = (MODEL_BLOCKS, team, piece, model_share)
    attention_terms = [
        query_terms.astype(LOW).reshape(column_shape),
        kv_weight_terms.astype(LOW).reshape(2 * KV_BLOCKS, piece, D),
        out_terms.astype(LOW).reshape(column_shape),
    ]
    early_sums = lax.psum_scatter(
        place_attention(
            block_owner[:GATE_AT], slots[:GATE_AT], attention_terms, early_terms, early_slots, team
        ),
        "grp",
        scatter_dimension=0,
        tiled=True,
    )

    grad_hone = scatter_dp(
        contract_rows(grad_query_share, query_share) + plain_dot(grad_kv_share, kv_rows)
    )
    scaled_one = grad_hone * gain_one
    input_grad = (
        (
            grad_resid
            + root_one
            * (scaled_one - normed_one * jnp.mean(scaled_one * normed_one, axis=-1, keepdims=True))
        )
        .astype(LOW)
        .reshape(sequence_count, segment_rows, D)
    )
    gain_grad = sum_everywhere(
        jnp.stack(
            [jnp.sum(grad_hone * normed_one, axis=0), jnp.sum(grad_htwo * normed_two, axis=0)]
        )
    )

    def sums_early():
        return late_sums

    def sums_spilled():
        by_columns = [
            attention_terms[k].transpose(0, 2, 1, 3).reshape(MODEL_BLOCKS, piece, D) for k in (0, 2)
        ]
        found = jnp.concatenate([by_columns[0], attention_terms[1], by_columns[1]], axis=0)
        every_slot = jnp.arange(slot_count * lax.axis_size("grp"), dtype=jnp.int32)
        hits = (block_owner * slot_count + slots)[None, :GATE_AT] == every_slot[:, None]
        which = jnp.sum(jnp.where(hits, block_order[None, :GATE_AT], 0), axis=1)
        spread = jnp.where(
            jnp.any(hits, axis=1)[:, None, None],
            jnp.take(found, which, axis=0, mode="clip"),
            jnp.zeros((), LOW),
        )
        extra = lax.psum_scatter(spread, "grp", scatter_dimension=0, tiled=True)
        return jnp.where(
            my_attention[early_slots:][:, None, None], extra[early_slots:], late_sums
        )

    late_sums = lax.cond(spills, sums_spilled, sums_early)
    states = (weight_master, weight_first, weight_second)
    updated = adamw_slots(kinds, *states, gather_parts(late_sums), early_slots, None)
    updated = adamw_slots(kinds, *states, gather_parts(early_sums), 0, updated)
    new_master, new_first, new_second, weight_copy = updated

    share_width = gain_master.shape[1]
    gain_share = lax.dynamic_slice_in_dim(gain_grad, member * share_width, share_width, 1)
    new_gain, new_gain_first, new_gain_second = adamw(
        gain_master, gain_first, gain_second, gain_share, GAIN_RATE, 0.0
    )
    return (
        layer_output,
        input_grad,
        new_master,
        new_first,
        new_second,
        weight_copy,
        new_gain,
        new_gain_first,
        new_gain_second,
    )


def solution(mesh):
    return jax.shard_map(
        per_device,
        mesh=mesh,
        in_specs=(
            P("dp", "grp", None),
            P("dp", "grp", None),
            P("dp"),
            P(),
            P("grp", None, None),
            P("grp", None, None),
            P("grp", None, None),
            P(None, "grp"),
            P(None, "grp"),
            P(None, "grp"),
        ),
        out_specs=(
            P("dp", "grp", None),
            P("dp", "grp", None),
            P("grp", None, None),
            P("grp", None, None),
            P("grp", None, None),
            P("grp", None, None),
            P(None, "grp"),
            P(None, "grp"),
            P(None, "grp"),
        ),
        check_vma=False,
    )
```

```python
import functools
import math

import jax
import jax.numpy as jnp
from jax import lax
from jax.experimental import pallas as pl
from jax.experimental.pallas import tpu as pltpu
from jax.sharding import PartitionSpec as P

D = 2048
QUERY_HEADS = 32
KEY_VALUE_HEADS = 4
HEAD_WIDTH = 64
FF = 5632
ROW_LENGTH = 2048
R = 128
STEP = 7
KEY_VALUE_WIDTH = 256
MODEL_BLOCKS = D // R
KV_BLOCKS = KEY_VALUE_WIDTH // R
FF_BLOCKS = FF // R
KEY_AT = MODEL_BLOCKS
OUT_AT = MODEL_BLOCKS + 2 * KV_BLOCKS
GATE_AT = OUT_AT + MODEL_BLOCKS
UP_AT = GATE_AT + FF_BLOCKS
DOWN_AT = UP_AT + FF_BLOCKS
BLOCKS = DOWN_AT + FF_BLOCKS

NORM_EPS = 1e-05
BETA_ONE = 0.9
BETA_TWO = 0.95
ADAM_EPS = 1e-08
WEIGHT_RATE = 0.1
GAIN_RATE = 0.5
WEIGHT_DECAY = 0.1
MASKED = -1e30
LOW = jnp.bfloat16
FULL = jnp.float32


def rotary_tables(positions, head_size):
    halfway = head_size // 2
    spacing = jnp.arange(halfway, dtype=FULL) * (-2.0 * math.log(10000.0) / head_size)
    angles = positions.astype(FULL)[:, None] * jnp.exp(spacing)[None, :]
    return (jnp.cos(angles), jnp.sin(angles))


def apply_rotation(values, cosine_rows, sine_rows):
    halfway = values.shape[-1] // 2
    leading = values[..., :halfway]
    trailing = values[..., halfway:]
    cos_rows = cosine_rows[:, None, :]
    sin_rows = sine_rows[:, None, :]
    return jnp.concatenate(
        [leading * cos_rows - trailing * sin_rows, trailing * cos_rows + leading * sin_rows],
        axis=-1,
    )


def contract_rows(left, right):
    return lax.dot_general(left, right, (((1,), (1,)), ((), ())), preferred_element_type=FULL)


def contract_first(left, right):
    return lax.dot_general(left, right, (((0,), (0,)), ((), ())), preferred_element_type=FULL)


def plain_dot(left, right):
    return jnp.dot(left, right, preferred_element_type=FULL)


def adamw(master, first, second, gradient, rate, decay):
    first_new = BETA_ONE * first + (1.0 - BETA_ONE) * gradient
    second_new = BETA_TWO * second + (1.0 - BETA_TWO) * gradient * gradient
    first_fix = 1.0 - BETA_ONE**STEP
    second_fix = 1.0 - BETA_TWO**STEP
    stepped = first_new / first_fix / (jnp.sqrt(second_new / second_fix) + ADAM_EPS)
    return (master - rate * (stepped + decay * master), first_new, second_new)


KEY_CHUNK = 256
GROUP_WIDTH = D // KEY_VALUE_HEADS
PAIRS = GROUP_WIDTH // 128
EXP_SCALE = math.log2(math.e) / math.sqrt(HEAD_WIDTH)


def lanes_of(shape):
    return lax.broadcasted_iota(jnp.int32, shape, len(shape) - 1)


def swap_halves(values):
    first = (lanes_of(values.shape) % HEAD_WIDTH) < HEAD_WIDTH // 2
    return jnp.where(first, pltpu.roll(values, 96, 1), pltpu.roll(values, 32, 1))


def turn(values, cosine, sine):
    return values * cosine + swap_halves(values) * sine


def chunk_bounds(where_ref):
    start, rows, length = where_ref[0], where_ref[1], where_ref[2 + pl.program_id(0)]
    free = jnp.minimum(start // KEY_CHUNK, length // KEY_CHUNK)
    last = jnp.minimum(start + rows, length)
    return free, (last + KEY_CHUNK - 1) // KEY_CHUNK, start, length


def chunk_rows(spots_ref, chunk):
    return pl.ds(pl.multiple_of(spots_ref[chunk] * KEY_CHUNK, KEY_CHUNK), KEY_CHUNK)


def stacked(block, odd):
    wide = block.astype(FULL)
    wide = jnp.where(odd, pltpu.roll(wide, 64, 1), wide)
    low = jnp.where(lanes_of(wide.shape) < HEAD_WIDTH, wide, 0.0)
    return jnp.concatenate([low, pltpu.roll(low, 64, 1)], axis=0)


def mask_of(chunk, start, length, queries):
    keys = chunk * KEY_CHUNK + lax.broadcasted_iota(jnp.int32, (KEY_CHUNK, queries), 0)
    places = start + lax.broadcasted_iota(jnp.int32, (KEY_CHUNK, queries), 1)
    allowed = (keys <= places) & (keys < length)
    return jnp.concatenate([allowed, allowed], axis=0)


def across(left, right):
    return lax.dot_general(left, right, (((1,), (1,)), ((), ())), preferred_element_type=FULL)


def attend_forward_kernel(
    where_ref, spots_ref, cos_ref, sin_ref, q_ref, k_ref, v_ref, out_ref, log_ref, turned, peaks, sums, totals
):
    queries = q_ref.shape[1]
    odd = (pl.program_id(1) % 2) == 1
    free, end, start, length = chunk_bounds(where_ref)
    for pair in range(PAIRS):
        lanes = slice(128 * pair, 128 * pair + 128)
        turned[:, lanes] = turn(q_ref[0, :, lanes].astype(FULL), cos_ref[...], sin_ref[...]).astype(LOW)
    peaks[...] = jnp.full(peaks.shape, MASKED, FULL)
    sums[...] = jnp.zeros(sums.shape, FULL)
    totals[...] = jnp.zeros(totals.shape, FULL)

    def step(chunk, masked):
        rows = chunk_rows(spots_ref, chunk)
        keys = stacked(k_ref[0, rows, :], odd).astype(LOW)
        values = stacked(v_ref[0, rows, :], odd).T.astype(LOW)
        allowed = mask_of(chunk, start, length, queries) if masked else None
        for pair in range(PAIRS):
            scores = across(keys, turned[:, 128 * pair : 128 * pair + 128]) * EXP_SCALE
            if masked:
                scores = jnp.where(allowed, scores, MASKED)
            weights, fades = [], []
            for side in range(2):
                head = slice(2 * pair + side, 2 * pair + side + 1)
                part = scores[side * KEY_CHUNK : (side + 1) * KEY_CHUNK]
                old = peaks[head, :]
                new = jnp.maximum(old, jnp.max(part, axis=0, keepdims=True))
                weight = jnp.exp2(part - new)
                fade = jnp.exp2(old - new)
                peaks[head, :] = new
                sums[head, :] = sums[head, :] * fade + jnp.sum(weight, axis=0, keepdims=True)
                weights.append(weight.astype(LOW))
                fades.append(jnp.broadcast_to(fade, (HEAD_WIDTH, queries)))
            mixed = jnp.dot(values, jnp.concatenate(weights, axis=0), preferred_element_type=FULL)
            totals[pair] = totals[pair] * jnp.concatenate(fades, axis=0) + mixed

    @pl.loop(0, free)
    def _(chunk):
        step(chunk, False)

    @pl.loop(free, end)
    def _(chunk):
        step(chunk, True)

    for pair in range(PAIRS):
        shares = [
            jnp.broadcast_to(1.0 / sums[2 * pair + side : 2 * pair + side + 1, :], (HEAD_WIDTH, queries))
            for side in range(2)
        ]
        mixed = totals[pair] * jnp.concatenate(shares, axis=0)
        out_ref[0, :, 128 * pair : 128 * pair + 128] = mixed.T.astype(LOW)
    log_ref[0] = peaks[...] + jnp.log2(sums[...])


def attend_backward_kernel(
    where_ref, spots_ref, cos_ref, sin_ref, q_ref, k_ref, v_ref, out_ref, grad_ref, log_ref,
    dq_ref, dkv_ref, turned, dots, turning, key_sums, value_sums,
):
    queries = q_ref.shape[1]
    group = pl.program_id(1)
    odd = (group % 2) == 1
    free, end, start, length = chunk_bounds(where_ref)
    for pair in range(PAIRS):
        lanes = slice(128 * pair, 128 * pair + 128)
        turned[:, lanes] = turn(q_ref[0, :, lanes].astype(FULL), cos_ref[...], sin_ref[...]).astype(LOW)
        products = (out_ref[0, :, lanes].astype(FULL) * grad_ref[0, :, lanes].astype(FULL)).T
        dots[2 * pair : 2 * pair + 1, :] = jnp.sum(products[:HEAD_WIDTH], axis=0, keepdims=True)
        dots[2 * pair + 1 : 2 * pair + 2, :] = jnp.sum(products[HEAD_WIDTH:], axis=0, keepdims=True)
    turning[...] = jnp.zeros(turning.shape, FULL)

    @pl.when(group == 0)
    def _():
        dkv_ref[...] = jnp.zeros(dkv_ref.shape, LOW)

    key_lanes = pl.ds(pl.multiple_of((group // 2) * 128, 128), 128)
    value_lanes = pl.ds(pl.multiple_of(KEY_VALUE_WIDTH + (group // 2) * 128, 128), 128)

    def step(chunk, masked):
        rows = chunk_rows(spots_ref, chunk)
        wide_keys = stacked(k_ref[0, rows, :], odd)
        keys = wide_keys.astype(LOW)
        keys_down = wide_keys.T.astype(LOW)
        values = stacked(v_ref[0, rows, :], odd).astype(LOW)
        allowed = mask_of(chunk, start, length, queries) if masked else None
        for pair in range(PAIRS):
            lanes = slice(128 * pair, 128 * pair + 128)
            asked = turned[:, lanes]
            given = grad_ref[0, :, lanes]
            scores = across(keys, asked) * EXP_SCALE
            if masked:
                scores = jnp.where(allowed, scores, MASKED)
            slopes = across(values, given)
            weights, moves = [], []
            for side in range(2):
                head = slice(2 * pair + side, 2 * pair + side + 1)
                part = slice(side * KEY_CHUNK, (side + 1) * KEY_CHUNK)
                weight = jnp.exp2(scores[part] - log_ref[0, head, :])
                weights.append(weight.astype(LOW))
                moves.append((weight * (slopes[part] - dots[head, :])).astype(LOW))
            weights = jnp.concatenate(weights, axis=0)
            moves = jnp.concatenate(moves, axis=0)
            value_part = jnp.dot(weights, given, preferred_element_type=FULL)
            key_part = jnp.dot(moves, asked, preferred_element_type=FULL)
            if pair == 0:
                value_sums[...] = value_part
                key_sums[...] = key_part
            else:
                value_sums[...] += value_part
                key_sums[...] += key_part
            turning[pair] += jnp.dot(keys_down, moves, preferred_element_type=FULL)
        for sums, lanes, scale in (
            (key_sums, key_lanes, 1.0 / math.sqrt(HEAD_WIDTH)),
            (value_sums, value_lanes, 1.0),
        ):
            both = (sums[:KEY_CHUNK] + pltpu.roll(sums[KEY_CHUNK:], 64, 1)) * scale
            low_side = lanes_of(both.shape) < HEAD_WIDTH
            kept = dkv_ref[0, rows, lanes].astype(FULL)
            mine = jnp.where(odd, pltpu.roll(both, 64, 1), both)
            dkv_ref[0, rows, lanes] = jnp.where(low_side != odd, mine, kept).astype(LOW)

    @pl.loop(0, free)
    def _(chunk):
        step(chunk, False)

    @pl.loop(free, end)
    def _(chunk):
        step(chunk, True)

    for pair in range(PAIRS):
        back = turning[pair].T * (1.0 / math.sqrt(HEAD_WIDTH))
        dq_ref[0, :, 128 * pair : 128 * pair + 128] = turn(back, cos_ref[...], -sin_ref[...]).astype(LOW)


def attention_specs(sequences, rows, row_length):
    q_spec = pl.BlockSpec((1, rows, GROUP_WIDTH), lambda s, g, w, t: (s, 0, g))
    k_spec = pl.BlockSpec((1, row_length, 128), lambda s, g, w, t: (s, 0, g // 2))
    v_spec = pl.BlockSpec((1, row_length, 128), lambda s, g, w, t: (s, 0, 2 + g // 2))
    table_spec = pl.BlockSpec((rows, 128), lambda s, g, w, t: (0, 0))
    log_spec = pl.BlockSpec((1, 2 * PAIRS, rows), lambda s, g, w, t: (s, g, 0))
    return q_spec, k_spec, v_spec, table_spec, log_spec


def attend_forward(places, spots, cosine, sine, query_proj, kv_all):
    sequences, rows, _ = query_proj.shape
    row_length = kv_all.shape[1]
    q_spec, k_spec, v_spec, table_spec, log_spec = attention_specs(sequences, rows, row_length)
    pairs = sequences * QUERY_HEADS * rows * row_length
    return pl.pallas_call(
        attend_forward_kernel,
        grid_spec=pltpu.PrefetchScalarGridSpec(
            num_scalar_prefetch=2,
            grid=(sequences, KEY_VALUE_HEADS),
            in_specs=[table_spec, table_spec, q_spec, k_spec, v_spec],
            out_specs=[q_spec, log_spec],
            scratch_shapes=[
                pltpu.VMEM((rows, GROUP_WIDTH), LOW),
                pltpu.VMEM((2 * PAIRS, rows), FULL),
                pltpu.VMEM((2 * PAIRS, rows), FULL),
                pltpu.VMEM((PAIRS, 128, rows), FULL),
            ],
        ),
        out_shape=[
            jax.ShapeDtypeStruct(query_proj.shape, LOW),
            jax.ShapeDtypeStruct((sequences, QUERY_HEADS, rows), FULL),
        ],
        compiler_params=pltpu.CompilerParams(vmem_limit_bytes=40 * 1024 * 1024),
        cost_estimate=pl.CostEstimate(
            flops=4 * HEAD_WIDTH * pairs, bytes_accessed=8 * 1024 * 1024, transcendentals=pairs
        ),
        name="attend_forward",
    )(places, spots, cosine, sine, query_proj, kv_all, kv_all)


def attend_backward(places, spots, cosine, sine, query_proj, kv_all, attended, grad_attended, logs):
    sequences, rows, _ = query_proj.shape
    row_length = kv_all.shape[1]
    q_spec, k_spec, v_spec, table_spec, log_spec = attention_specs(sequences, rows, row_length)
    pairs = sequences * QUERY_HEADS * rows * row_length
    return pl.pallas_call(
        attend_backward_kernel,
        grid_spec=pltpu.PrefetchScalarGridSpec(
            num_scalar_prefetch=2,
            grid=(sequences, KEY_VALUE_HEADS),
            in_specs=[table_spec, table_spec, q_spec, k_spec, v_spec, q_spec, q_spec, log_spec],
            out_specs=[
                q_spec,
                pl.BlockSpec((1, row_length, 2 * KEY_VALUE_WIDTH), lambda s, g, w, t: (s, 0, 0)),
            ],
            scratch_shapes=[
                pltpu.VMEM((rows, GROUP_WIDTH), LOW),
                pltpu.VMEM((2 * PAIRS, rows), FULL),
                pltpu.VMEM((PAIRS, 128, rows), FULL),
                pltpu.VMEM((2 * KEY_CHUNK, 128), FULL),
                pltpu.VMEM((2 * KEY_CHUNK, 128), FULL),
            ],
        ),
        out_shape=[
            jax.ShapeDtypeStruct(query_proj.shape, LOW),
            jax.ShapeDtypeStruct((sequences, row_length, 2 * KEY_VALUE_WIDTH), LOW),
        ],
        compiler_params=pltpu.CompilerParams(vmem_limit_bytes=40 * 1024 * 1024),
        cost_estimate=pl.CostEstimate(
            flops=10 * HEAD_WIDTH * pairs, bytes_accessed=12 * 1024 * 1024, transcendentals=pairs
        ),
        name="attend_backward",
    )(places, spots, cosine, sine, query_proj, kv_all, kv_all, attended, grad_attended, logs)


def swap_dp(value, distance):
    size = lax.axis_size("dp")
    return lax.ppermute(value, "dp", [(a, a ^ distance) for a in range(size)])


def part_members():
    size = lax.axis_size("dp")
    rank = lax.axis_index("dp")
    return [rank ^ d if size == 4 else jnp.int32(d) for d in range(size)]


def near_far(value):
    return [swap_dp(value, 1), swap_dp(value, 2)]


def cross_of(near, far):
    half = near.shape[0] // 2
    return [swap_dp(far[:half], 1), swap_dp(near[half:], 2)]


def gather_parts(value):
    size = lax.axis_size("dp")
    if size != 4:
        whole = lax.all_gather(value, "dp", axis=0)
        return [whole[d] for d in range(size)]
    beside = near_far(value)
    return [value, *beside, jnp.concatenate(cross_of(*beside), axis=0)]


def gather_dp(value):
    return jnp.concatenate(gather_parts(value), axis=0)


def gather_direct(value):
    size = lax.axis_size("dp")
    if size != 4:
        return gather_parts(value)
    near, far = swap_dp(value, 1), swap_dp(value, 2)
    return [value, near, far, swap_dp(value, 3)]


def send_parts(parts):
    size = lax.axis_size("dp")
    if size != 4:
        stack = jnp.concatenate([part.astype(LOW) for part in parts], axis=0)
        total = lax.psum_scatter(stack, "dp", scatter_dimension=0, tiled=True)
        return [jnp.zeros_like(total), total]
    return [parts[0]] + [swap_dp(parts[distance], distance) for distance in range(1, size)]


def add_up(own, received):
    total = own.astype(FULL)
    for part in received:
        total = total + part.astype(FULL)
    return total


def exchange_parts(parts):
    size = lax.axis_size("dp")
    if size != 4:
        whole = lax.all_to_all(jnp.stack(parts), "dp", 0, 0)
        return [whole[d] for d in range(size)]
    return [parts[0]] + [swap_dp(parts[d], d) for d in range(1, size)]


def split_parts(value):
    size = lax.axis_size("dp")
    rows = value.shape[0] // size
    return [value[d * rows : (d + 1) * rows] for d in range(size)]


def scatter_dp(value):
    size = lax.axis_size("dp")
    if size != 4:
        return lax.psum_scatter(
            value.astype(LOW), "dp", scatter_dimension=0, tiled=True
        ).astype(FULL)
    own, near, far, cross = split_parts(value)
    half = own.shape[0] // 2
    near, far, cross = near.astype(LOW), far.astype(LOW), cross.astype(LOW)
    by_near = swap_dp(cross[:half], 1)
    by_far = swap_dp(cross[half:], 2)
    near_first = swap_dp(near[:half], 1)
    far_second = swap_dp(far[half:], 2)
    far_first = swap_dp((far[:half].astype(FULL) + by_near.astype(FULL)).astype(LOW), 2)
    near_second = swap_dp((near[half:].astype(FULL) + by_far.astype(FULL)).astype(LOW), 1)
    return own + jnp.concatenate(
        [
            near_first.astype(FULL) + far_first.astype(FULL),
            near_second.astype(FULL) + far_second.astype(FULL),
        ]
    )


def line_up(parts, width):
    rows = parts[0].shape[0]
    whole = jnp.zeros((rows, len(parts) * width), parts[0].dtype)
    for part, who in zip(parts, part_members()):
        whole = lax.dynamic_update_slice_in_dim(whole, part, who * width, 1)
    return whole


def cut_up(value, width):
    return [lax.dynamic_slice_in_dim(value, who * width, width, 1) for who in part_members()]


def is_line():
    return lax.axis_size("grp") == 8


def chip_shift(value, steps):
    pairs = []
    for chip in range(4):
        if 0 <= chip + steps < 4:
            pairs += [(2 * chip + core, 2 * (chip + steps) + core) for core in range(2)]
    return lax.ppermute(value, "grp", pairs)


def core_swap(value):
    return lax.ppermute(value, "grp", [(a, a ^ 1) for a in range(8)])


def gather_earlier(value):
    sequences, rows, width = value.shape
    member = lax.axis_index("grp")
    chunks = ROW_LENGTH // KEY_CHUNK
    if not is_line() or rows != KEY_CHUNK:
        whole = lax.all_gather(value, "grp", axis=1, tiled=True)
        return whole, jnp.arange(chunks, dtype=jnp.int32)
    pieces = [value] + [chip_shift(value, steps) for steps in range(1, 4)]
    pieces += [core_swap(piece) for piece in pieces]
    order = jnp.arange(chunks, dtype=jnp.int32)
    other_core = (order % 2 != member % 2).astype(jnp.int32)
    spots = 4 * other_core + jnp.maximum(member // 2 - order // 2, 0)
    return jnp.concatenate(pieces, axis=1), spots


def scatter_earlier(terms, meanwhile):
    sequences, row_length, width = terms.shape
    if not is_line() or ROW_LENGTH // 8 != KEY_CHUNK:
        return lax.psum_scatter(terms, "grp", scatter_dimension=1, tiled=True).astype(FULL)
    kept, given = terms[:, : row_length // 2], terms[:, row_length // 2 :]
    swapped = after(core_swap(given), meanwhile)
    chip_sums = kept.astype(FULL) + swapped.astype(FULL)
    total = chip_sums[:, :KEY_CHUNK]
    for steps in range(3, 0, -1):
        some = chip_sums[:, steps * KEY_CHUNK : (steps + 1) * KEY_CHUNK]
        total = total + chip_shift(some.astype(LOW), -steps).astype(FULL)
    return total


def line_terms(sums, step, upward, downward):
    chip = lax.axis_index("grp") // 2
    up, down = of_chip(sums, chip + 4 - step), of_chip(sums, chip - 4 + step)
    if step > 1:
        up = (up.astype(FULL) + upward.astype(FULL)).astype(LOW)
        down = (down.astype(FULL) + downward.astype(FULL)).astype(LOW)
    return up, down


def line_step(up, down, step):
    up_pairs = [(2 * c + k, 2 * c + 2 + k) for c in range(step) for k in range(2)]
    down_pairs = [(2 * c + k, 2 * c - 2 + k) for c in range(4 - step, 4) for k in range(2)]
    return lax.ppermute(up, "grp", up_pairs), lax.ppermute(down, "grp", down_pairs)


def of_chip(sums, index):
    return lax.dynamic_index_in_dim(sums, jnp.clip(index, 0, 3), 0, keepdims=False)


def sum_everywhere(value):
    if lax.axis_size("dp") != 4 or not is_line():
        return lax.psum(value, ("dp", "grp"))
    value = value + swap_dp(value, 1)
    value = value + swap_dp(value, 2)
    value = value + core_swap(value)
    total = value
    for steps in range(1, 4):
        pairs = [(a, (a + 2 * steps) % 8) for a in range(8)]
        total = total + lax.ppermute(value, "grp", pairs)
    return total


ANY_SPEC = pl.BlockSpec(memory_space=pltpu.HBM)
READ_GROUPS = 8


def move(source, target, sem, start):
    copy = pltpu.make_async_copy(source, target, sem)
    if start:
        copy.start()
    else:
        copy.wait()


def block_call(kernel, name, table, inputs, outputs, count, piece, aliases=None, spare=4):
    hold = pltpu.VMEM((count, piece, D), LOW)
    return pl.pallas_call(
        kernel,
        grid_spec=pltpu.PrefetchScalarGridSpec(
            num_scalar_prefetch=1,
            grid=(1,),
            in_specs=[ANY_SPEC] * len(inputs),
            out_specs=[ANY_SPEC] * len(outputs),
            scratch_shapes=[hold, pltpu.SemaphoreType.DMA((READ_GROUPS,)), pltpu.SemaphoreType.DMA],
        ),
        out_shape=outputs,
        input_output_aliases=aliases or {},
        compiler_params=pltpu.CompilerParams(
            vmem_limit_bytes=2 * count * piece * D + spare * 1024 * 1024
        ),
        cost_estimate=pl.CostEstimate(
            flops=0, bytes_accessed=4 * count * piece * D, transcendentals=0
        ),
        name=name,
    )(table, *inputs)


def pick_kernel(at_ref, early_ref, late_ref, *refs):
    outs, hold, read_sems, write_sem = refs[:2], refs[2], refs[3], refs[4]
    count = 3 * FF_BLOCKS
    half = FF_BLOCKS // 2
    early_slots, late_slots = at_ref[2 * count], at_ref[2 * count + 1]
    stages = [(0, 0, low) for low in range(0, 2 * FF_BLOCKS, half)]
    stages += [(1, 2 * FF_BLOCKS, low) for low in (0, half)]
    for group, (_, first, low) in enumerate(stages):

        @pl.loop(first + low, first + low + half)
        def _(block):
            owner, slot = at_ref[block], at_ref[count + block]

            @pl.when(slot < early_slots)
            def _():
                source = early_ref.at[owner * early_slots + slot]
                move(source, hold.at[block], read_sems.at[group], True)

            @pl.when(slot >= early_slots)
            def _():
                source = late_ref.at[owner * late_slots + slot - early_slots]
                move(source, hold.at[block], read_sems.at[group], True)

    for start in (True, False):
        for group, (index, first, low) in enumerate(stages):
            some = hold.at[pl.ds(first + low, half)]
            if start:
                move(some, some, read_sems.at[group], False)
            move(some, outs[index].at[pl.ds(low, half)], write_sem, start)


def pick_blocks(owners, slots, early, late, early_slots, late_slots):
    table = jnp.concatenate([owners, slots, jnp.array([early_slots, late_slots], jnp.int32)])
    piece = early.shape[1]
    outs = [jax.ShapeDtypeStruct((count * FF_BLOCKS, piece, D), LOW) for count in (2, 1)]
    return block_call(
        pick_kernel, "pick_blocks", table, (early, late), outs, 3 * FF_BLOCKS, piece, spare=16
    )


def pick_early_kernel(
    team, at_ref, early_ref, query_ref, kv_ref, out_ref, hold, read_sems, write_sem
):
    early_slots = at_ref[2 * GATE_AT]
    share = D // team
    stages = (
        (0, KEY_AT, query_ref, True),
        (KEY_AT, OUT_AT, kv_ref, False),
        (OUT_AT, GATE_AT, out_ref, True),
    )
    for group, (low, high, _, _) in enumerate(stages):

        @pl.loop(low, high)
        def _(block):
            source = early_ref.at[at_ref[block] * early_slots + at_ref[GATE_AT + block]]
            move(source, hold.at[block], read_sems.at[group], True)

    for start in (True, False):
        for group, (low, high, target, by_columns) in enumerate(stages):
            some = pl.ds(low, high - low)
            if start:
                move(hold.at[some], hold.at[some], read_sems.at[group], False)
            if by_columns:
                for band in range(team):
                    lanes = pl.ds(band * share, share)
                    move(hold.at[some, :, lanes], target.at[:, band], write_sem, start)
            else:
                move(hold.at[some], target, write_sem, start)


def pick_early(owners, slots, early, early_slots, team):
    piece = early.shape[1]
    columns = jax.ShapeDtypeStruct((MODEL_BLOCKS, team, piece, D // team), LOW)
    rows = jax.ShapeDtypeStruct((2 * KV_BLOCKS, piece, D), LOW)
    return block_call(
        functools.partial(pick_early_kernel, team),
        "pick_early",
        jnp.concatenate([owners, slots, jnp.array([early_slots], jnp.int32)]),
        (early,),
        [columns, rows, columns],
        GATE_AT,
        piece,
    )


def assemble_kernel(order_ref, *refs):
    count = len(refs) - 4
    parts, whole, hold, read_sems, write_sem = refs[:count], refs[-4], refs[-3], refs[-2], refs[-1]
    rows, width = parts[0].shape
    band = rows // 4
    for start in (True, False):
        for group in range(4):
            some = pl.ds(group * band, band)
            for index, part in enumerate(parts):
                lanes = pl.ds(pl.multiple_of(order_ref[index] * width, width), width)
                move(part.at[some], hold.at[some, lanes], read_sems.at[group], start)
            if not start:
                move(hold.at[some], whole.at[some], write_sem, True)
    move(hold, whole, write_sem, False)


def assemble_columns(parts):
    rows, width = parts[0].shape
    wide = width * len(parts)
    return pl.pallas_call(
        assemble_kernel,
        grid_spec=pltpu.PrefetchScalarGridSpec(
            num_scalar_prefetch=1,
            grid=(1,),
            in_specs=[ANY_SPEC] * len(parts),
            out_specs=ANY_SPEC,
            scratch_shapes=[
                pltpu.VMEM((rows, wide), LOW),
                pltpu.SemaphoreType.DMA((4,)),
                pltpu.SemaphoreType.DMA,
            ],
        ),
        out_shape=jax.ShapeDtypeStruct((rows, wide), LOW),
        compiler_params=pltpu.CompilerParams(vmem_limit_bytes=2 * rows * wide + 4 * 1024 * 1024),
        cost_estimate=pl.CostEstimate(
            flops=0, bytes_accessed=4 * rows * wide, transcendentals=0
        ),
        name="assemble_columns",
    )(jnp.stack(part_members()), *parts)


def in_cut(targets, core, outs, owner, slot, act):
    for (low, high, side), out_ref in zip(targets, outs):
        here = (slot >= low) & (slot < high)
        row = owner
        if side is not None:
            here = here & ((owner % 2 == core) if side == 0 else (owner % 2 != core))
            row = owner // 2

        @pl.when(here)
        def _():
            act(out_ref.at[row * (high - low) + slot - low])


def target_shape(target, piece):
    low, high, side = target
    owners = lax.axis_size("grp") // (1 if side is None else 2)
    return jax.ShapeDtypeStruct((owners * (high - low), piece, D), LOW)


def place_ff_kernel(targets, at_ref, *refs):
    terms, outs = refs[:2], refs[2:-3]
    hold, read_sems, write_sem = refs[-3:]
    count = 3 * FF_BLOCKS
    half = FF_BLOCKS // 2
    stages = [(0, 0, low) for low in range(0, 2 * FF_BLOCKS, half)]
    stages += [(1, 2 * FF_BLOCKS, low) for low in (0, half)]
    for start in (True, False):
        for group, (index, first, low) in enumerate(stages):
            target = hold.at[pl.ds(first + low, half)]
            move(terms[index].at[pl.ds(low, half)], target, read_sems.at[group], start)
            if start:
                continue

            @pl.loop(first + low, first + low + half)
            def _(block):
                in_cut(
                    targets,
                    at_ref[2 * count],
                    outs,
                    at_ref[block],
                    at_ref[count + block],
                    lambda target: move(hold.at[block], target, write_sem, True),
                )

    move(hold, hold, write_sem, False)


def place_ff(owners, slots, terms, targets):
    piece = terms[0].shape[1]
    return block_call(
        functools.partial(place_ff_kernel, targets),
        "place_ff",
        jnp.concatenate([owners, slots, lax.axis_index("grp")[None] % 2]),
        terms,
        [target_shape(target, piece) for target in targets],
        3 * FF_BLOCKS,
        piece,
    )


def place_more_kernel(team, targets, kinds, at_ref, *refs):
    sources, outs = refs[: len(kinds)], refs[-3 - len(targets) : -3]
    hold, read_sems, write_sem = refs[-3:]
    share = D // team
    total = sum(count for count, _ in kinds)

    def write(block, start):
        in_cut(
            targets,
            at_ref[2 * total],
            outs,
            at_ref[block],
            at_ref[total + block],
            lambda target: move(hold.at[block], target, write_sem, start),
        )

    for start in (True, False):
        low = 0
        for group, ((count, by_columns), source) in enumerate(zip(kinds, sources)):
            some = pl.ds(low, count)
            if by_columns:
                for band in range(team):
                    lanes = pl.ds(band * share, share)
                    move(source.at[:, band], hold.at[some, :, lanes], read_sems.at[group], start)
            else:
                move(source, hold.at[some], read_sems.at[group], start)
            if not start:

                @pl.loop(low, low + count)
                def _(block):
                    write(block, True)

            low += count

    @pl.loop(0, total)
    def _(block):
        write(block, False)


def place_more(name, owners, slots, terms, kinds, placed, targets, team):
    piece = placed[0].shape[1]
    return block_call(
        functools.partial(place_more_kernel, team, targets, kinds),
        name,
        jnp.concatenate([owners, slots, lax.axis_index("grp")[None] % 2]),
        (*terms, *placed),
        [jax.ShapeDtypeStruct(part.shape, LOW) for part in placed],
        sum(count for count, _ in kinds),
        piece,
        {1 + len(terms) + index: index for index in range(len(placed))},
    )


def adamw_kernel(team, first_slot, at_ref, master, first, second, *refs):
    parts = refs[:team]
    new_master, new_first, new_second, copy, shares = refs[-5:]
    kind = at_ref[team + first_slot + pl.program_id(0)]
    piece, share = R // team, D // team
    for index in range(team):
        shares[at_ref[index]] = parts[index][0]

    def update(rows, lanes, gradient):
        results = adamw(
            master[0, rows, lanes], first[0, rows, lanes], second[0, rows, lanes],
            gradient, WEIGHT_RATE, WEIGHT_DECAY,
        )
        for target, value in zip((new_master, new_first, new_second), results):
            target[0, rows, lanes] = value
        copy[0, rows, lanes] = results[0].astype(LOW)

    for band in range(team):
        rows = slice(band * piece, (band + 1) * piece)

        @pl.when(kind == 1)
        def _():
            update(rows, slice(0, D), shares[band].astype(FULL))

        @pl.when(kind == 2)
        def _():
            for index in range(team):
                lanes = slice(index * share, (index + 1) * share)
                update(rows, lanes, shares[index, :, band * share : (band + 1) * share].astype(FULL))

        @pl.when(kind == 0)
        def _():
            update(rows, slice(0, D), jnp.zeros((piece, D), FULL))


def adamw_slots(kinds, master, first, second, parts, first_slot, so_far):
    team = len(parts)
    count = parts[0].shape[0]
    slot_spec = pl.BlockSpec((1, R, D), lambda i, a: (first_slot + i, 0, 0))
    part_spec = pl.BlockSpec((1, R // team, D), lambda i, a: (i, 0, 0))
    whole = jax.ShapeDtypeStruct(master.shape, FULL)
    extra = [] if so_far is None else list(so_far)
    return pl.pallas_call(
        functools.partial(adamw_kernel, team, first_slot),
        grid_spec=pltpu.PrefetchScalarGridSpec(
            num_scalar_prefetch=1,
            grid=(count,),
            in_specs=[slot_spec] * 3 + [part_spec] * team + [ANY_SPEC] * len(extra),
            out_specs=[slot_spec] * 4,
            scratch_shapes=[pltpu.VMEM((team, R // team, D), LOW)],
        ),
        out_shape=[whole, whole, whole, jax.ShapeDtypeStruct(master.shape, LOW)],
        input_output_aliases={4 + team + k: k for k in range(len(extra))},
        compiler_params=pltpu.CompilerParams(vmem_limit_bytes=40 * 1024 * 1024),
        cost_estimate=pl.CostEstimate(
            flops=20 * count * R * D, bytes_accessed=28 * count * R * D, transcendentals=0
        ),
        name="adamw_slots",
    )(jnp.concatenate([jnp.stack(part_members()), kinds]), master, first, second, *parts, *extra)


def after(value, *others):
    return lax.optimization_barrier((value,) + others)[0]


def per_device(
    layer_input,
    out_cotangent,
    seq_lengths,
    block_owner,
    weight_master,
    weight_first,
    weight_second,
    gain_master,
    gain_first,
    gain_second,
):
    slot_count = weight_master.shape[0]
    team = lax.axis_size("dp")
    rank = lax.axis_index("dp")
    member = lax.axis_index("grp")
    piece = R // team
    sequence_count = layer_input.shape[0]
    segment_rows = layer_input.shape[1]
    token_count = sequence_count * segment_rows
    model_share = D // team
    kv_share = KEY_VALUE_WIDTH // team
    ff_share = FF // team
    early_slots = slot_count * 5 // 12
    late_slots = slot_count - early_slots
    first_slots = slot_count * 7 // 24
    sides = (0, 1) if is_line() and team == 4 else (None,)
    targets = tuple((0, first_slots, side) for side in sides) + (
        (first_slots, early_slots, None),
        (early_slots, slot_count, None),
    )

    block_order = jnp.arange(BLOCKS, dtype=jnp.int32)
    same_owner = block_owner[:, None] == block_owner[None, :]
    earlier = block_order[None, :] < block_order[:, None]
    slots = jnp.sum((same_owner & earlier).astype(jnp.int32), axis=1)
    whole_columns = (block_order < KEY_AT) | ((block_order >= OUT_AT) & (block_order < GATE_AT))
    block_kind = jnp.where(whole_columns, 2, 1)
    mine = (block_owner == member)[None, :] & (
        slots[None, :] == jnp.arange(slot_count, dtype=jnp.int32)[:, None]
    )
    kinds = jnp.sum(jnp.where(mine, block_kind[None, :], 0), axis=1)
    my_attention = jnp.any(mine & (block_order < GATE_AT)[None, :], axis=1)
    spills = jnp.any(slots[:OUT_AT] >= first_slots) | jnp.any(slots[OUT_AT:GATE_AT] >= early_slots)

    def shares_of(low, high):
        count = high - low
        by_rows = lax.dynamic_slice(weight_master, (low, rank * piece, 0), (count, piece, D))
        by_columns = lax.dynamic_slice(
            weight_master, (low, 0, rank * model_share), (count, R, model_share)
        ).astype(LOW)
        by_columns = jnp.concatenate(
            [by_columns[:, j * piece : (j + 1) * piece] for j in range(team)], axis=-1
        )
        return jnp.where((kinds[low:high] == 2)[:, None, None], by_columns, by_rows.astype(LOW))

    shares_early = shares_of(0, early_slots)
    shares_late = shares_of(early_slots, slot_count)
    gathered_early = lax.all_gather(shares_early, "grp", axis=0, tiled=True)
    gathered_late = lax.all_gather(shares_late, "grp", axis=0, tiled=True)
    gains_all = lax.all_gather(gain_master.astype(LOW), "grp", axis=1, tiled=True)

    positions = member * segment_rows + jnp.arange(segment_rows, dtype=jnp.int32)
    valid_rows = (positions[None, :] < seq_lengths[:, None]).reshape(token_count, 1)
    cosine_rows, sine_rows = rotary_tables(positions, HEAD_WIDTH)
    wide_cosine = jnp.concatenate([cosine_rows] * 4, axis=1)
    wide_sine = jnp.concatenate([-sine_rows, sine_rows] * 2, axis=1)
    places = jnp.concatenate(
        [jnp.stack([member * segment_rows, jnp.int32(segment_rows)]), seq_lengths]
    ).astype(jnp.int32)
    inputs = layer_input.reshape(token_count, D).astype(FULL)
    root_one = lax.rsqrt(jnp.mean(inputs * inputs, axis=-1, keepdims=True) + NORM_EPS)
    normed_one = inputs * root_one
    gain_one = gains_all[0].astype(FULL)
    gain_two = gains_all[1].astype(FULL)
    hidden_one = (normed_one * gain_one).astype(LOW)
    hidden_one_all = gather_dp(hidden_one)
    grad_out = jnp.where(valid_rows, out_cotangent.reshape(token_count, D), jnp.zeros((), LOW))
    grad_out_all = gather_dp(after(grad_out, hidden_one_all))
    gathered_early = after(gathered_early, hidden_one_all, grad_out_all)

    def attention_early():
        return tuple(
            pick_early(block_owner[:GATE_AT], slots[:GATE_AT], gathered_early, early_slots, team)
        )

    def attention_spilled():
        everything = lax.all_gather(
            jnp.concatenate([shares_early, shares_late]), "grp", axis=0, tiled=True
        )
        found = jnp.take(
            everything, (block_owner * slot_count + slots)[:GATE_AT], axis=0, mode="clip"
        )

        def columns(first):
            chosen = found[first : first + MODEL_BLOCKS]
            return chosen.reshape(MODEL_BLOCKS, piece, team, model_share).transpose(0, 2, 1, 3)

        return columns(0), found[KEY_AT:OUT_AT], columns(OUT_AT)

    query_share, kv_rows, out_share = lax.cond(spills, attention_spilled, attention_early)
    query_share = query_share.reshape(D, model_share)
    kv_rows = kv_rows.reshape(2 * kv_share, D)
    out_share = out_share.reshape(D, model_share)


    kv_shares = contract_rows(hidden_one_all, kv_rows).astype(LOW)
    kv_parts = exchange_parts(split_parts(kv_shares))
    query_shares = plain_dot(after(hidden_one_all, kv_shares), query_share).astype(LOW)
    query_parts = exchange_parts(split_parts(query_shares))
    kv_proj = (
        line_up(kv_parts, 2 * kv_share)
        .reshape(token_count, team, 2 * KV_BLOCKS, piece)
        .transpose(0, 2, 1, 3)
        .reshape(token_count, 2 * KEY_VALUE_WIDTH)
    )
    keys_local = apply_rotation(
        kv_proj[:, :KEY_VALUE_WIDTH]
        .astype(FULL)
        .reshape(sequence_count, segment_rows, KEY_VALUE_HEADS, HEAD_WIDTH),
        cosine_rows,
        sine_rows,
    ).astype(LOW)
    kv_local = jnp.concatenate(
        [
            keys_local.reshape(sequence_count, segment_rows, KEY_VALUE_WIDTH),
            kv_proj[:, KEY_VALUE_WIDTH:].reshape(sequence_count, segment_rows, KEY_VALUE_WIDTH),
        ],
        axis=-1,
    )
    kv_all, spots = gather_earlier(kv_local)
    query_proj = line_up(query_parts, model_share).reshape(sequence_count, segment_rows, D)
    w_out = assemble_columns(gather_parts(after(out_share, query_proj, kv_local)))

    attended, logs = attend_forward(places, spots, wide_cosine, wide_sine, query_proj, kv_all)
    attended_flat = attended.reshape(token_count, D)
    residual = inputs + plain_dot(attended_flat, w_out)
    root_two = lax.rsqrt(jnp.mean(residual * residual, axis=-1, keepdims=True) + NORM_EPS)
    normed_two = residual * root_two
    hidden_two = (normed_two * gain_two).astype(LOW)

    hidden_two_parts = gather_direct(hidden_two)
    ff_blocks = pick_blocks(
        block_owner[GATE_AT:],
        slots[GATE_AT:],
        gathered_early,
        after(gathered_late, hidden_two),
        early_slots,
        late_slots,
    )
    w_both, w_down = ff_blocks[0].reshape(2 * ff_share, D), ff_blocks[1].reshape(ff_share, D)
    grad_out_parts = split_parts(grad_out_all)
    inner = jnp.zeros((team * token_count, ff_share), LOW)
    grad_both = jnp.zeros((team * token_count, 2 * ff_share), LOW)
    inner_parts, grad_htwo_parts = [], []
    for index, (hidden, given) in enumerate(zip(hidden_two_parts, grad_out_parts)):
        if index > 0:
            hidden = after(hidden, grad_htwo_parts[-1])
        both = contract_rows(hidden, w_both)
        gate_pre, up_pre = both[:, :ff_share], both[:, ff_share:]
        sigmoid_gate = jax.nn.sigmoid(gate_pre)
        activated = gate_pre * sigmoid_gate
        inner_parts.append((activated * up_pre).astype(LOW))
        grad_inner = contract_rows(given, w_down)
        grad_gate = grad_inner * up_pre * (sigmoid_gate * (1.0 + gate_pre * (1.0 - sigmoid_gate)))
        grad_up = grad_inner * activated
        grad_part = jnp.concatenate([grad_gate.astype(LOW), grad_up.astype(LOW)], axis=1)
        part = plain_dot(grad_part, w_both)
        grad_htwo_parts.append(part if index == 0 else part.astype(LOW))
        first = index * token_count
        inner = lax.dynamic_update_slice(inner, inner_parts[-1], (first, 0))
        grad_both = lax.dynamic_update_slice(grad_both, grad_part, (first, 0))
    grad_htwo_sent = send_parts(grad_htwo_parts)
    grad_htwo = add_up(grad_htwo_sent[0], grad_htwo_sent[1:])
    hidden_two_all = jnp.concatenate(hidden_two_parts, axis=0)
    inner_parts = lax.optimization_barrier((inner_parts, grad_htwo_parts[-1]))[0]
    down_parts = [plain_dot(part, w_down) for part in inner_parts]
    down_parts = down_parts[:1] + [part.astype(LOW) for part in down_parts[1:]]
    grad_both = after(grad_both, grad_htwo_sent[1], *down_parts)
    both_terms = contract_first(grad_both, hidden_two_all).astype(LOW)
    inner = after(inner, both_terms, *grad_htwo_sent[1:])
    ff_terms = [
        both_terms.reshape(-1, piece, D),
        contract_first(inner, grad_out_all).astype(LOW).reshape(-1, piece, D),
    ]
    down_parts = [after(part, *grad_htwo_sent[1:]) for part in down_parts]
    down_sent = send_parts(down_parts)
    cut_terms = place_ff(block_owner[GATE_AT:], slots[GATE_AT:], ff_terms, targets)
    late_terms = cut_terms[-1]
    late_sums = lax.psum_scatter(late_terms, "grp", scatter_dimension=0, tiled=True)

    grad_htwo = after(grad_htwo, late_terms)
    scaled_two = grad_htwo * gain_two
    grad_resid = grad_out.astype(FULL) + root_two * (
        scaled_two - normed_two * jnp.mean(scaled_two * normed_two, axis=-1, keepdims=True)
    )
    resid_low = grad_resid.astype(LOW)
    grad_attended = contract_rows(resid_low, w_out).astype(LOW)
    down_sent, grad_attended = lax.optimization_barrier((down_sent, grad_attended))
    crossing = exchange_parts(
        [
            jnp.concatenate([after(attended_flat, grad_attended), share], axis=1)
            for share in cut_up(resid_low, model_share)
        ]
    )
    grad_query, kv_terms = attend_backward(
        places,
        spots,
        wide_cosine,
        wide_sine,
        query_proj,
        kv_all,
        attended,
        grad_attended.reshape(sequence_count, segment_rows, D),
        logs,
    )
    grad_query, kv_terms, crossing = lax.optimization_barrier((grad_query, kv_terms, crossing))
    attended_all = jnp.concatenate([part[:, :D] for part in crossing], axis=0)
    resid_share = jnp.concatenate([part[:, D:] for part in crossing], axis=0)
    column_shape = (MODEL_BLOCKS, team, piece, model_share)
    out_terms = contract_first(attended_all, resid_share).astype(LOW).reshape(column_shape)
    *early_terms, middle_terms = place_more(
        "place_out",
        block_owner[OUT_AT:GATE_AT],
        slots[OUT_AT:GATE_AT],
        (out_terms,),
        ((MODEL_BLOCKS, True),),
        cut_terms[:-1],
        targets[:-1],
        team,
    )
    query_share_parts = exchange_parts(cut_up(grad_query.reshape(token_count, D), model_share))
    grad_query_share = jnp.concatenate(query_share_parts, axis=0)
    key_value_sums = scatter_earlier(kv_terms, middle_terms)
    grad_keys = apply_rotation(
        key_value_sums[:, :, :KEY_VALUE_WIDTH].reshape(
            sequence_count, segment_rows, KEY_VALUE_HEADS, HEAD_WIDTH
        ),
        cosine_rows,
        -sine_rows,
    ).reshape(token_count, KEY_VALUE_WIDTH)
    grad_values = key_value_sums[:, :, KEY_VALUE_WIDTH:].reshape(token_count, KEY_VALUE_WIDTH)
    grad_kv = (
        jnp.concatenate([grad_keys, grad_values], axis=1)
        .astype(LOW)
        .reshape(token_count, 2 * KV_BLOCKS, team, piece)
        .transpose(0, 2, 1, 3)
        .reshape(token_count, 2 * KEY_VALUE_WIDTH)
    )
    grad_kv_share = jnp.concatenate(exchange_parts(cut_up(grad_kv, 2 * kv_share)), axis=0)

    query_terms = contract_first(hidden_one_all, grad_query_share).astype(LOW)
    kv_weight_terms = contract_first(grad_kv_share, hidden_one_all).astype(LOW)
    attention_terms = [
        query_terms.reshape(column_shape),
        kv_weight_terms.reshape(2 * KV_BLOCKS, piece, D),
        out_terms,
    ]
    early_terms = place_more(
        "place_query",
        block_owner[:OUT_AT],
        slots[:OUT_AT],
        attention_terms[:2],
        ((MODEL_BLOCKS, True), (2 * KV_BLOCKS, False)),
        early_terms,
        targets[:-2],
        team,
    )

    def nothing_spilled():
        return jnp.zeros((late_slots, piece, D), LOW), jnp.zeros(
            (early_slots - first_slots, piece, D), LOW
        )

    def sums_spilled():
        by_columns = [
            attention_terms[k].transpose(0, 2, 1, 3).reshape(MODEL_BLOCKS, piece, D) for k in (0, 2)
        ]
        found = jnp.concatenate([by_columns[0], attention_terms[1], by_columns[1]], axis=0)
        every_slot = jnp.arange(slot_count * lax.axis_size("grp"), dtype=jnp.int32)
        hits = (block_owner * slot_count + slots)[None, :GATE_AT] == every_slot[:, None]
        which = jnp.sum(jnp.where(hits, block_order[None, :GATE_AT], 0), axis=1)
        spread = jnp.where(
            jnp.any(hits, axis=1)[:, None, None],
            jnp.take(found, which, axis=0, mode="clip"),
            jnp.zeros((), LOW),
        )
        extra = lax.psum_scatter(spread, "grp", scatter_dimension=0, tiled=True)
        return extra[early_slots:], extra[first_slots:early_slots]

    late_extra, middle_extra = lax.cond(
        after(spills, late_sums, early_terms[0]), sums_spilled, nothing_spilled
    )

    def with_extra(low, high, sums, extra):
        spilled = spills & my_attention[low:high]
        return jnp.where(spilled[:, None, None], extra, sums)

    late_sums = with_extra(early_slots, slot_count, late_sums, late_extra)
    late_half = late_slots // 2
    half = (first_slots + 1) // 2
    states = (weight_master, weight_first, weight_second)

    def query_gradient(share):
        return contract_rows(share, query_share) + plain_dot(grad_kv_share, kv_rows)

    def finish_input(grad_hone):
        scaled_one = grad_hone * gain_one
        spread = jnp.mean(scaled_one * normed_one, axis=-1, keepdims=True)
        input_grad = grad_resid + root_one * (scaled_one - normed_one * spread)
        gain_terms = [
            jnp.sum(grad_hone * normed_one, axis=0), jnp.sum(grad_htwo * normed_two, axis=0)
        ]
        return (
            input_grad.astype(LOW).reshape(sequence_count, segment_rows, D),
            jnp.stack(gain_terms),
        )

    def finish_output(sent):
        output = residual + add_up(sent[0], sent[1:])
        return (
            jnp.where(valid_rows, output, 0.0)
            .astype(LOW)
            .reshape(sequence_count, segment_rows, D)
        )

    def middle_total(terms):
        sums = lax.psum_scatter(terms, "grp", scatter_dimension=0, tiled=True)
        return with_extra(first_slots, early_slots, sums, middle_extra)

    def update(parts, low, updated):
        return adamw_slots(kinds, *states, parts, low, updated)

    if is_line() and team == 4:
        tie = lax.optimization_barrier
        kept, given = early_terms
        given, late_sums, middle_terms, grad_query_share = tie(
            (given, late_sums, middle_terms, grad_query_share)
        )
        swapped = core_swap(given)
        first, second = late_sums[:late_half], late_sums[late_half:]
        first_near = near_far(first)
        middle_sums = middle_total(middle_terms)
        grad_hone = query_gradient(grad_query_share)
        swapped, grad_hone = tie((swapped, grad_hone))
        sums = (kept.astype(FULL) + swapped.astype(FULL)).astype(LOW)
        sums = sums.reshape(4, first_slots, piece, D)
        up, down = line_terms(sums, 1, None, None)
        upward, downward = line_step(up, down, 1)
        second, *first_near, _, _ = tie((second, *first_near, up, down))
        first_cross = cross_of(*first_near)
        second_near = near_far(second)
        *down_sent, _ = tie((*down_sent, second))
        layer_output = finish_output(down_sent)
        upward, downward, layer_output = tie((upward, downward, layer_output))
        up, down = line_terms(sums, 2, upward, downward)
        upward, downward = line_step(up, down, 2)
        *second_near, _, _ = tie((*second_near, up, down))
        second_cross = cross_of(*second_near)
        parts = [first, *first_near, jnp.concatenate(first_cross, axis=0)]
        parts, second_near = tie((parts, second_near))
        updated = update(parts, early_slots, None)
        upward, downward, middle_sums, grad_hone, *updated = tie(
            (upward, downward, middle_sums, grad_hone, *updated)
        )
        up, down = line_terms(sums, 3, upward, downward)
        upward, downward = line_step(up, down, 3)
        middle_near = near_far(middle_sums) + [swap_dp(middle_sums, 3)]
        own, near, far, cross = split_parts(grad_hone)
        rows = token_count // 2
        near, far, cross = near.astype(LOW), far.astype(LOW), cross.astype(LOW)
        hone_sent = [
            swap_dp(near[:rows], 1), swap_dp(cross[:rows], 1),
            swap_dp(far[rows:], 2), swap_dp(cross[rows:], 2),
        ]
        parts = [second, *second_near, jnp.concatenate(second_cross, axis=0)]
        parts, _, _, near, far, updated = tie((parts, up, down, near, far, updated))
        updated = update(parts, early_slots + late_half, updated)
        upward, downward, *updated = tie((upward, downward, *updated))
        early_sums = of_chip(sums, member // 2).astype(FULL)
        early_sums = (early_sums + upward.astype(FULL) + downward.astype(FULL)).astype(LOW)
        early = [early_sums[:half], early_sums[half:]]
        early_near = [near_far(part) for part in early]
        *hone_sent, _ = tie((*hone_sent, early_sums))
        far_first = (far[:rows].astype(FULL) + hone_sent[1].astype(FULL)).astype(LOW)
        near_second = (near[rows:].astype(FULL) + hone_sent[3].astype(FULL)).astype(LOW)
        hone_more = [swap_dp(far_first, 2), swap_dp(near_second, 1)]
        parts = [middle_sums, *middle_near]
        parts, _, _, updated = tie((parts, far_first, near_second, updated))
        updated = update(parts, first_slots, updated)
        early_near, updated = tie((early_near, updated))
        early_cross = [cross_of(*parts) for parts in early_near]
        hone_more, early_near = tie((hone_more, early_near))
        grad_hone = own + jnp.concatenate(
            [
                hone_sent[0].astype(FULL) + hone_more[0].astype(FULL),
                hone_more[1].astype(FULL) + hone_sent[2].astype(FULL),
            ]
        )
        input_grad, gain_terms = finish_input(grad_hone)
        input_grad, gain_terms, early_cross = tie((input_grad, gain_terms, early_cross))
        gain_grad = sum_everywhere(gain_terms)
        for low, part, beside, across_parts in zip((0, half), early, early_near, early_cross):
            parts = [part, *beside, jnp.concatenate(across_parts, axis=0)]
            updated = update(parts, low, updated)
    else:
        updated = update(gather_parts(late_sums), early_slots, None)
        updated = update(gather_parts(middle_total(middle_terms)), first_slots, updated)
        early_sums = lax.psum_scatter(early_terms[0], "grp", scatter_dimension=0, tiled=True)
        updated = update(gather_parts(early_sums), 0, updated)
        input_grad, gain_terms = finish_input(scatter_dp(query_gradient(grad_query_share)))
        gain_grad = sum_everywhere(gain_terms)
        layer_output = finish_output(down_sent)
    new_master, new_first, new_second, weight_copy = updated

    share_width = gain_master.shape[1]
    gain_share = lax.dynamic_slice_in_dim(gain_grad, member * share_width, share_width, 1)
    new_gain, new_gain_first, new_gain_second = adamw(
        gain_master, gain_first, gain_second, gain_share, GAIN_RATE, 0.0
    )
    return (
        layer_output,
        input_grad,
        new_master,
        new_first,
        new_second,
        weight_copy,
        new_gain,
        new_gain_first,
        new_gain_second,
    )


def solution(mesh):
    return jax.shard_map(
        per_device,
        mesh=mesh,
        in_specs=(
            P("dp", "grp", None),
            P("dp", "grp", None),
            P("dp"),
            P(),
            P("grp", None, None),
            P("grp", None, None),
            P("grp", None, None),
            P(None, "grp"),
            P(None, "grp"),
            P(None, "grp"),
        ),
        out_specs=(
            P("dp", "grp", None),
            P("dp", "grp", None),
            P("grp", None, None),
            P("grp", None, None),
            P("grp", None, None),
            P("grp", None, None),
            P(None, "grp"),
            P(None, "grp"),
            P(None, "grp"),
        ),
        check_vma=False,
    )
```

```python
import functools
import math

import jax
import jax.numpy as jnp
from jax import lax
from jax.experimental import pallas as pl
from jax.experimental.pallas import tpu as pltpu
from jax.sharding import PartitionSpec as P

D = 2048
QUERY_HEADS = 32
KEY_VALUE_HEADS = 4
HEAD_WIDTH = 64
FF = 5632
ROW_LENGTH = 2048
R = 128
STEP = 7
KEY_VALUE_WIDTH = 256
MODEL_BLOCKS = D // R
KV_BLOCKS = KEY_VALUE_WIDTH // R
FF_BLOCKS = FF // R
KEY_AT = MODEL_BLOCKS
OUT_AT = MODEL_BLOCKS + 2 * KV_BLOCKS
GATE_AT = OUT_AT + MODEL_BLOCKS
UP_AT = GATE_AT + FF_BLOCKS
DOWN_AT = UP_AT + FF_BLOCKS
BLOCKS = DOWN_AT + FF_BLOCKS

NORM_EPS = 1e-05
BETA_ONE = 0.9
BETA_TWO = 0.95
ADAM_EPS = 1e-08
WEIGHT_RATE = 0.1
GAIN_RATE = 0.5
WEIGHT_DECAY = 0.1
MASKED = -1e30
LOW = jnp.bfloat16
FULL = jnp.float32


def rotary_tables(positions, head_size):
    halfway = head_size // 2
    spacing = jnp.arange(halfway, dtype=FULL) * (-2.0 * math.log(10000.0) / head_size)
    angles = positions.astype(FULL)[:, None] * jnp.exp(spacing)[None, :]
    return (jnp.cos(angles), jnp.sin(angles))


def apply_rotation(values, cosine_rows, sine_rows):
    halfway = values.shape[-1] // 2
    leading = values[..., :halfway]
    trailing = values[..., halfway:]
    cos_rows = cosine_rows[:, None, :]
    sin_rows = sine_rows[:, None, :]
    return jnp.concatenate(
        [leading * cos_rows - trailing * sin_rows, trailing * cos_rows + leading * sin_rows],
        axis=-1,
    )


def contract_rows(left, right):
    return lax.dot_general(left, right, (((1,), (1,)), ((), ())), preferred_element_type=FULL)


def contract_first(left, right):
    return lax.dot_general(left, right, (((0,), (0,)), ((), ())), preferred_element_type=FULL)


def plain_dot(left, right):
    return jnp.dot(left, right, preferred_element_type=FULL)


def adamw(master, first, second, gradient, rate, decay):
    first_new = BETA_ONE * first + (1.0 - BETA_ONE) * gradient
    second_new = BETA_TWO * second + (1.0 - BETA_TWO) * gradient * gradient
    first_fix = 1.0 - BETA_ONE**STEP
    second_fix = 1.0 - BETA_TWO**STEP
    stepped = first_new / first_fix / (jnp.sqrt(second_new / second_fix) + ADAM_EPS)
    return (master - rate * (stepped + decay * master), first_new, second_new)


KEY_CHUNK = 256
GROUP_WIDTH = D // KEY_VALUE_HEADS
PAIRS = GROUP_WIDTH // 128
EXP_SCALE = math.log2(math.e) / math.sqrt(HEAD_WIDTH)


def lanes_of(shape):
    return lax.broadcasted_iota(jnp.int32, shape, len(shape) - 1)


def swap_halves(values):
    first = (lanes_of(values.shape) % HEAD_WIDTH) < HEAD_WIDTH // 2
    return jnp.where(first, pltpu.roll(values, 96, 1), pltpu.roll(values, 32, 1))


def turn(values, cosine, sine):
    return values * cosine + swap_halves(values) * sine


def chunk_bounds(where_ref):
    start, rows, length = where_ref[0], where_ref[1], where_ref[2 + pl.program_id(0)]
    free = jnp.minimum(start // KEY_CHUNK, length // KEY_CHUNK)
    last = jnp.minimum(start + rows, length)
    return free, (last + KEY_CHUNK - 1) // KEY_CHUNK, start, length


def chunk_rows(spots_ref, chunk):
    return pl.ds(pl.multiple_of(spots_ref[chunk] * KEY_CHUNK, KEY_CHUNK), KEY_CHUNK)


def stacked(block, odd):
    wide = block.astype(FULL)
    wide = jnp.where(odd, pltpu.roll(wide, 64, 1), wide)
    low = jnp.where(lanes_of(wide.shape) < HEAD_WIDTH, wide, 0.0)
    return jnp.concatenate([low, pltpu.roll(low, 64, 1)], axis=0)


def mask_of(chunk, start, length, queries):
    keys = chunk * KEY_CHUNK + lax.broadcasted_iota(jnp.int32, (KEY_CHUNK, queries), 0)
    places = start + lax.broadcasted_iota(jnp.int32, (KEY_CHUNK, queries), 1)
    allowed = (keys <= places) & (keys < length)
    return jnp.concatenate([allowed, allowed], axis=0)


def across(left, right):
    return lax.dot_general(left, right, (((1,), (1,)), ((), ())), preferred_element_type=FULL)


def attend_forward_kernel(
    where_ref, spots_ref, cos_ref, sin_ref, q_ref, k_ref, v_ref, out_ref, log_ref, turned, peaks, sums, totals
):
    queries = q_ref.shape[1]
    odd = (pl.program_id(1) % 2) == 1
    free, end, start, length = chunk_bounds(where_ref)
    for pair in range(PAIRS):
        lanes = slice(128 * pair, 128 * pair + 128)
        turned[:, lanes] = turn(q_ref[0, :, lanes].astype(FULL), cos_ref[...], sin_ref[...]).astype(LOW)
    peaks[...] = jnp.full(peaks.shape, MASKED, FULL)
    sums[...] = jnp.zeros(sums.shape, FULL)
    totals[...] = jnp.zeros(totals.shape, FULL)

    def step(chunk, masked):
        rows = chunk_rows(spots_ref, chunk)
        keys = stacked(k_ref[0, rows, :], odd).astype(LOW)
        values = stacked(v_ref[0, rows, :], odd).T.astype(LOW)
        allowed = mask_of(chunk, start, length, queries) if masked else None
        for pair in range(PAIRS):
            scores = across(keys, turned[:, 128 * pair : 128 * pair + 128]) * EXP_SCALE
            if masked:
                scores = jnp.where(allowed, scores, MASKED)
            weights, fades = [], []
            for side in range(2):
                head = slice(2 * pair + side, 2 * pair + side + 1)
                part = scores[side * KEY_CHUNK : (side + 1) * KEY_CHUNK]
                old = peaks[head, :]
                new = jnp.maximum(old, jnp.max(part, axis=0, keepdims=True))
                weight = jnp.exp2(part - new)
                fade = jnp.exp2(old - new)
                peaks[head, :] = new
                sums[head, :] = sums[head, :] * fade + jnp.sum(weight, axis=0, keepdims=True)
                weights.append(weight.astype(LOW))
                fades.append(jnp.broadcast_to(fade, (HEAD_WIDTH, queries)))
            mixed = jnp.dot(values, jnp.concatenate(weights, axis=0), preferred_element_type=FULL)
            totals[pair] = totals[pair] * jnp.concatenate(fades, axis=0) + mixed

    @pl.loop(0, free)
    def _(chunk):
        step(chunk, False)

    @pl.loop(free, end)
    def _(chunk):
        step(chunk, True)

    for pair in range(PAIRS):
        shares = [
            jnp.broadcast_to(1.0 / sums[2 * pair + side : 2 * pair + side + 1, :], (HEAD_WIDTH, queries))
            for side in range(2)
        ]
        mixed = totals[pair] * jnp.concatenate(shares, axis=0)
        out_ref[0, :, 128 * pair : 128 * pair + 128] = mixed.T.astype(LOW)
    log_ref[0] = peaks[...] + jnp.log2(sums[...])


def attend_backward_kernel(
    where_ref, spots_ref, cos_ref, sin_ref, q_ref, k_ref, v_ref, out_ref, grad_ref, log_ref,
    dq_ref, dkv_ref, turned, dots, turning, key_sums, value_sums,
):
    queries = q_ref.shape[1]
    group = pl.program_id(1)
    odd = (group % 2) == 1
    free, end, start, length = chunk_bounds(where_ref)
    for pair in range(PAIRS):
        lanes = slice(128 * pair, 128 * pair + 128)
        turned[:, lanes] = turn(q_ref[0, :, lanes].astype(FULL), cos_ref[...], sin_ref[...]).astype(LOW)
        products = (out_ref[0, :, lanes].astype(FULL) * grad_ref[0, :, lanes].astype(FULL)).T
        dots[2 * pair : 2 * pair + 1, :] = jnp.sum(products[:HEAD_WIDTH], axis=0, keepdims=True)
        dots[2 * pair + 1 : 2 * pair + 2, :] = jnp.sum(products[HEAD_WIDTH:], axis=0, keepdims=True)
    turning[...] = jnp.zeros(turning.shape, FULL)

    @pl.when(group == 0)
    def _():
        dkv_ref[...] = jnp.zeros(dkv_ref.shape, LOW)

    key_lanes = pl.ds(pl.multiple_of((group // 2) * 128, 128), 128)
    value_lanes = pl.ds(pl.multiple_of(KEY_VALUE_WIDTH + (group // 2) * 128, 128), 128)

    def step(chunk, masked):
        rows = chunk_rows(spots_ref, chunk)
        wide_keys = stacked(k_ref[0, rows, :], odd)
        keys = wide_keys.astype(LOW)
        keys_down = wide_keys.T.astype(LOW)
        values = stacked(v_ref[0, rows, :], odd).astype(LOW)
        allowed = mask_of(chunk, start, length, queries) if masked else None
        for pair in range(PAIRS):
            lanes = slice(128 * pair, 128 * pair + 128)
            asked = turned[:, lanes]
            given = grad_ref[0, :, lanes]
            scores = across(keys, asked) * EXP_SCALE
            if masked:
                scores = jnp.where(allowed, scores, MASKED)
            slopes = across(values, given)
            weights, moves = [], []
            for side in range(2):
                head = slice(2 * pair + side, 2 * pair + side + 1)
                part = slice(side * KEY_CHUNK, (side + 1) * KEY_CHUNK)
                weight = jnp.exp2(scores[part] - log_ref[0, head, :])
                weights.append(weight.astype(LOW))
                moves.append((weight * (slopes[part] - dots[head, :])).astype(LOW))
            weights = jnp.concatenate(weights, axis=0)
            moves = jnp.concatenate(moves, axis=0)
            value_part = jnp.dot(weights, given, preferred_element_type=FULL)
            key_part = jnp.dot(moves, asked, preferred_element_type=FULL)
            if pair == 0:
                value_sums[...] = value_part
                key_sums[...] = key_part
            else:
                value_sums[...] += value_part
                key_sums[...] += key_part
            turning[pair] += jnp.dot(keys_down, moves, preferred_element_type=FULL)
        for sums, lanes, scale in (
            (key_sums, key_lanes, 1.0 / math.sqrt(HEAD_WIDTH)),
            (value_sums, value_lanes, 1.0),
        ):
            both = (sums[:KEY_CHUNK] + pltpu.roll(sums[KEY_CHUNK:], 64, 1)) * scale
            low_side = lanes_of(both.shape) < HEAD_WIDTH
            kept = dkv_ref[0, rows, lanes].astype(FULL)
            mine = jnp.where(odd, pltpu.roll(both, 64, 1), both)
            dkv_ref[0, rows, lanes] = jnp.where(low_side != odd, mine, kept).astype(LOW)

    @pl.loop(0, free)
    def _(chunk):
        step(chunk, False)

    @pl.loop(free, end)
    def _(chunk):
        step(chunk, True)

    for pair in range(PAIRS):
        back = turning[pair].T * (1.0 / math.sqrt(HEAD_WIDTH))
        dq_ref[0, :, 128 * pair : 128 * pair + 128] = turn(back, cos_ref[...], -sin_ref[...]).astype(LOW)


def attention_specs(sequences, rows, row_length):
    q_spec = pl.BlockSpec((1, rows, GROUP_WIDTH), lambda s, g, w, t: (s, 0, g))
    k_spec = pl.BlockSpec((1, row_length, 128), lambda s, g, w, t: (s, 0, g // 2))
    v_spec = pl.BlockSpec((1, row_length, 128), lambda s, g, w, t: (s, 0, 2 + g // 2))
    table_spec = pl.BlockSpec((rows, 128), lambda s, g, w, t: (0, 0))
    log_spec = pl.BlockSpec((1, 2 * PAIRS, rows), lambda s, g, w, t: (s, g, 0))
    return q_spec, k_spec, v_spec, table_spec, log_spec


def attend_forward(places, spots, cosine, sine, query_proj, kv_all):
    sequences, rows, _ = query_proj.shape
    row_length = kv_all.shape[1]
    q_spec, k_spec, v_spec, table_spec, log_spec = attention_specs(sequences, rows, row_length)
    pairs = sequences * QUERY_HEADS * rows * row_length
    return pl.pallas_call(
        attend_forward_kernel,
        grid_spec=pltpu.PrefetchScalarGridSpec(
            num_scalar_prefetch=2,
            grid=(sequences, KEY_VALUE_HEADS),
            in_specs=[table_spec, table_spec, q_spec, k_spec, v_spec],
            out_specs=[q_spec, log_spec],
            scratch_shapes=[
                pltpu.VMEM((rows, GROUP_WIDTH), LOW),
                pltpu.VMEM((2 * PAIRS, rows), FULL),
                pltpu.VMEM((2 * PAIRS, rows), FULL),
                pltpu.VMEM((PAIRS, 128, rows), FULL),
            ],
        ),
        out_shape=[
            jax.ShapeDtypeStruct(query_proj.shape, LOW),
            jax.ShapeDtypeStruct((sequences, QUERY_HEADS, rows), FULL),
        ],
        compiler_params=pltpu.CompilerParams(vmem_limit_bytes=40 * 1024 * 1024),
        cost_estimate=pl.CostEstimate(
            flops=4 * HEAD_WIDTH * pairs, bytes_accessed=8 * 1024 * 1024, transcendentals=pairs
        ),
        name="attend_forward",
    )(places, spots, cosine, sine, query_proj, kv_all, kv_all)


def attend_backward(places, spots, cosine, sine, query_proj, kv_all, attended, grad_attended, logs):
    sequences, rows, _ = query_proj.shape
    row_length = kv_all.shape[1]
    q_spec, k_spec, v_spec, table_spec, log_spec = attention_specs(sequences, rows, row_length)
    pairs = sequences * QUERY_HEADS * rows * row_length
    return pl.pallas_call(
        attend_backward_kernel,
        grid_spec=pltpu.PrefetchScalarGridSpec(
            num_scalar_prefetch=2,
            grid=(sequences, KEY_VALUE_HEADS),
            in_specs=[table_spec, table_spec, q_spec, k_spec, v_spec, q_spec, q_spec, log_spec],
            out_specs=[
                q_spec,
                pl.BlockSpec((1, row_length, 2 * KEY_VALUE_WIDTH), lambda s, g, w, t: (s, 0, 0)),
            ],
            scratch_shapes=[
                pltpu.VMEM((rows, GROUP_WIDTH), LOW),
                pltpu.VMEM((2 * PAIRS, rows), FULL),
                pltpu.VMEM((PAIRS, 128, rows), FULL),
                pltpu.VMEM((2 * KEY_CHUNK, 128), FULL),
                pltpu.VMEM((2 * KEY_CHUNK, 128), FULL),
            ],
        ),
        out_shape=[
            jax.ShapeDtypeStruct(query_proj.shape, LOW),
            jax.ShapeDtypeStruct((sequences, row_length, 2 * KEY_VALUE_WIDTH), LOW),
        ],
        compiler_params=pltpu.CompilerParams(vmem_limit_bytes=40 * 1024 * 1024),
        cost_estimate=pl.CostEstimate(
            flops=10 * HEAD_WIDTH * pairs, bytes_accessed=12 * 1024 * 1024, transcendentals=pairs
        ),
        name="attend_backward",
    )(places, spots, cosine, sine, query_proj, kv_all, kv_all, attended, grad_attended, logs)


def swap_dp(value, distance):
    size = lax.axis_size("dp")
    return lax.ppermute(value, "dp", [(a, a ^ distance) for a in range(size)])


def part_members():
    size = lax.axis_size("dp")
    rank = lax.axis_index("dp")
    return [rank ^ d if size == 4 else jnp.int32(d) for d in range(size)]


def near_far(value):
    return [swap_dp(value, 1), swap_dp(value, 2)]


def cross_of(near, far):
    half = near.shape[0] // 2
    return [swap_dp(far[:half], 1), swap_dp(near[half:], 2)]


def gather_parts(value):
    size = lax.axis_size("dp")
    if size != 4:
        whole = lax.all_gather(value, "dp", axis=0)
        return [whole[d] for d in range(size)]
    beside = near_far(value)
    return [value, *beside, jnp.concatenate(cross_of(*beside), axis=0)]


def gather_dp(value):
    return jnp.concatenate(gather_parts(value), axis=0)


def gather_direct(value):
    size = lax.axis_size("dp")
    if size != 4:
        return gather_parts(value)
    near, far = swap_dp(value, 1), swap_dp(value, 2)
    return [value, near, far, swap_dp(value, 3)]


def send_parts(parts):
    size = lax.axis_size("dp")
    if size != 4:
        stack = jnp.concatenate([part.astype(LOW) for part in parts], axis=0)
        total = lax.psum_scatter(stack, "dp", scatter_dimension=0, tiled=True)
        return [jnp.zeros_like(total), total]
    return [parts[0]] + [swap_dp(parts[distance], distance) for distance in range(1, size)]


def add_up(own, received):
    total = own.astype(FULL)
    for part in received:
        total = total + part.astype(FULL)
    return total


def exchange_parts(parts):
    size = lax.axis_size("dp")
    if size != 4:
        whole = lax.all_to_all(jnp.stack(parts), "dp", 0, 0)
        return [whole[d] for d in range(size)]
    return [parts[0]] + [swap_dp(parts[d], d) for d in range(1, size)]


def split_parts(value):
    size = lax.axis_size("dp")
    rows = value.shape[0] // size
    return [value[d * rows : (d + 1) * rows] for d in range(size)]


def scatter_dp(value):
    size = lax.axis_size("dp")
    if size != 4:
        return lax.psum_scatter(
            value.astype(LOW), "dp", scatter_dimension=0, tiled=True
        ).astype(FULL)
    own, near, far, cross = split_parts(value)
    half = own.shape[0] // 2
    near, far, cross = near.astype(LOW), far.astype(LOW), cross.astype(LOW)
    by_near = swap_dp(cross[:half], 1)
    by_far = swap_dp(cross[half:], 2)
    near_first = swap_dp(near[:half], 1)
    far_second = swap_dp(far[half:], 2)
    far_first = swap_dp((far[:half].astype(FULL) + by_near.astype(FULL)).astype(LOW), 2)
    near_second = swap_dp((near[half:].astype(FULL) + by_far.astype(FULL)).astype(LOW), 1)
    return own + jnp.concatenate(
        [
            near_first.astype(FULL) + far_first.astype(FULL),
            near_second.astype(FULL) + far_second.astype(FULL),
        ]
    )


def split_rows(value, rows):
    return value[:rows], value[rows:]


def line_up(parts, width):
    rows = parts[0].shape[0]
    whole = jnp.zeros((rows, len(parts) * width), parts[0].dtype)
    for part, who in zip(parts, part_members()):
        whole = lax.dynamic_update_slice_in_dim(whole, part, who * width, 1)
    return whole


def cut_up(value, width):
    return [lax.dynamic_slice_in_dim(value, who * width, width, 1) for who in part_members()]


def is_line():
    return lax.axis_size("grp") == 8


def chip_shift(value, steps):
    pairs = []
    for chip in range(4):
        if 0 <= chip + steps < 4:
            pairs += [(2 * chip + core, 2 * (chip + steps) + core) for core in range(2)]
    return lax.ppermute(value, "grp", pairs)


def core_swap(value):
    return lax.ppermute(value, "grp", [(a, a ^ 1) for a in range(8)])


def gather_earlier(value):
    sequences, rows, width = value.shape
    member = lax.axis_index("grp")
    chunks = ROW_LENGTH // KEY_CHUNK
    if not is_line() or rows != KEY_CHUNK:
        whole = lax.all_gather(value, "grp", axis=1, tiled=True)
        return whole, jnp.arange(chunks, dtype=jnp.int32)
    pieces = [value] + [chip_shift(value, steps) for steps in range(1, 4)]
    pieces += [core_swap(piece) for piece in pieces]
    order = jnp.arange(chunks, dtype=jnp.int32)
    other_core = (order % 2 != member % 2).astype(jnp.int32)
    spots = 4 * other_core + jnp.maximum(member // 2 - order // 2, 0)
    return jnp.concatenate(pieces, axis=1), spots


def scatter_earlier(terms):
    sequences, row_length, width = terms.shape
    if not is_line() or ROW_LENGTH // 8 != KEY_CHUNK:
        total = lax.psum_scatter(terms, "grp", scatter_dimension=1, tiled=True)
        return [total], [total]
    kept, given = terms[:, : row_length // 2], terms[:, row_length // 2 :]
    chip_sums = kept.astype(FULL) + core_swap(given).astype(FULL)
    sent = [chip_sums[:, k * KEY_CHUNK : (k + 1) * KEY_CHUNK].astype(LOW) for k in range(1, 4)]
    own = chip_sums[:, :KEY_CHUNK]
    return [own] + [chip_shift(part, -k) for k, part in enumerate(sent, 1)], sent


def finish_earlier(sums, *meanwhile):
    *sums, _ = lax.optimization_barrier((*sums, meanwhile))
    return add_up(sums[0], sums[1:])


def line_terms(sums, step, upward, downward):
    chip = lax.axis_index("grp") // 2
    up, down = of_chip(sums, chip + 4 - step), of_chip(sums, chip - 4 + step)
    if step > 1:
        up = (up.astype(FULL) + upward.astype(FULL)).astype(LOW)
        down = (down.astype(FULL) + downward.astype(FULL)).astype(LOW)
    return up, down


def line_step(up, down, step):
    up_pairs = [(2 * c + k, 2 * c + 2 + k) for c in range(step) for k in range(2)]
    down_pairs = [(2 * c + k, 2 * c - 2 + k) for c in range(4 - step, 4) for k in range(2)]
    return lax.ppermute(up, "grp", up_pairs), lax.ppermute(down, "grp", down_pairs)


def of_chip(sums, index):
    return lax.dynamic_index_in_dim(sums, jnp.clip(index, 0, 3), 0, keepdims=False)


ANY_SPEC = pl.BlockSpec(memory_space=pltpu.HBM)
READ_GROUPS = 8


def move(source, target, sem, start):
    copy = pltpu.make_async_copy(source, target, sem)
    if start:
        copy.start()
    else:
        copy.wait()


def block_call(kernel, name, table, inputs, outputs, count, piece, aliases=None, spare=4):
    hold = pltpu.VMEM((count, piece, D), LOW)
    return pl.pallas_call(
        kernel,
        grid_spec=pltpu.PrefetchScalarGridSpec(
            num_scalar_prefetch=1,
            grid=(1,),
            in_specs=[ANY_SPEC] * len(inputs),
            out_specs=[ANY_SPEC] * len(outputs),
            scratch_shapes=[hold, pltpu.SemaphoreType.DMA((READ_GROUPS,)), pltpu.SemaphoreType.DMA],
        ),
        out_shape=outputs,
        input_output_aliases=aliases or {},
        compiler_params=pltpu.CompilerParams(
            vmem_limit_bytes=2 * count * piece * D + spare * 1024 * 1024
        ),
        cost_estimate=pl.CostEstimate(
            flops=0, bytes_accessed=4 * count * piece * D, transcendentals=0
        ),
        name=name,
    )(table, *inputs)


def pick_kernel(at_ref, early_ref, late_ref, *refs):
    outs, hold, read_sems, write_sem = refs[:2], refs[2], refs[3], refs[4]
    count = 3 * FF_BLOCKS
    half = FF_BLOCKS // 2
    early_slots, late_slots = at_ref[2 * count], at_ref[2 * count + 1]
    stages = [(0, 0, low) for low in range(0, 2 * FF_BLOCKS, half)]
    stages += [(1, 2 * FF_BLOCKS, low) for low in (0, half)]
    for group, (_, first, low) in enumerate(stages):

        @pl.loop(first + low, first + low + half)
        def _(block):
            owner, slot = at_ref[block], at_ref[count + block]

            @pl.when(slot < early_slots)
            def _():
                source = early_ref.at[owner * early_slots + slot]
                move(source, hold.at[block], read_sems.at[group], True)

            @pl.when(slot >= early_slots)
            def _():
                source = late_ref.at[owner * late_slots + slot - early_slots]
                move(source, hold.at[block], read_sems.at[group], True)

    for start in (True, False):
        for group, (index, first, low) in enumerate(stages):
            some = hold.at[pl.ds(first + low, half)]
            if start:
                move(some, some, read_sems.at[group], False)
            move(some, outs[index].at[pl.ds(low, half)], write_sem, start)


def pick_blocks(owners, slots, early, late, early_slots, late_slots):
    table = jnp.concatenate([owners, slots, jnp.array([early_slots, late_slots], jnp.int32)])
    piece = early.shape[1]
    outs = [jax.ShapeDtypeStruct((count * FF_BLOCKS, piece, D), LOW) for count in (2, 1)]
    return block_call(
        pick_kernel, "pick_blocks", table, (early, late), outs, 3 * FF_BLOCKS, piece, spare=16
    )


def pick_early_kernel(
    team, at_ref, early_ref, query_ref, kv_ref, out_ref, hold, read_sems, write_sem
):
    early_slots = at_ref[2 * GATE_AT]
    share = D // team
    stages = (
        (0, KEY_AT, query_ref, True),
        (KEY_AT, OUT_AT, kv_ref, False),
        (OUT_AT, GATE_AT, out_ref, True),
    )
    for group, (low, high, _, _) in enumerate(stages):

        @pl.loop(low, high)
        def _(block):
            source = early_ref.at[at_ref[block] * early_slots + at_ref[GATE_AT + block]]
            move(source, hold.at[block], read_sems.at[group], True)

    for start in (True, False):
        for group, (low, high, target, by_columns) in enumerate(stages):
            some = pl.ds(low, high - low)
            if start:
                move(hold.at[some], hold.at[some], read_sems.at[group], False)
            if by_columns:
                for band in range(team):
                    lanes = pl.ds(band * share, share)
                    move(hold.at[some, :, lanes], target.at[:, band], write_sem, start)
            else:
                move(hold.at[some], target, write_sem, start)


def pick_early(owners, slots, early, early_slots, team):
    piece = early.shape[1]
    columns = jax.ShapeDtypeStruct((MODEL_BLOCKS, team, piece, D // team), LOW)
    rows = jax.ShapeDtypeStruct((2 * KV_BLOCKS, piece, D), LOW)
    return block_call(
        functools.partial(pick_early_kernel, team),
        "pick_early",
        jnp.concatenate([owners, slots, jnp.array([early_slots], jnp.int32)]),
        (early,),
        [columns, rows, columns],
        GATE_AT,
        piece,
    )


def assemble_kernel(order_ref, *refs):
    count = len(refs) - 4
    parts, whole, hold, read_sems, write_sem = refs[:count], refs[-4], refs[-3], refs[-2], refs[-1]
    rows, width = parts[0].shape
    band = rows // 4
    for start in (True, False):
        for group in range(4):
            some = pl.ds(group * band, band)
            for index, part in enumerate(parts):
                lanes = pl.ds(pl.multiple_of(order_ref[index] * width, width), width)
                move(part.at[some], hold.at[some, lanes], read_sems.at[group], start)
            if not start:
                move(hold.at[some], whole.at[some], write_sem, True)
    move(hold, whole, write_sem, False)


def assemble_columns(parts):
    rows, width = parts[0].shape
    wide = width * len(parts)
    return pl.pallas_call(
        assemble_kernel,
        grid_spec=pltpu.PrefetchScalarGridSpec(
            num_scalar_prefetch=1,
            grid=(1,),
            in_specs=[ANY_SPEC] * len(parts),
            out_specs=ANY_SPEC,
            scratch_shapes=[
                pltpu.VMEM((rows, wide), LOW),
                pltpu.SemaphoreType.DMA((4,)),
                pltpu.SemaphoreType.DMA,
            ],
        ),
        out_shape=jax.ShapeDtypeStruct((rows, wide), LOW),
        compiler_params=pltpu.CompilerParams(vmem_limit_bytes=2 * rows * wide + 4 * 1024 * 1024),
        cost_estimate=pl.CostEstimate(
            flops=0, bytes_accessed=4 * rows * wide, transcendentals=0
        ),
        name="assemble_columns",
    )(jnp.stack(part_members()), *parts)


def in_cut(targets, core, outs, owner, slot, act):
    for (low, high, side), out_ref in zip(targets, outs):
        here = (slot >= low) & (slot < high)
        row = owner
        if side is not None:
            here = here & ((owner % 2 == core) if side == 0 else (owner % 2 != core))
            row = owner // 2

        @pl.when(here)
        def _():
            act(out_ref.at[row * (high - low) + slot - low])


def target_shape(target, piece):
    low, high, side = target
    owners = lax.axis_size("grp") // (1 if side is None else 2)
    return jax.ShapeDtypeStruct((owners * (high - low), piece, D), LOW)


def place_ff_kernel(targets, at_ref, *refs):
    terms, outs = refs[:2], refs[2:-3]
    hold, read_sems, write_sem = refs[-3:]
    count = 3 * FF_BLOCKS
    half = FF_BLOCKS // 2
    stages = [(0, 0, low) for low in range(0, 2 * FF_BLOCKS, half)]
    stages += [(1, 2 * FF_BLOCKS, low) for low in (0, half)]
    for start in (True, False):
        for group, (index, first, low) in enumerate(stages):
            target = hold.at[pl.ds(first + low, half)]
            move(terms[index].at[pl.ds(low, half)], target, read_sems.at[group], start)
            if start:
                continue

            @pl.loop(first + low, first + low + half)
            def _(block):
                in_cut(
                    targets,
                    at_ref[2 * count],
                    outs,
                    at_ref[block],
                    at_ref[count + block],
                    lambda target: move(hold.at[block], target, write_sem, True),
                )

    move(hold, hold, write_sem, False)


def place_ff(owners, slots, terms, targets):
    piece = terms[0].shape[1]
    return block_call(
        functools.partial(place_ff_kernel, targets),
        "place_ff",
        jnp.concatenate([owners, slots, lax.axis_index("grp")[None] % 2]),
        terms,
        [target_shape(target, piece) for target in targets],
        3 * FF_BLOCKS,
        piece,
    )


def place_more_kernel(team, targets, kinds, at_ref, *refs):
    sources, outs = refs[: len(kinds)], refs[-3 - len(targets) : -3]
    hold, read_sems, write_sem = refs[-3:]
    share = D // team
    total = sum(count for count, _ in kinds)

    def write(block, start):
        in_cut(
            targets,
            at_ref[2 * total],
            outs,
            at_ref[block],
            at_ref[total + block],
            lambda target: move(hold.at[block], target, write_sem, start),
        )

    for start in (True, False):
        low = 0
        for group, ((count, by_columns), source) in enumerate(zip(kinds, sources)):
            some = pl.ds(low, count)
            if by_columns:
                for band in range(team):
                    lanes = pl.ds(band * share, share)
                    move(source.at[:, band], hold.at[some, :, lanes], read_sems.at[group], start)
            else:
                move(source, hold.at[some], read_sems.at[group], start)
            if not start:

                @pl.loop(low, low + count)
                def _(block):
                    write(block, True)

            low += count

    @pl.loop(0, total)
    def _(block):
        write(block, False)


def place_more(name, owners, slots, terms, kinds, placed, targets, team):
    piece = placed[0].shape[1]
    return block_call(
        functools.partial(place_more_kernel, team, targets, kinds),
        name,
        jnp.concatenate([owners, slots, lax.axis_index("grp")[None] % 2]),
        (*terms, *placed),
        [jax.ShapeDtypeStruct(part.shape, LOW) for part in placed],
        sum(count for count, _ in kinds),
        piece,
        {1 + len(terms) + index: index for index in range(len(placed))},
    )


def adamw_by_products(master, first, second, gradient):
    first_new = BETA_ONE * first + (1.0 - BETA_ONE) * gradient
    second_new = BETA_TWO * second + (1.0 - BETA_TWO) * (gradient * gradient)
    root = jnp.sqrt(second_new * (1.0 / (1.0 - BETA_TWO**STEP))) + ADAM_EPS
    stepped = (first_new * (WEIGHT_RATE / (1.0 - BETA_ONE**STEP))) / root
    return ((1.0 - WEIGHT_RATE * WEIGHT_DECAY) * master - stepped, first_new, second_new)


STRIPS = 1


def adamw_kernel(team, first_slot, at_ref, master, first, second, *refs):
    parts = refs[:team]
    new_master, new_first, new_second, copy, shares = refs[-5:]
    kind = at_ref[team + first_slot + pl.program_id(0)]
    strip = pl.program_id(1)
    piece, share = R // team, D // team

    @pl.when(strip == 0)
    def _():
        for index in range(team):
            shares[at_ref[index]] = parts[index][0]

    def update(rows, lanes, gradient):
        results = adamw_by_products(
            master[0, rows, lanes], first[0, rows, lanes], second[0, rows, lanes], gradient
        )
        for target, value in zip((new_master, new_first, new_second), results):
            target[0, rows, lanes] = value
        copy[0, rows, lanes] = results[0].astype(LOW)

    bands = team // STRIPS
    for turn_of in range(STRIPS):
        for band in range(bands):
            rows = slice(band * piece, (band + 1) * piece)
            source = turn_of * bands + band
            here = strip == turn_of

            @pl.when(here & (kind == 1))
            def _():
                update(rows, slice(0, D), shares[source].astype(FULL))

            @pl.when(here & (kind == 2))
            def _():
                for index in range(team):
                    lanes = slice(index * share, (index + 1) * share)
                    gradient = shares[index, :, source * share : (source + 1) * share]
                    update(rows, lanes, gradient.astype(FULL))

            @pl.when(here & (kind == 0))
            def _():
                update(rows, slice(0, D), jnp.zeros((piece, D), FULL))


def adamw_slots(kinds, master, first, second, parts, first_slot, so_far):
    team = len(parts)
    count = parts[0].shape[0]
    slot_spec = pl.BlockSpec((1, R // STRIPS, D), lambda i, j, a: (first_slot + i, j, 0))
    part_spec = pl.BlockSpec((1, R // team, D), lambda i, j, a: (i, 0, 0))
    whole = jax.ShapeDtypeStruct(master.shape, FULL)
    extra = [] if so_far is None else list(so_far)
    return pl.pallas_call(
        functools.partial(adamw_kernel, team, first_slot),
        grid_spec=pltpu.PrefetchScalarGridSpec(
            num_scalar_prefetch=1,
            grid=(count, STRIPS),
            in_specs=[slot_spec] * 3 + [part_spec] * team + [ANY_SPEC] * len(extra),
            out_specs=[slot_spec] * 4,
            scratch_shapes=[pltpu.VMEM((team, R // team, D), LOW)],
        ),
        out_shape=[whole, whole, whole, jax.ShapeDtypeStruct(master.shape, LOW)],
        input_output_aliases={4 + team + k: k for k in range(len(extra))},
        compiler_params=pltpu.CompilerParams(vmem_limit_bytes=52 * 1024 * 1024),
        cost_estimate=pl.CostEstimate(
            flops=20 * count * R * D, bytes_accessed=28 * count * R * D, transcendentals=0
        ),
        name="adamw_slots",
    )(jnp.concatenate([jnp.stack(part_members()), kinds]), master, first, second, *parts, *extra)


def after(value, *others):
    return lax.optimization_barrier((value,) + others)[0]


def per_device(
    layer_input,
    out_cotangent,
    seq_lengths,
    block_owner,
    weight_master,
    weight_first,
    weight_second,
    gain_master,
    gain_first,
    gain_second,
):
    slot_count = weight_master.shape[0]
    team = lax.axis_size("dp")
    rank = lax.axis_index("dp")
    member = lax.axis_index("grp")
    piece = R // team
    sequence_count = layer_input.shape[0]
    segment_rows = layer_input.shape[1]
    token_count = sequence_count * segment_rows
    model_share = D // team
    kv_share = KEY_VALUE_WIDTH // team
    ff_share = FF // team
    early_slots = slot_count * 5 // 12
    late_slots = slot_count - early_slots
    sides = (0, 1) if is_line() and team == 4 else (None,)
    targets = tuple((0, early_slots, side) for side in sides) + ((early_slots, slot_count, None),)

    block_order = jnp.arange(BLOCKS, dtype=jnp.int32)
    same_owner = block_owner[:, None] == block_owner[None, :]
    earlier = block_order[None, :] < block_order[:, None]
    slots = jnp.sum((same_owner & earlier).astype(jnp.int32), axis=1)
    whole_columns = (block_order < KEY_AT) | ((block_order >= OUT_AT) & (block_order < GATE_AT))
    block_kind = jnp.where(whole_columns, 2, 1)
    mine = (block_owner == member)[None, :] & (
        slots[None, :] == jnp.arange(slot_count, dtype=jnp.int32)[:, None]
    )
    kinds = jnp.sum(jnp.where(mine, block_kind[None, :], 0), axis=1)
    my_attention = jnp.any(mine & (block_order < GATE_AT)[None, :], axis=1)
    spills = jnp.any(slots[:GATE_AT] >= early_slots)

    def shares_of(low, high):
        count = high - low
        by_rows = lax.dynamic_slice(weight_master, (low, rank * piece, 0), (count, piece, D))
        by_columns = lax.dynamic_slice(
            weight_master, (low, 0, rank * model_share), (count, R, model_share)
        ).astype(LOW)
        by_columns = jnp.concatenate(
            [by_columns[:, j * piece : (j + 1) * piece] for j in range(team)], axis=-1
        )
        return jnp.where((kinds[low:high] == 2)[:, None, None], by_columns, by_rows.astype(LOW))

    shares_early = shares_of(0, early_slots)
    shares_late = shares_of(early_slots, slot_count)
    gathered_early = lax.all_gather(shares_early, "grp", axis=0, tiled=True)
    gathered_late = lax.all_gather(shares_late, "grp", axis=0, tiled=True)
    gains_all = lax.all_gather(gain_master.astype(LOW), "grp", axis=1, tiled=True)

    positions = member * segment_rows + jnp.arange(segment_rows, dtype=jnp.int32)
    valid_rows = (positions[None, :] < seq_lengths[:, None]).reshape(token_count, 1)
    cosine_rows, sine_rows = rotary_tables(positions, HEAD_WIDTH)
    wide_cosine = jnp.concatenate([cosine_rows] * 4, axis=1)
    wide_sine = jnp.concatenate([-sine_rows, sine_rows] * 2, axis=1)
    places = jnp.concatenate(
        [jnp.stack([member * segment_rows, jnp.int32(segment_rows)]), seq_lengths]
    ).astype(jnp.int32)
    inputs = layer_input.reshape(token_count, D).astype(FULL)
    root_one = lax.rsqrt(jnp.mean(inputs * inputs, axis=-1, keepdims=True) + NORM_EPS)
    normed_one = inputs * root_one
    gain_one = gains_all[0].astype(FULL)
    gain_two = gains_all[1].astype(FULL)
    hidden_one = (normed_one * gain_one).astype(LOW)
    hidden_one_all = gather_dp(hidden_one)
    grad_out = jnp.where(valid_rows, out_cotangent.reshape(token_count, D), jnp.zeros((), LOW))
    grad_out_all = gather_dp(after(grad_out, hidden_one_all))
    gathered_early = after(gathered_early, hidden_one_all, grad_out_all)

    def attention_early():
        return tuple(
            pick_early(block_owner[:GATE_AT], slots[:GATE_AT], gathered_early, early_slots, team)
        )

    def attention_spilled():
        everything = lax.all_gather(
            jnp.concatenate([shares_early, shares_late]), "grp", axis=0, tiled=True
        )
        found = jnp.take(
            everything, (block_owner * slot_count + slots)[:GATE_AT], axis=0, mode="clip"
        )

        def columns(first):
            chosen = found[first : first + MODEL_BLOCKS]
            return chosen.reshape(MODEL_BLOCKS, piece, team, model_share).transpose(0, 2, 1, 3)

        return columns(0), found[KEY_AT:OUT_AT], columns(OUT_AT)

    query_share, kv_rows, out_share = lax.cond(spills, attention_spilled, attention_early)
    query_share = query_share.reshape(D, model_share)
    kv_rows = kv_rows.reshape(2 * kv_share, D)
    out_share = out_share.reshape(D, model_share)


    kv_shares = contract_rows(hidden_one_all, kv_rows).astype(LOW)
    kv_parts = exchange_parts(split_parts(kv_shares))
    query_shares = plain_dot(after(hidden_one_all, kv_shares), query_share).astype(LOW)
    query_parts = exchange_parts(split_parts(query_shares))
    kv_proj = (
        line_up(kv_parts, 2 * kv_share)
        .reshape(token_count, team, 2 * KV_BLOCKS, piece)
        .transpose(0, 2, 1, 3)
        .reshape(token_count, 2 * KEY_VALUE_WIDTH)
    )
    keys_local = apply_rotation(
        kv_proj[:, :KEY_VALUE_WIDTH]
        .astype(FULL)
        .reshape(sequence_count, segment_rows, KEY_VALUE_HEADS, HEAD_WIDTH),
        cosine_rows,
        sine_rows,
    ).astype(LOW)
    kv_local = jnp.concatenate(
        [
            keys_local.reshape(sequence_count, segment_rows, KEY_VALUE_WIDTH),
            kv_proj[:, KEY_VALUE_WIDTH:].reshape(sequence_count, segment_rows, KEY_VALUE_WIDTH),
        ],
        axis=-1,
    )
    kv_all, spots = gather_earlier(kv_local)
    query_proj = line_up(query_parts, model_share).reshape(sequence_count, segment_rows, D)
    w_out = assemble_columns(gather_parts(after(out_share, query_proj, kv_local)))

    attended, logs = attend_forward(places, spots, wide_cosine, wide_sine, query_proj, kv_all)
    attended_flat = attended.reshape(token_count, D)
    residual = inputs + plain_dot(attended_flat, w_out)
    root_two = lax.rsqrt(jnp.mean(residual * residual, axis=-1, keepdims=True) + NORM_EPS)
    normed_two = residual * root_two
    hidden_two = (normed_two * gain_two).astype(LOW)

    hidden_two_parts = gather_direct(hidden_two)
    ff_blocks = pick_blocks(
        block_owner[GATE_AT:],
        slots[GATE_AT:],
        gathered_early,
        after(gathered_late, hidden_two),
        early_slots,
        late_slots,
    )
    w_both, w_down = ff_blocks[0].reshape(2 * ff_share, D), ff_blocks[1].reshape(ff_share, D)
    grad_out_parts = split_parts(grad_out_all)
    inner = jnp.zeros((team * token_count, ff_share), LOW)
    grad_both = jnp.zeros((team * token_count, 2 * ff_share), LOW)
    inner_parts, grad_htwo_parts = [], []
    for index, (hidden, given) in enumerate(zip(hidden_two_parts, grad_out_parts)):
        if index > 0:
            hidden = after(hidden, grad_htwo_parts[-1])
        both = contract_rows(hidden, w_both)
        gate_pre, up_pre = both[:, :ff_share], both[:, ff_share:]
        sigmoid_gate = jax.nn.sigmoid(gate_pre)
        activated = gate_pre * sigmoid_gate
        inner_parts.append((activated * up_pre).astype(LOW))
        grad_inner = contract_rows(given, w_down)
        grad_gate = grad_inner * up_pre * (sigmoid_gate * (1.0 + gate_pre * (1.0 - sigmoid_gate)))
        grad_up = grad_inner * activated
        grad_part = jnp.concatenate([grad_gate.astype(LOW), grad_up.astype(LOW)], axis=1)
        part = plain_dot(grad_part, w_both)
        grad_htwo_parts.append(part if index == 0 else part.astype(LOW))
        first = index * token_count
        inner = lax.dynamic_update_slice(inner, inner_parts[-1], (first, 0))
        grad_both = lax.dynamic_update_slice(grad_both, grad_part, (first, 0))
    grad_htwo_sent = send_parts(grad_htwo_parts)
    grad_htwo = add_up(grad_htwo_sent[0], grad_htwo_sent[1:])
    hidden_two_all = jnp.concatenate(hidden_two_parts, axis=0)
    grad_both = after(grad_both, grad_htwo_sent[1])
    both_terms = contract_first(grad_both, hidden_two_all).astype(LOW)
    inner = after(inner, both_terms, *grad_htwo_sent[1:])
    ff_terms = [
        both_terms.reshape(-1, piece, D),
        contract_first(inner, grad_out_all).astype(LOW).reshape(-1, piece, D),
    ]
    cut_terms = place_ff(block_owner[GATE_AT:], slots[GATE_AT:], ff_terms, targets)
    late_terms = cut_terms[-1]
    late_sums = lax.psum_scatter(late_terms, "grp", scatter_dimension=0, tiled=True)

    grad_htwo = after(grad_htwo, late_terms)
    scaled_two = grad_htwo * gain_two
    grad_resid = grad_out.astype(FULL) + root_two * (
        scaled_two - normed_two * jnp.mean(scaled_two * normed_two, axis=-1, keepdims=True)
    )
    resid_low = grad_resid.astype(LOW)
    grad_attended = contract_rows(resid_low, w_out).astype(LOW)
    resid_parts = exchange_parts(cut_up(resid_low, model_share))
    attended_here = after(attended_flat, grad_attended)
    attended_parts = near_far(attended_here) if team == 4 else gather_parts(attended_here)
    grad_query, kv_terms = attend_backward(
        places,
        spots,
        wide_cosine,
        wide_sine,
        query_proj,
        kv_all,
        attended,
        grad_attended.reshape(sequence_count, segment_rows, D),
        logs,
    )
    grad_query, kv_terms, resid_parts, attended_parts = lax.optimization_barrier(
        (grad_query, kv_terms, resid_parts, attended_parts)
    )
    query_share_parts = exchange_parts(cut_up(grad_query.reshape(token_count, D), model_share))
    key_value_sums, kv_terms = scatter_earlier(kv_terms)
    query_share_parts = lax.optimization_barrier((query_share_parts, kv_terms))[0]
    grad_query_share = jnp.concatenate(query_share_parts, axis=0)
    if team == 4:
        farthest = swap_dp(after(attended_flat, *kv_terms), 3)
        attended_parts = [attended_flat, *attended_parts, farthest]
    down_parts = [plain_dot(part, after(w_down, kv_terms)) for part in inner_parts]
    down_parts = down_parts[:1] + [part.astype(LOW) for part in down_parts[1:]]
    attended_parts = lax.optimization_barrier((attended_parts, down_parts))[0]
    attended_all = jnp.concatenate(attended_parts, axis=0)
    resid_share = jnp.concatenate(resid_parts, axis=0)
    column_shape = (MODEL_BLOCKS, team, piece, model_share)
    out_terms = contract_first(attended_all, resid_share).astype(LOW).reshape(column_shape)
    early_terms = place_more(
        "place_out",
        block_owner[OUT_AT:GATE_AT],
        slots[OUT_AT:GATE_AT],
        (out_terms,),
        ((MODEL_BLOCKS, True),),
        cut_terms[:-1],
        targets[:-1],
        team,
    )
    query_terms = contract_first(hidden_one_all, grad_query_share).astype(LOW)
    down_sent = send_parts(down_parts)
    key_value_sums = finish_earlier(key_value_sums, early_terms, query_terms)
    grad_keys = apply_rotation(
        key_value_sums[:, :, :KEY_VALUE_WIDTH].reshape(
            sequence_count, segment_rows, KEY_VALUE_HEADS, HEAD_WIDTH
        ),
        cosine_rows,
        -sine_rows,
    ).reshape(token_count, KEY_VALUE_WIDTH)
    grad_values = key_value_sums[:, :, KEY_VALUE_WIDTH:].reshape(token_count, KEY_VALUE_WIDTH)
    grad_kv = (
        jnp.concatenate([grad_keys, grad_values], axis=1)
        .astype(LOW)
        .reshape(token_count, 2 * KV_BLOCKS, team, piece)
        .transpose(0, 2, 1, 3)
        .reshape(token_count, 2 * KEY_VALUE_WIDTH)
    )
    grad_kv_share = jnp.concatenate(exchange_parts(cut_up(grad_kv, 2 * kv_share)), axis=0)

    kv_weight_terms = contract_first(grad_kv_share, hidden_one_all).astype(LOW)
    attention_terms = [
        query_terms.reshape(column_shape),
        kv_weight_terms.reshape(2 * KV_BLOCKS, piece, D),
        out_terms,
    ]
    attention_terms, down_sent = lax.optimization_barrier((attention_terms, down_sent))
    early_terms = place_more(
        "place_query",
        block_owner[:OUT_AT],
        slots[:OUT_AT],
        attention_terms[:2],
        ((MODEL_BLOCKS, True), (2 * KV_BLOCKS, False)),
        early_terms,
        targets[:-1],
        team,
    )

    def nothing_spilled():
        return jnp.zeros((late_slots, piece, D), LOW)

    def sums_spilled():
        by_columns = [
            attention_terms[k].transpose(0, 2, 1, 3).reshape(MODEL_BLOCKS, piece, D) for k in (0, 2)
        ]
        found = jnp.concatenate([by_columns[0], attention_terms[1], by_columns[1]], axis=0)
        every_slot = jnp.arange(slot_count * lax.axis_size("grp"), dtype=jnp.int32)
        hits = (block_owner * slot_count + slots)[None, :GATE_AT] == every_slot[:, None]
        which = jnp.sum(jnp.where(hits, block_order[None, :GATE_AT], 0), axis=1)
        spread = jnp.where(
            jnp.any(hits, axis=1)[:, None, None],
            jnp.take(found, which, axis=0, mode="clip"),
            jnp.zeros((), LOW),
        )
        extra = lax.psum_scatter(spread, "grp", scatter_dimension=0, tiled=True)
        return extra[early_slots:]

    late_extra = lax.cond(
        after(spills, late_sums, early_terms[0]), sums_spilled, nothing_spilled
    )

    spilled = spills & my_attention[early_slots:]
    late_sums = jnp.where(spilled[:, None, None], late_extra, late_sums)
    late_half = late_slots // 2
    states = (weight_master, weight_first, weight_second)

    def query_gradient(share):
        return contract_rows(share, query_share) + plain_dot(grad_kv_share, kv_rows)

    def finish_input(grad_hone):
        scaled_one = grad_hone * gain_one
        spread = jnp.mean(scaled_one * normed_one, axis=-1, keepdims=True)
        input_grad = grad_resid + root_one * (scaled_one - normed_one * spread)
        gain_terms = [
            jnp.sum(grad_hone * normed_one, axis=0), jnp.sum(grad_htwo * normed_two, axis=0)
        ]
        return (
            input_grad.astype(LOW).reshape(sequence_count, segment_rows, D),
            jnp.stack(gain_terms),
        )

    def finish_output(sent):
        output = residual + add_up(sent[0], sent[1:])
        return (
            jnp.where(valid_rows, output, 0.0)
            .astype(LOW)
            .reshape(sequence_count, segment_rows, D)
        )

    def update(parts, low, updated):
        return adamw_slots(kinds, *states, parts, low, updated)

    if is_line() and team == 4:
        tie = lax.optimization_barrier

        def as_slots(rows):
            return rows.reshape(-1, piece, D)

        def join(*pieces):
            return jnp.concatenate([as_slots(rows) for rows in pieces], axis=0)

        kept, given = early_terms
        given, late_sums, grad_query_share = tie((given, late_sums, grad_query_share))
        swapped = core_swap(given)
        first, second = late_sums[:late_half], late_sums[late_half:]
        first_near = near_far(first)
        grad_hone = query_gradient(grad_query_share)
        swapped, grad_hone = tie((swapped, grad_hone))
        sums = (kept.astype(FULL) + swapped.astype(FULL)).astype(LOW)
        sums = sums.reshape(4, early_slots, piece, D)
        up, down = line_terms(sums, 1, None, None)
        upward, downward = line_step(up, down, 1)
        own, near, far, cross = split_parts(grad_hone)
        near, far, cross = near.astype(LOW), far.astype(LOW), cross.astype(LOW)
        rows = token_count // 2
        step = late_half // 2
        first_near, near, far, cross, _, _ = tie((first_near, near, far, cross, up, down))
        by_near = swap_dp(join(first_near[1][:step], near[:rows], cross[:rows]), 1)
        by_far = swap_dp(join(first_near[0][step:], far[rows:], cross[rows:]), 2)
        upward, downward, near, far = tie((upward, downward, near, far))
        up, down = line_terms(sums, 2, upward, downward)
        upward, downward = line_step(up, down, 2)
        by_near, by_far, near, far, _, _ = tie((by_near, by_far, near, far, up, down))
        first_cross = join(by_near[:step], by_far[: late_half - step])
        near_first, by_way_near = split_rows(by_near[step:].reshape(-1, D), rows)
        far_second, by_way_far = split_rows(by_far[late_half - step :].reshape(-1, D), rows)
        far_first = (far[:rows].astype(FULL) + by_way_near.astype(FULL)).astype(LOW)
        near_second = (near[rows:].astype(FULL) + by_way_far.astype(FULL)).astype(LOW)
        by_near = swap_dp(join(second, near_second), 1)
        by_far = swap_dp(join(second, far_first), 2)
        upward, downward, near_second, far_first = tie(
            (upward, downward, near_second, far_first)
        )
        up, down = line_terms(sums, 3, upward, downward)
        upward, downward = line_step(up, down, 3)
        by_near, by_far, _, _ = tie((by_near, by_far, up, down))
        second_near = [by_near[:late_half], by_far[:late_half]]
        second_cross = cross_of(*second_near)
        parts, second_near = tie(([first, *first_near, first_cross], second_near))
        updated = update(parts, early_slots, None)
        upward, downward, updated = tie((upward, downward, updated))
        early_sums = of_chip(sums, member // 2).astype(FULL)
        early_sums = (early_sums + upward.astype(FULL) + downward.astype(FULL)).astype(LOW)
        early_near = near_far(early_sums)
        parts = [second, *second_near, jnp.concatenate(second_cross, axis=0)]
        parts, updated, early_sums = tie((parts, updated, early_sums))
        updated = update(parts, early_slots + late_half, updated)
        near_first, by_far, updated = tie((near_first, by_far, updated))
        grad_hone = own + jnp.concatenate(
            [
                near_first.astype(FULL) + by_far[late_half:].reshape(rows, D).astype(FULL),
                by_near[late_half:].reshape(rows, D).astype(FULL) + far_second.astype(FULL),
            ]
        )
        input_grad, gain_terms = finish_input(grad_hone)
        others = [swap_dp(gain_terms, distance) for distance in range(1, team)]
        early_near, gain_terms = tie((early_near, gain_terms))
        early_cross = cross_of(*early_near)
        down_sent, early_near = tie((down_sent, early_near))
        layer_output = finish_output(down_sent)
        gain_terms, others, layer_output = tie((gain_terms, others, layer_output))
        gain_terms = add_up(gain_terms, others)
        other = core_swap(gain_terms)
        gain_terms, other, early_cross = tie((gain_terms, other, early_cross))
        gain_terms = gain_terms + other
        around = [
            lax.ppermute(gain_terms, "grp", [(a, (a + 2 * turn_by) % 8) for a in range(8)])
            for turn_by in range(1, 4)
        ]
        parts = [early_sums, *early_near, jnp.concatenate(early_cross, axis=0)]
        parts, gain_terms, updated = tie((parts, gain_terms, updated))
        updated = update(parts, 0, updated)
        gain_grad = add_up(gain_terms, around)
    else:
        updated = update(gather_parts(late_sums), early_slots, None)
        early_sums = lax.psum_scatter(early_terms[0], "grp", scatter_dimension=0, tiled=True)
        updated = update(gather_parts(early_sums), 0, updated)
        input_grad, gain_terms = finish_input(scatter_dp(query_gradient(grad_query_share)))
        gain_grad = lax.psum(gain_terms, ("dp", "grp"))
        layer_output = finish_output(down_sent)
    new_master, new_first, new_second, weight_copy = updated

    share_width = gain_master.shape[1]
    gain_share = lax.dynamic_slice_in_dim(gain_grad, member * share_width, share_width, 1)
    new_gain, new_gain_first, new_gain_second = adamw(
        gain_master, gain_first, gain_second, gain_share, GAIN_RATE, 0.0
    )
    return (
        layer_output,
        input_grad,
        new_master,
        new_first,
        new_second,
        weight_copy,
        new_gain,
        new_gain_first,
        new_gain_second,
    )


def solution(mesh):
    return jax.shard_map(
        per_device,
        mesh=mesh,
        in_specs=(
            P("dp", "grp", None),
            P("dp", "grp", None),
            P("dp"),
            P(),
            P("grp", None, None),
            P("grp", None, None),
            P("grp", None, None),
            P(None, "grp"),
            P(None, "grp"),
            P(None, "grp"),
        ),
        out_specs=(
            P("dp", "grp", None),
            P("dp", "grp", None),
            P("grp", None, None),
            P("grp", None, None),
            P("grp", None, None),
            P("grp", None, None),
            P(None, "grp"),
            P(None, "grp"),
            P(None, "grp"),
        ),
        check_vma=False,
    )
```

```python
import functools
import math

import jax
import jax.numpy as jnp
from jax import lax
from jax.experimental import pallas as pl
from jax.experimental.pallas import tpu as pltpu
from jax.sharding import PartitionSpec as P

D = 2048
QUERY_HEADS = 32
KEY_VALUE_HEADS = 4
HEAD_WIDTH = 64
FF = 5632
ROW_LENGTH = 2048
R = 128
STEP = 7
KEY_VALUE_WIDTH = 256
MODEL_BLOCKS = D // R
KV_BLOCKS = KEY_VALUE_WIDTH // R
FF_BLOCKS = FF // R
KEY_AT = MODEL_BLOCKS
OUT_AT = MODEL_BLOCKS + 2 * KV_BLOCKS
GATE_AT = OUT_AT + MODEL_BLOCKS
UP_AT = GATE_AT + FF_BLOCKS
DOWN_AT = UP_AT + FF_BLOCKS
BLOCKS = DOWN_AT + FF_BLOCKS

NORM_EPS = 1e-05
BETA_ONE = 0.9
BETA_TWO = 0.95
ADAM_EPS = 1e-08
WEIGHT_RATE = 0.1
GAIN_RATE = 0.5
WEIGHT_DECAY = 0.1
MASKED = -1e30
LOW = jnp.bfloat16
FULL = jnp.float32


def rotary_tables(positions, head_size):
    halfway = head_size // 2
    spacing = jnp.arange(halfway, dtype=FULL) * (-2.0 * math.log(10000.0) / head_size)
    angles = positions.astype(FULL)[:, None] * jnp.exp(spacing)[None, :]
    return (jnp.cos(angles), jnp.sin(angles))


def apply_rotation(values, cosine_rows, sine_rows):
    halfway = values.shape[-1] // 2
    leading = values[..., :halfway]
    trailing = values[..., halfway:]
    cos_rows = cosine_rows[:, None, :]
    sin_rows = sine_rows[:, None, :]
    return jnp.concatenate(
        [leading * cos_rows - trailing * sin_rows, trailing * cos_rows + leading * sin_rows],
        axis=-1,
    )


def contract_rows(left, right):
    return lax.dot_general(left, right, (((1,), (1,)), ((), ())), preferred_element_type=FULL)


def contract_first(left, right):
    return lax.dot_general(left, right, (((0,), (0,)), ((), ())), preferred_element_type=FULL)


def plain_dot(left, right):
    return jnp.dot(left, right, preferred_element_type=FULL)


def adamw(master, first, second, gradient, rate, decay):
    first_new = BETA_ONE * first + (1.0 - BETA_ONE) * gradient
    second_new = BETA_TWO * second + (1.0 - BETA_TWO) * gradient * gradient
    first_fix = 1.0 - BETA_ONE**STEP
    second_fix = 1.0 - BETA_TWO**STEP
    stepped = first_new / first_fix / (jnp.sqrt(second_new / second_fix) + ADAM_EPS)
    return (master - rate * (stepped + decay * master), first_new, second_new)


KEY_CHUNK = 256
GROUP_WIDTH = D // KEY_VALUE_HEADS
PAIRS = GROUP_WIDTH // 128
EXP_SCALE = math.log2(math.e) / math.sqrt(HEAD_WIDTH)


def lanes_of(shape):
    return lax.broadcasted_iota(jnp.int32, shape, len(shape) - 1)


def swap_halves(values):
    first = (lanes_of(values.shape) % HEAD_WIDTH) < HEAD_WIDTH // 2
    return jnp.where(first, pltpu.roll(values, 96, 1), pltpu.roll(values, 32, 1))


def turn(values, cosine, sine):
    return values * cosine + swap_halves(values) * sine


def chunk_bounds(where_ref):
    start, rows, length = where_ref[0], where_ref[1], where_ref[2 + pl.program_id(0)]
    free = jnp.minimum(start // KEY_CHUNK, length // KEY_CHUNK)
    last = jnp.minimum(start + rows, length)
    return free, (last + KEY_CHUNK - 1) // KEY_CHUNK, start, length


def chunk_rows(spots_ref, chunk):
    return pl.ds(pl.multiple_of(spots_ref[chunk] * KEY_CHUNK, KEY_CHUNK), KEY_CHUNK)


def stacked(block, odd):
    wide = block.astype(FULL)
    wide = jnp.where(odd, pltpu.roll(wide, 64, 1), wide)
    low = jnp.where(lanes_of(wide.shape) < HEAD_WIDTH, wide, 0.0)
    return jnp.concatenate([low, pltpu.roll(low, 64, 1)], axis=0)


def mask_of(chunk, start, length, queries):
    keys = chunk * KEY_CHUNK + lax.broadcasted_iota(jnp.int32, (KEY_CHUNK, queries), 0)
    places = start + lax.broadcasted_iota(jnp.int32, (KEY_CHUNK, queries), 1)
    allowed = (keys <= places) & (keys < length)
    return jnp.concatenate([allowed, allowed], axis=0)


def across(left, right):
    return lax.dot_general(left, right, (((1,), (1,)), ((), ())), preferred_element_type=FULL)


def attend_forward_kernel(
    where_ref, spots_ref, cos_ref, sin_ref, q_ref, k_ref, v_ref, out_ref, log_ref, turned, peaks, sums, totals
):
    queries = q_ref.shape[1]
    odd = (pl.program_id(1) % 2) == 1
    free, end, start, length = chunk_bounds(where_ref)
    for pair in range(PAIRS):
        lanes = slice(128 * pair, 128 * pair + 128)
        turned[:, lanes] = turn(q_ref[0, :, lanes].astype(FULL), cos_ref[...], sin_ref[...]).astype(LOW)
    peaks[...] = jnp.full(peaks.shape, MASKED, FULL)
    sums[...] = jnp.zeros(sums.shape, FULL)
    totals[...] = jnp.zeros(totals.shape, FULL)

    def step(chunk, masked):
        rows = chunk_rows(spots_ref, chunk)
        keys = stacked(k_ref[0, rows, :], odd).astype(LOW)
        values = stacked(v_ref[0, rows, :], odd).T.astype(LOW)
        allowed = mask_of(chunk, start, length, queries) if masked else None
        for pair in range(PAIRS):
            scores = across(keys, turned[:, 128 * pair : 128 * pair + 128]) * EXP_SCALE
            if masked:
                scores = jnp.where(allowed, scores, MASKED)
            weights, fades = [], []
            for side in range(2):
                head = slice(2 * pair + side, 2 * pair + side + 1)
                part = scores[side * KEY_CHUNK : (side + 1) * KEY_CHUNK]
                old = peaks[head, :]
                new = jnp.maximum(old, jnp.max(part, axis=0, keepdims=True))
                weight = jnp.exp2(part - new)
                fade = jnp.exp2(old - new)
                peaks[head, :] = new
                sums[head, :] = sums[head, :] * fade + jnp.sum(weight, axis=0, keepdims=True)
                weights.append(weight.astype(LOW))
                fades.append(jnp.broadcast_to(fade, (HEAD_WIDTH, queries)))
            mixed = jnp.dot(values, jnp.concatenate(weights, axis=0), preferred_element_type=FULL)
            totals[pair] = totals[pair] * jnp.concatenate(fades, axis=0) + mixed

    @pl.loop(0, free)
    def _(chunk):
        step(chunk, False)

    @pl.loop(free, end)
    def _(chunk):
        step(chunk, True)

    for pair in range(PAIRS):
        shares = [
            jnp.broadcast_to(1.0 / sums[2 * pair + side : 2 * pair + side + 1, :], (HEAD_WIDTH, queries))
            for side in range(2)
        ]
        mixed = totals[pair] * jnp.concatenate(shares, axis=0)
        out_ref[0, :, 128 * pair : 128 * pair + 128] = mixed.T.astype(LOW)
    log_ref[0] = peaks[...] + jnp.log2(sums[...])


def attend_backward_kernel(
    where_ref, spots_ref, cos_ref, sin_ref, q_ref, k_ref, v_ref, out_ref, grad_ref, log_ref,
    dq_ref, dkv_ref, turned, dots, turning, key_sums, value_sums,
):
    queries = q_ref.shape[1]
    group = pl.program_id(1)
    odd = (group % 2) == 1
    free, end, start, length = chunk_bounds(where_ref)
    for pair in range(PAIRS):
        lanes = slice(128 * pair, 128 * pair + 128)
        turned[:, lanes] = turn(q_ref[0, :, lanes].astype(FULL), cos_ref[...], sin_ref[...]).astype(LOW)
        products = (out_ref[0, :, lanes].astype(FULL) * grad_ref[0, :, lanes].astype(FULL)).T
        dots[2 * pair : 2 * pair + 1, :] = jnp.sum(products[:HEAD_WIDTH], axis=0, keepdims=True)
        dots[2 * pair + 1 : 2 * pair + 2, :] = jnp.sum(products[HEAD_WIDTH:], axis=0, keepdims=True)
    turning[...] = jnp.zeros(turning.shape, FULL)

    @pl.when(group == 0)
    def _():
        dkv_ref[...] = jnp.zeros(dkv_ref.shape, LOW)

    key_lanes = pl.ds(pl.multiple_of((group // 2) * 128, 128), 128)
    value_lanes = pl.ds(pl.multiple_of(KEY_VALUE_WIDTH + (group // 2) * 128, 128), 128)

    def step(chunk, masked):
        rows = chunk_rows(spots_ref, chunk)
        wide_keys = stacked(k_ref[0, rows, :], odd)
        keys = wide_keys.astype(LOW)
        keys_down = wide_keys.T.astype(LOW)
        values = stacked(v_ref[0, rows, :], odd).astype(LOW)
        allowed = mask_of(chunk, start, length, queries) if masked else None
        for pair in range(PAIRS):
            lanes = slice(128 * pair, 128 * pair + 128)
            asked = turned[:, lanes]
            given = grad_ref[0, :, lanes]
            scores = across(keys, asked) * EXP_SCALE
            if masked:
                scores = jnp.where(allowed, scores, MASKED)
            slopes = across(values, given)
            weights, moves = [], []
            for side in range(2):
                head = slice(2 * pair + side, 2 * pair + side + 1)
                part = slice(side * KEY_CHUNK, (side + 1) * KEY_CHUNK)
                weight = jnp.exp2(scores[part] - log_ref[0, head, :])
                weights.append(weight.astype(LOW))
                moves.append((weight * (slopes[part] - dots[head, :])).astype(LOW))
            weights = jnp.concatenate(weights, axis=0)
            moves = jnp.concatenate(moves, axis=0)
            value_part = jnp.dot(weights, given, preferred_element_type=FULL)
            key_part = jnp.dot(moves, asked, preferred_element_type=FULL)
            if pair == 0:
                value_sums[...] = value_part
                key_sums[...] = key_part
            else:
                value_sums[...] += value_part
                key_sums[...] += key_part
            turning[pair] += jnp.dot(keys_down, moves, preferred_element_type=FULL)
        for sums, lanes, scale in (
            (key_sums, key_lanes, 1.0 / math.sqrt(HEAD_WIDTH)),
            (value_sums, value_lanes, 1.0),
        ):
            both = (sums[:KEY_CHUNK] + pltpu.roll(sums[KEY_CHUNK:], 64, 1)) * scale
            low_side = lanes_of(both.shape) < HEAD_WIDTH
            kept = dkv_ref[0, rows, lanes].astype(FULL)
            mine = jnp.where(odd, pltpu.roll(both, 64, 1), both)
            dkv_ref[0, rows, lanes] = jnp.where(low_side != odd, mine, kept).astype(LOW)

    @pl.loop(0, free)
    def _(chunk):
        step(chunk, False)

    @pl.loop(free, end)
    def _(chunk):
        step(chunk, True)

    for pair in range(PAIRS):
        back = turning[pair].T * (1.0 / math.sqrt(HEAD_WIDTH))
        dq_ref[0, :, 128 * pair : 128 * pair + 128] = turn(back, cos_ref[...], -sin_ref[...]).astype(LOW)


def attention_specs(sequences, rows, row_length):
    q_spec = pl.BlockSpec((1, rows, GROUP_WIDTH), lambda s, g, w, t: (s, 0, g))
    k_spec = pl.BlockSpec((1, row_length, 128), lambda s, g, w, t: (s, 0, g // 2))
    v_spec = pl.BlockSpec((1, row_length, 128), lambda s, g, w, t: (s, 0, 2 + g // 2))
    table_spec = pl.BlockSpec((rows, 128), lambda s, g, w, t: (0, 0))
    log_spec = pl.BlockSpec((1, 2 * PAIRS, rows), lambda s, g, w, t: (s, g, 0))
    return q_spec, k_spec, v_spec, table_spec, log_spec


def attend_forward(places, spots, cosine, sine, query_proj, kv_all):
    sequences, rows, _ = query_proj.shape
    row_length = kv_all.shape[1]
    q_spec, k_spec, v_spec, table_spec, log_spec = attention_specs(sequences, rows, row_length)
    pairs = sequences * QUERY_HEADS * rows * row_length
    return pl.pallas_call(
        attend_forward_kernel,
        grid_spec=pltpu.PrefetchScalarGridSpec(
            num_scalar_prefetch=2,
            grid=(sequences, KEY_VALUE_HEADS),
            in_specs=[table_spec, table_spec, q_spec, k_spec, v_spec],
            out_specs=[q_spec, log_spec],
            scratch_shapes=[
                pltpu.VMEM((rows, GROUP_WIDTH), LOW),
                pltpu.VMEM((2 * PAIRS, rows), FULL),
                pltpu.VMEM((2 * PAIRS, rows), FULL),
                pltpu.VMEM((PAIRS, 128, rows), FULL),
            ],
        ),
        out_shape=[
            jax.ShapeDtypeStruct(query_proj.shape, LOW),
            jax.ShapeDtypeStruct((sequences, QUERY_HEADS, rows), FULL),
        ],
        compiler_params=pltpu.CompilerParams(vmem_limit_bytes=40 * 1024 * 1024),
        cost_estimate=pl.CostEstimate(
            flops=4 * HEAD_WIDTH * pairs, bytes_accessed=8 * 1024 * 1024, transcendentals=pairs
        ),
        name="attend_forward",
    )(places, spots, cosine, sine, query_proj, kv_all, kv_all)


def attend_backward(places, spots, cosine, sine, query_proj, kv_all, attended, grad_attended, logs):
    sequences, rows, _ = query_proj.shape
    row_length = kv_all.shape[1]
    q_spec, k_spec, v_spec, table_spec, log_spec = attention_specs(sequences, rows, row_length)
    pairs = sequences * QUERY_HEADS * rows * row_length
    return pl.pallas_call(
        attend_backward_kernel,
        grid_spec=pltpu.PrefetchScalarGridSpec(
            num_scalar_prefetch=2,
            grid=(sequences, KEY_VALUE_HEADS),
            in_specs=[table_spec, table_spec, q_spec, k_spec, v_spec, q_spec, q_spec, log_spec],
            out_specs=[
                q_spec,
                pl.BlockSpec((1, row_length, 2 * KEY_VALUE_WIDTH), lambda s, g, w, t: (s, 0, 0)),
            ],
            scratch_shapes=[
                pltpu.VMEM((rows, GROUP_WIDTH), LOW),
                pltpu.VMEM((2 * PAIRS, rows), FULL),
                pltpu.VMEM((PAIRS, 128, rows), FULL),
                pltpu.VMEM((2 * KEY_CHUNK, 128), FULL),
                pltpu.VMEM((2 * KEY_CHUNK, 128), FULL),
            ],
        ),
        out_shape=[
            jax.ShapeDtypeStruct(query_proj.shape, LOW),
            jax.ShapeDtypeStruct((sequences, row_length, 2 * KEY_VALUE_WIDTH), LOW),
        ],
        compiler_params=pltpu.CompilerParams(vmem_limit_bytes=40 * 1024 * 1024),
        cost_estimate=pl.CostEstimate(
            flops=10 * HEAD_WIDTH * pairs, bytes_accessed=12 * 1024 * 1024, transcendentals=pairs
        ),
        name="attend_backward",
    )(places, spots, cosine, sine, query_proj, kv_all, kv_all, attended, grad_attended, logs)


def swap_dp(value, distance):
    size = lax.axis_size("dp")
    return lax.ppermute(value, "dp", [(a, a ^ distance) for a in range(size)])


def part_members():
    size = lax.axis_size("dp")
    rank = lax.axis_index("dp")
    return [rank ^ d if size == 4 else jnp.int32(d) for d in range(size)]


def near_far(value):
    return [swap_dp(value, 1), swap_dp(value, 2)]


def cross_of(near, far):
    half = near.shape[0] // 2
    return [swap_dp(far[:half], 1), swap_dp(near[half:], 2)]


def gather_parts(value):
    size = lax.axis_size("dp")
    if size != 4:
        whole = lax.all_gather(value, "dp", axis=0)
        return [whole[d] for d in range(size)]
    beside = near_far(value)
    return [value, *beside, jnp.concatenate(cross_of(*beside), axis=0)]


def gather_dp(value):
    return jnp.concatenate(gather_parts(value), axis=0)


def gather_direct(value):
    size = lax.axis_size("dp")
    if size != 4:
        return gather_parts(value)
    near, far = swap_dp(value, 1), swap_dp(value, 2)
    return [value, near, far, swap_dp(value, 3)]


def send_parts(parts):
    size = lax.axis_size("dp")
    if size != 4:
        stack = jnp.concatenate([part.astype(LOW) for part in parts], axis=0)
        total = lax.psum_scatter(stack, "dp", scatter_dimension=0, tiled=True)
        return [jnp.zeros_like(total), total]
    return [parts[0]] + [swap_dp(parts[distance], distance) for distance in range(1, size)]


def add_up(own, received):
    total = own.astype(FULL)
    for part in received:
        total = total + part.astype(FULL)
    return total


def exchange_parts(parts):
    size = lax.axis_size("dp")
    if size != 4:
        whole = lax.all_to_all(jnp.stack(parts), "dp", 0, 0)
        return [whole[d] for d in range(size)]
    return [parts[0]] + [swap_dp(parts[d], d) for d in range(1, size)]


def split_parts(value):
    size = lax.axis_size("dp")
    rows = value.shape[0] // size
    return [value[d * rows : (d + 1) * rows] for d in range(size)]


def scatter_dp(value):
    size = lax.axis_size("dp")
    if size != 4:
        return lax.psum_scatter(
            value.astype(LOW), "dp", scatter_dimension=0, tiled=True
        ).astype(FULL)
    own, near, far, cross = split_parts(value)
    half = own.shape[0] // 2
    near, far, cross = near.astype(LOW), far.astype(LOW), cross.astype(LOW)
    by_near = swap_dp(cross[:half], 1)
    by_far = swap_dp(cross[half:], 2)
    near_first = swap_dp(near[:half], 1)
    far_second = swap_dp(far[half:], 2)
    far_first = swap_dp((far[:half].astype(FULL) + by_near.astype(FULL)).astype(LOW), 2)
    near_second = swap_dp((near[half:].astype(FULL) + by_far.astype(FULL)).astype(LOW), 1)
    return own + jnp.concatenate(
        [
            near_first.astype(FULL) + far_first.astype(FULL),
            near_second.astype(FULL) + far_second.astype(FULL),
        ]
    )


def split_rows(value, rows):
    return value[:rows], value[rows:]


def line_up(parts, width):
    rows = parts[0].shape[0]
    whole = jnp.zeros((rows, len(parts) * width), parts[0].dtype)
    for part, who in zip(parts, part_members()):
        whole = lax.dynamic_update_slice_in_dim(whole, part, who * width, 1)
    return whole


def cut_up(value, width):
    return [lax.dynamic_slice_in_dim(value, who * width, width, 1) for who in part_members()]


def is_line():
    return lax.axis_size("grp") == 8


def chip_shift(value, steps):
    pairs = []
    for chip in range(4):
        if 0 <= chip + steps < 4:
            pairs += [(2 * chip + core, 2 * (chip + steps) + core) for core in range(2)]
    return lax.ppermute(value, "grp", pairs)


def core_swap(value):
    return lax.ppermute(value, "grp", [(a, a ^ 1) for a in range(8)])


def gather_earlier(value):
    sequences, rows, width = value.shape
    member = lax.axis_index("grp")
    chunks = ROW_LENGTH // KEY_CHUNK
    if not is_line() or rows != KEY_CHUNK:
        whole = lax.all_gather(value, "grp", axis=1, tiled=True)
        return whole, jnp.arange(chunks, dtype=jnp.int32)
    pieces = [value] + [chip_shift(value, steps) for steps in range(1, 4)]
    pieces += [core_swap(piece) for piece in pieces]
    order = jnp.arange(chunks, dtype=jnp.int32)
    other_core = (order % 2 != member % 2).astype(jnp.int32)
    spots = 4 * other_core + jnp.maximum(member // 2 - order // 2, 0)
    return jnp.concatenate(pieces, axis=1), spots


def scatter_earlier(terms):
    sequences, row_length, width = terms.shape
    if not is_line() or ROW_LENGTH // 8 != KEY_CHUNK:
        total = lax.psum_scatter(terms, "grp", scatter_dimension=1, tiled=True)
        return [total], [total]
    kept, given = terms[:, : row_length // 2], terms[:, row_length // 2 :]
    chip_sums = kept.astype(FULL) + core_swap(given).astype(FULL)
    sent = [chip_sums[:, k * KEY_CHUNK : (k + 1) * KEY_CHUNK].astype(LOW) for k in range(1, 4)]
    own = chip_sums[:, :KEY_CHUNK]
    return [own] + [chip_shift(part, -k) for k, part in enumerate(sent, 1)], sent


def finish_earlier(sums, *meanwhile):
    *sums, _ = lax.optimization_barrier((*sums, meanwhile))
    return add_up(sums[0], sums[1:])


def line_terms(sums, step, upward, downward):
    chip = lax.axis_index("grp") // 2
    up, down = of_chip(sums, chip + 4 - step), of_chip(sums, chip - 4 + step)
    if step > 1:
        up = (up.astype(FULL) + upward.astype(FULL)).astype(LOW)
        down = (down.astype(FULL) + downward.astype(FULL)).astype(LOW)
    return up, down


def line_step(up, down, step):
    up_pairs = [(2 * c + k, 2 * c + 2 + k) for c in range(step) for k in range(2)]
    down_pairs = [(2 * c + k, 2 * c - 2 + k) for c in range(4 - step, 4) for k in range(2)]
    return lax.ppermute(up, "grp", up_pairs), lax.ppermute(down, "grp", down_pairs)


def of_chip(sums, index):
    return lax.dynamic_index_in_dim(sums, jnp.clip(index, 0, 3), 0, keepdims=False)


ANY_SPEC = pl.BlockSpec(memory_space=pltpu.HBM)
READ_GROUPS = 8


def move(source, target, sem, start):
    copy = pltpu.make_async_copy(source, target, sem)
    if start:
        copy.start()
    else:
        copy.wait()


def block_call(kernel, name, table, inputs, outputs, count, piece, aliases=None, spare=4):
    hold = pltpu.VMEM((count, piece, D), LOW)
    return pl.pallas_call(
        kernel,
        grid_spec=pltpu.PrefetchScalarGridSpec(
            num_scalar_prefetch=1,
            grid=(1,),
            in_specs=[ANY_SPEC] * len(inputs),
            out_specs=[ANY_SPEC] * len(outputs),
            scratch_shapes=[hold, pltpu.SemaphoreType.DMA((READ_GROUPS,)), pltpu.SemaphoreType.DMA],
        ),
        out_shape=outputs,
        input_output_aliases=aliases or {},
        compiler_params=pltpu.CompilerParams(
            vmem_limit_bytes=2 * count * piece * D + spare * 1024 * 1024
        ),
        cost_estimate=pl.CostEstimate(
            flops=0, bytes_accessed=4 * count * piece * D, transcendentals=0
        ),
        name=name,
    )(table, *inputs)


def pick_kernel(at_ref, early_ref, late_ref, *refs):
    outs, hold, read_sems, write_sem = refs[:2], refs[2], refs[3], refs[4]
    count = 3 * FF_BLOCKS
    half = FF_BLOCKS // 2
    early_slots, late_slots = at_ref[2 * count], at_ref[2 * count + 1]
    stages = [(0, 0, low) for low in range(0, 2 * FF_BLOCKS, half)]
    stages += [(1, 2 * FF_BLOCKS, low) for low in (0, half)]
    for group, (_, first, low) in enumerate(stages):

        @pl.loop(first + low, first + low + half)
        def _(block):
            owner, slot = at_ref[block], at_ref[count + block]

            @pl.when(slot < early_slots)
            def _():
                source = early_ref.at[owner * early_slots + slot]
                move(source, hold.at[block], read_sems.at[group], True)

            @pl.when(slot >= early_slots)
            def _():
                source = late_ref.at[owner * late_slots + slot - early_slots]
                move(source, hold.at[block], read_sems.at[group], True)

    for start in (True, False):
        for group, (index, first, low) in enumerate(stages):
            some = hold.at[pl.ds(first + low, half)]
            if start:
                move(some, some, read_sems.at[group], False)
            move(some, outs[index].at[pl.ds(low, half)], write_sem, start)


def pick_blocks(owners, slots, early, late, early_slots, late_slots):
    table = jnp.concatenate([owners, slots, jnp.array([early_slots, late_slots], jnp.int32)])
    piece = early.shape[1]
    outs = [jax.ShapeDtypeStruct((count * FF_BLOCKS, piece, D), LOW) for count in (2, 1)]
    return block_call(
        pick_kernel, "pick_blocks", table, (early, late), outs, 3 * FF_BLOCKS, piece, spare=16
    )


def pick_early_kernel(
    team, at_ref, early_ref, query_ref, kv_ref, out_ref, hold, read_sems, write_sem
):
    early_slots = at_ref[2 * GATE_AT]
    share = D // team
    stages = (
        (0, KEY_AT, query_ref, True),
        (KEY_AT, OUT_AT, kv_ref, False),
        (OUT_AT, GATE_AT, out_ref, True),
    )
    for group, (low, high, _, _) in enumerate(stages):

        @pl.loop(low, high)
        def _(block):
            source = early_ref.at[at_ref[block] * early_slots + at_ref[GATE_AT + block]]
            move(source, hold.at[block], read_sems.at[group], True)

    for start in (True, False):
        for group, (low, high, target, by_columns) in enumerate(stages):
            some = pl.ds(low, high - low)
            if start:
                move(hold.at[some], hold.at[some], read_sems.at[group], False)
            if by_columns:
                for band in range(team):
                    lanes = pl.ds(band * share, share)
                    move(hold.at[some, :, lanes], target.at[:, band], write_sem, start)
            else:
                move(hold.at[some], target, write_sem, start)


def pick_early(owners, slots, early, early_slots, team):
    piece = early.shape[1]
    columns = jax.ShapeDtypeStruct((MODEL_BLOCKS, team, piece, D // team), LOW)
    rows = jax.ShapeDtypeStruct((2 * KV_BLOCKS, piece, D), LOW)
    return block_call(
        functools.partial(pick_early_kernel, team),
        "pick_early",
        jnp.concatenate([owners, slots, jnp.array([early_slots], jnp.int32)]),
        (early,),
        [columns, rows, columns],
        GATE_AT,
        piece,
    )


def assemble_kernel(order_ref, *refs):
    count = len(refs) - 4
    parts, whole, hold, read_sems, write_sem = refs[:count], refs[-4], refs[-3], refs[-2], refs[-1]
    rows, width = parts[0].shape
    band = rows // 4
    for start in (True, False):
        for group in range(4):
            some = pl.ds(group * band, band)
            for index, part in enumerate(parts):
                lanes = pl.ds(pl.multiple_of(order_ref[index] * width, width), width)
                move(part.at[some], hold.at[some, lanes], read_sems.at[group], start)
            if not start:
                move(hold.at[some], whole.at[some], write_sem, True)
    move(hold, whole, write_sem, False)


def assemble_columns(parts):
    rows, width = parts[0].shape
    wide = width * len(parts)
    return pl.pallas_call(
        assemble_kernel,
        grid_spec=pltpu.PrefetchScalarGridSpec(
            num_scalar_prefetch=1,
            grid=(1,),
            in_specs=[ANY_SPEC] * len(parts),
            out_specs=ANY_SPEC,
            scratch_shapes=[
                pltpu.VMEM((rows, wide), LOW),
                pltpu.SemaphoreType.DMA((4,)),
                pltpu.SemaphoreType.DMA,
            ],
        ),
        out_shape=jax.ShapeDtypeStruct((rows, wide), LOW),
        compiler_params=pltpu.CompilerParams(vmem_limit_bytes=2 * rows * wide + 4 * 1024 * 1024),
        cost_estimate=pl.CostEstimate(
            flops=0, bytes_accessed=4 * rows * wide, transcendentals=0
        ),
        name="assemble_columns",
    )(jnp.stack(part_members()), *parts)


def in_cut(targets, core, outs, owner, slot, act):
    for (low, high, side), out_ref in zip(targets, outs):
        here = (slot >= low) & (slot < high)
        row = owner
        if side is not None:
            here = here & ((owner % 2 == core) if side == 0 else (owner % 2 != core))
            row = owner // 2

        @pl.when(here)
        def _():
            act(out_ref.at[row * (high - low) + slot - low])


def target_shape(target, piece):
    low, high, side = target
    owners = lax.axis_size("grp") // (1 if side is None else 2)
    return jax.ShapeDtypeStruct((owners * (high - low), piece, D), LOW)


def place_ff_kernel(targets, at_ref, *refs):
    terms, outs = refs[:2], refs[2:-3]
    hold, read_sems, write_sem = refs[-3:]
    count = 3 * FF_BLOCKS
    half = FF_BLOCKS // 2
    stages = [(0, 0, low) for low in range(0, 2 * FF_BLOCKS, half)]
    stages += [(1, 2 * FF_BLOCKS, low) for low in (0, half)]
    for start in (True, False):
        for group, (index, first, low) in enumerate(stages):
            target = hold.at[pl.ds(first + low, half)]
            move(terms[index].at[pl.ds(low, half)], target, read_sems.at[group], start)
            if start:
                continue

            @pl.loop(first + low, first + low + half)
            def _(block):
                in_cut(
                    targets,
                    at_ref[2 * count],
                    outs,
                    at_ref[block],
                    at_ref[count + block],
                    lambda target: move(hold.at[block], target, write_sem, True),
                )

    move(hold, hold, write_sem, False)


def place_ff(owners, slots, terms, targets):
    piece = terms[0].shape[1]
    return block_call(
        functools.partial(place_ff_kernel, targets),
        "place_ff",
        jnp.concatenate([owners, slots, lax.axis_index("grp")[None] % 2]),
        terms,
        [target_shape(target, piece) for target in targets],
        3 * FF_BLOCKS,
        piece,
    )


def place_more_kernel(team, targets, kinds, at_ref, *refs):
    sources, outs = refs[: len(kinds)], refs[-3 - len(targets) : -3]
    hold, read_sems, write_sem = refs[-3:]
    share = D // team
    total = sum(count for count, _ in kinds)

    def write(block, start):
        in_cut(
            targets,
            at_ref[2 * total],
            outs,
            at_ref[block],
            at_ref[total + block],
            lambda target: move(hold.at[block], target, write_sem, start),
        )

    for start in (True, False):
        low = 0
        for group, ((count, by_columns), source) in enumerate(zip(kinds, sources)):
            some = pl.ds(low, count)
            if by_columns:
                for band in range(team):
                    lanes = pl.ds(band * share, share)
                    move(source.at[:, band], hold.at[some, :, lanes], read_sems.at[group], start)
            else:
                move(source, hold.at[some], read_sems.at[group], start)
            if not start:

                @pl.loop(low, low + count)
                def _(block):
                    write(block, True)

            low += count

    @pl.loop(0, total)
    def _(block):
        write(block, False)


def place_more(name, owners, slots, terms, kinds, placed, targets, team):
    piece = placed[0].shape[1]
    return block_call(
        functools.partial(place_more_kernel, team, targets, kinds),
        name,
        jnp.concatenate([owners, slots, lax.axis_index("grp")[None] % 2]),
        (*terms, *placed),
        [jax.ShapeDtypeStruct(part.shape, LOW) for part in placed],
        sum(count for count, _ in kinds),
        piece,
        {1 + len(terms) + index: index for index in range(len(placed))},
    )


def adamw_by_products(master, first, second, gradient):
    first_new = BETA_ONE * first + (1.0 - BETA_ONE) * gradient
    second_new = BETA_TWO * second + (1.0 - BETA_TWO) * (gradient * gradient)
    root = jnp.sqrt(second_new * (1.0 / (1.0 - BETA_TWO**STEP))) + ADAM_EPS
    stepped = (first_new * (WEIGHT_RATE / (1.0 - BETA_ONE**STEP))) / root
    return ((1.0 - WEIGHT_RATE * WEIGHT_DECAY) * master - stepped, first_new, second_new)


STRIPS = 1


def adamw_kernel(team, first_slot, at_ref, master, first, second, *refs):
    parts = refs[:team]
    new_master, new_first, new_second, copy, shares = refs[-5:]
    kind = at_ref[team + first_slot + pl.program_id(0)]
    strip = pl.program_id(1)
    piece, share = R // team, D // team

    @pl.when(strip == 0)
    def _():
        for index in range(team):
            shares[at_ref[index]] = parts[index][0]

    def update(rows, lanes, gradient):
        results = adamw_by_products(
            master[0, rows, lanes], first[0, rows, lanes], second[0, rows, lanes], gradient
        )
        for target, value in zip((new_master, new_first, new_second), results):
            target[0, rows, lanes] = value
        copy[0, rows, lanes] = results[0].astype(LOW)

    bands = team // STRIPS
    for turn_of in range(STRIPS):
        for band in range(bands):
            rows = slice(band * piece, (band + 1) * piece)
            source = turn_of * bands + band
            here = strip == turn_of

            @pl.when(here & (kind == 1))
            def _():
                update(rows, slice(0, D), shares[source].astype(FULL))

            @pl.when(here & (kind == 2))
            def _():
                for index in range(team):
                    lanes = slice(index * share, (index + 1) * share)
                    gradient = shares[index, :, source * share : (source + 1) * share]
                    update(rows, lanes, gradient.astype(FULL))

            @pl.when(here & (kind == 0))
            def _():
                update(rows, slice(0, D), jnp.zeros((piece, D), FULL))


def adamw_slots(kinds, master, first, second, parts, first_slot, so_far):
    team = len(parts)
    count = parts[0].shape[0]
    slot_spec = pl.BlockSpec((1, R // STRIPS, D), lambda i, j, a: (first_slot + i, j, 0))
    part_spec = pl.BlockSpec((1, R // team, D), lambda i, j, a: (i, 0, 0))
    whole = jax.ShapeDtypeStruct(master.shape, FULL)
    extra = [] if so_far is None else list(so_far)
    return pl.pallas_call(
        functools.partial(adamw_kernel, team, first_slot),
        grid_spec=pltpu.PrefetchScalarGridSpec(
            num_scalar_prefetch=1,
            grid=(count, STRIPS),
            in_specs=[slot_spec] * 3 + [part_spec] * team + [ANY_SPEC] * len(extra),
            out_specs=[slot_spec] * 4,
            scratch_shapes=[pltpu.VMEM((team, R // team, D), LOW)],
        ),
        out_shape=[whole, whole, whole, jax.ShapeDtypeStruct(master.shape, LOW)],
        input_output_aliases={4 + team + k: k for k in range(len(extra))},
        compiler_params=pltpu.CompilerParams(vmem_limit_bytes=52 * 1024 * 1024),
        cost_estimate=pl.CostEstimate(
            flops=20 * count * R * D, bytes_accessed=28 * count * R * D, transcendentals=0
        ),
        name="adamw_slots",
    )(jnp.concatenate([jnp.stack(part_members()), kinds]), master, first, second, *parts, *extra)


def after(value, *others):
    return lax.optimization_barrier((value,) + others)[0]


def per_device(
    layer_input,
    out_cotangent,
    seq_lengths,
    block_owner,
    weight_master,
    weight_first,
    weight_second,
    gain_master,
    gain_first,
    gain_second,
):
    slot_count = weight_master.shape[0]
    team = lax.axis_size("dp")
    rank = lax.axis_index("dp")
    member = lax.axis_index("grp")
    piece = R // team
    sequence_count = layer_input.shape[0]
    segment_rows = layer_input.shape[1]
    token_count = sequence_count * segment_rows
    model_share = D // team
    kv_share = KEY_VALUE_WIDTH // team
    ff_share = FF // team
    early_slots = slot_count * 5 // 12
    late_slots = slot_count - early_slots
    sides = (0, 1) if is_line() and team == 4 else (None,)
    targets = tuple((0, early_slots, side) for side in sides) + ((early_slots, slot_count, None),)

    block_order = jnp.arange(BLOCKS, dtype=jnp.int32)
    same_owner = block_owner[:, None] == block_owner[None, :]
    earlier = block_order[None, :] < block_order[:, None]
    slots = jnp.sum((same_owner & earlier).astype(jnp.int32), axis=1)
    whole_columns = (block_order < KEY_AT) | ((block_order >= OUT_AT) & (block_order < GATE_AT))
    block_kind = jnp.where(whole_columns, 2, 1)
    mine = (block_owner == member)[None, :] & (
        slots[None, :] == jnp.arange(slot_count, dtype=jnp.int32)[:, None]
    )
    kinds = jnp.sum(jnp.where(mine, block_kind[None, :], 0), axis=1)
    my_attention = jnp.any(mine & (block_order < GATE_AT)[None, :], axis=1)
    spills = jnp.any(slots[:GATE_AT] >= early_slots)

    def shares_of(low, high):
        count = high - low
        by_rows = lax.dynamic_slice(weight_master, (low, rank * piece, 0), (count, piece, D))
        by_columns = lax.dynamic_slice(
            weight_master, (low, 0, rank * model_share), (count, R, model_share)
        ).astype(LOW)
        by_columns = jnp.concatenate(
            [by_columns[:, j * piece : (j + 1) * piece] for j in range(team)], axis=-1
        )
        return jnp.where((kinds[low:high] == 2)[:, None, None], by_columns, by_rows.astype(LOW))

    shares_early = shares_of(0, early_slots)
    shares_late = shares_of(early_slots, slot_count)
    gathered_early = lax.all_gather(shares_early, "grp", axis=0, tiled=True)
    gathered_late = lax.all_gather(shares_late, "grp", axis=0, tiled=True)
    gains_all = lax.all_gather(gain_master.astype(LOW), "grp", axis=1, tiled=True)

    positions = member * segment_rows + jnp.arange(segment_rows, dtype=jnp.int32)
    valid_rows = (positions[None, :] < seq_lengths[:, None]).reshape(token_count, 1)
    cosine_rows, sine_rows = rotary_tables(positions, HEAD_WIDTH)
    wide_cosine = jnp.concatenate([cosine_rows] * 4, axis=1)
    wide_sine = jnp.concatenate([-sine_rows, sine_rows] * 2, axis=1)
    places = jnp.concatenate(
        [jnp.stack([member * segment_rows, jnp.int32(segment_rows)]), seq_lengths]
    ).astype(jnp.int32)
    inputs = layer_input.reshape(token_count, D).astype(FULL)
    root_one = lax.rsqrt(jnp.mean(inputs * inputs, axis=-1, keepdims=True) + NORM_EPS)
    normed_one = inputs * root_one
    gain_one = gains_all[0].astype(FULL)
    gain_two = gains_all[1].astype(FULL)
    hidden_one = (normed_one * gain_one).astype(LOW)
    hidden_one_all = gather_dp(hidden_one)
    grad_out = jnp.where(valid_rows, out_cotangent.reshape(token_count, D), jnp.zeros((), LOW))
    grad_out_all = gather_dp(after(grad_out, hidden_one_all))
    gathered_early = after(gathered_early, hidden_one_all, grad_out_all)

    def attention_early():
        return tuple(
            pick_early(block_owner[:GATE_AT], slots[:GATE_AT], gathered_early, early_slots, team)
        )

    def attention_spilled():
        everything = lax.all_gather(
            jnp.concatenate([shares_early, shares_late]), "grp", axis=0, tiled=True
        )
        found = jnp.take(
            everything, (block_owner * slot_count + slots)[:GATE_AT], axis=0, mode="clip"
        )

        def columns(first):
            chosen = found[first : first + MODEL_BLOCKS]
            return chosen.reshape(MODEL_BLOCKS, piece, team, model_share).transpose(0, 2, 1, 3)

        return columns(0), found[KEY_AT:OUT_AT], columns(OUT_AT)

    query_share, kv_rows, out_share = lax.cond(spills, attention_spilled, attention_early)
    query_share = query_share.reshape(D, model_share)
    kv_rows = kv_rows.reshape(2 * kv_share, D)
    out_share = out_share.reshape(D, model_share)


    kv_shares = contract_rows(hidden_one_all, kv_rows).astype(LOW)
    kv_parts = exchange_parts(split_parts(kv_shares))
    query_shares = plain_dot(after(hidden_one_all, kv_shares), query_share).astype(LOW)
    query_parts = exchange_parts(split_parts(query_shares))
    kv_proj = (
        line_up(kv_parts, 2 * kv_share)
        .reshape(token_count, team, 2 * KV_BLOCKS, piece)
        .transpose(0, 2, 1, 3)
        .reshape(token_count, 2 * KEY_VALUE_WIDTH)
    )
    keys_local = apply_rotation(
        kv_proj[:, :KEY_VALUE_WIDTH]
        .astype(FULL)
        .reshape(sequence_count, segment_rows, KEY_VALUE_HEADS, HEAD_WIDTH),
        cosine_rows,
        sine_rows,
    ).astype(LOW)
    kv_local = jnp.concatenate(
        [
            keys_local.reshape(sequence_count, segment_rows, KEY_VALUE_WIDTH),
            kv_proj[:, KEY_VALUE_WIDTH:].reshape(sequence_count, segment_rows, KEY_VALUE_WIDTH),
        ],
        axis=-1,
    )
    kv_all, spots = gather_earlier(kv_local)
    query_proj = line_up(query_parts, model_share).reshape(sequence_count, segment_rows, D)
    w_out = assemble_columns(gather_parts(after(out_share, query_proj, kv_local)))

    attended, logs = attend_forward(places, spots, wide_cosine, wide_sine, query_proj, kv_all)
    attended_flat = attended.reshape(token_count, D)
    residual = inputs + plain_dot(attended_flat, w_out)
    root_two = lax.rsqrt(jnp.mean(residual * residual, axis=-1, keepdims=True) + NORM_EPS)
    normed_two = residual * root_two
    hidden_two = (normed_two * gain_two).astype(LOW)

    hidden_two_parts = gather_direct(hidden_two)
    ff_blocks = pick_blocks(
        block_owner[GATE_AT:],
        slots[GATE_AT:],
        gathered_early,
        after(gathered_late, hidden_two),
        early_slots,
        late_slots,
    )
    w_both, w_down = ff_blocks[0].reshape(2 * ff_share, D), ff_blocks[1].reshape(ff_share, D)
    grad_out_parts = split_parts(grad_out_all)
    inner = jnp.zeros((team * token_count, ff_share), LOW)
    grad_both = jnp.zeros((team * token_count, 2 * ff_share), LOW)
    inner_parts, grad_htwo_parts = [], []
    for index, (hidden, given) in enumerate(zip(hidden_two_parts, grad_out_parts)):
        if index > 0:
            hidden = after(hidden, grad_htwo_parts[-1])
        both = contract_rows(hidden, w_both)
        gate_pre, up_pre = both[:, :ff_share], both[:, ff_share:]
        sigmoid_gate = jax.nn.sigmoid(gate_pre)
        activated = gate_pre * sigmoid_gate
        inner_parts.append((activated * up_pre).astype(LOW))
        grad_inner = contract_rows(given, w_down)
        grad_gate = grad_inner * up_pre * (sigmoid_gate * (1.0 + gate_pre * (1.0 - sigmoid_gate)))
        grad_up = grad_inner * activated
        grad_part = jnp.concatenate([grad_gate.astype(LOW), grad_up.astype(LOW)], axis=1)
        part = plain_dot(grad_part, w_both)
        grad_htwo_parts.append(part if index == 0 else part.astype(LOW))
        first = index * token_count
        inner = lax.dynamic_update_slice(inner, inner_parts[-1], (first, 0))
        grad_both = lax.dynamic_update_slice(grad_both, grad_part, (first, 0))
    grad_htwo_sent = send_parts(grad_htwo_parts)
    grad_htwo = add_up(grad_htwo_sent[0], grad_htwo_sent[1:])
    hidden_two_all = jnp.concatenate(hidden_two_parts, axis=0)
    grad_both = after(grad_both, grad_htwo_sent[1])
    both_terms = contract_first(grad_both, hidden_two_all).astype(LOW)
    inner = after(inner, both_terms, *grad_htwo_sent[1:])
    ff_terms = [
        both_terms.reshape(-1, piece, D),
        contract_first(inner, grad_out_all).astype(LOW).reshape(-1, piece, D),
    ]
    cut_terms = place_ff(block_owner[GATE_AT:], slots[GATE_AT:], ff_terms, targets)
    late_terms = cut_terms[-1]
    late_sums = lax.psum_scatter(late_terms, "grp", scatter_dimension=0, tiled=True)

    grad_htwo = after(grad_htwo, late_terms)
    scaled_two = grad_htwo * gain_two
    grad_resid = grad_out.astype(FULL) + root_two * (
        scaled_two - normed_two * jnp.mean(scaled_two * normed_two, axis=-1, keepdims=True)
    )
    resid_low = grad_resid.astype(LOW)
    grad_attended = contract_rows(resid_low, w_out).astype(LOW)
    down_parts = [plain_dot(part, after(w_down, grad_attended)) for part in inner_parts]
    down_parts = down_parts[:1] + [part.astype(LOW) for part in down_parts[1:]]
    down_sent = send_parts(down_parts)
    crossing = [
        jnp.concatenate([after(attended_flat, grad_attended), share], axis=1)
        for share in cut_up(resid_low, model_share)
    ]
    if team == 4:
        farthest = crossing[3]
        crossing = [crossing[0], swap_dp(crossing[1], 1), swap_dp(crossing[2], 2)]
    else:
        crossing = exchange_parts(crossing)
    grad_query, kv_terms = attend_backward(
        places,
        spots,
        wide_cosine,
        wide_sine,
        query_proj,
        kv_all,
        attended,
        grad_attended.reshape(sequence_count, segment_rows, D),
        logs,
    )
    grad_query, kv_terms, crossing, down_sent = lax.optimization_barrier(
        (grad_query, kv_terms, crossing, down_sent)
    )
    query_share_parts = exchange_parts(cut_up(grad_query.reshape(token_count, D), model_share))
    key_value_sums, kv_terms = scatter_earlier(kv_terms)
    query_share_parts = lax.optimization_barrier((query_share_parts, kv_terms))[0]
    grad_query_share = jnp.concatenate(query_share_parts, axis=0)
    if team == 4:
        crossing = crossing + [swap_dp(after(farthest, *kv_terms), 3)]
    attended_all = jnp.concatenate([part[:, :D] for part in crossing], axis=0)
    resid_share = jnp.concatenate([part[:, D:] for part in crossing], axis=0)
    column_shape = (MODEL_BLOCKS, team, piece, model_share)
    out_terms = contract_first(attended_all, resid_share).astype(LOW).reshape(column_shape)
    early_terms = place_more(
        "place_out",
        block_owner[OUT_AT:GATE_AT],
        slots[OUT_AT:GATE_AT],
        (out_terms,),
        ((MODEL_BLOCKS, True),),
        cut_terms[:-1],
        targets[:-1],
        team,
    )
    query_terms = contract_first(hidden_one_all, grad_query_share).astype(LOW)
    key_value_sums = finish_earlier(key_value_sums, early_terms, query_terms)
    grad_keys = apply_rotation(
        key_value_sums[:, :, :KEY_VALUE_WIDTH].reshape(
            sequence_count, segment_rows, KEY_VALUE_HEADS, HEAD_WIDTH
        ),
        cosine_rows,
        -sine_rows,
    ).reshape(token_count, KEY_VALUE_WIDTH)
    grad_values = key_value_sums[:, :, KEY_VALUE_WIDTH:].reshape(token_count, KEY_VALUE_WIDTH)
    grad_kv = (
        jnp.concatenate([grad_keys, grad_values], axis=1)
        .astype(LOW)
        .reshape(token_count, 2 * KV_BLOCKS, team, piece)
        .transpose(0, 2, 1, 3)
        .reshape(token_count, 2 * KEY_VALUE_WIDTH)
    )
    grad_kv_share = jnp.concatenate(exchange_parts(cut_up(grad_kv, 2 * kv_share)), axis=0)

    kv_weight_terms = contract_first(grad_kv_share, hidden_one_all).astype(LOW)
    attention_terms = [
        query_terms.reshape(column_shape),
        kv_weight_terms.reshape(2 * KV_BLOCKS, piece, D),
        out_terms,
    ]
    early_terms = place_more(
        "place_query",
        block_owner[:OUT_AT],
        slots[:OUT_AT],
        attention_terms[:2],
        ((MODEL_BLOCKS, True), (2 * KV_BLOCKS, False)),
        early_terms,
        targets[:-1],
        team,
    )

    def nothing_spilled():
        return jnp.zeros((late_slots, piece, D), LOW)

    def sums_spilled():
        by_columns = [
            attention_terms[k].transpose(0, 2, 1, 3).reshape(MODEL_BLOCKS, piece, D) for k in (0, 2)
        ]
        found = jnp.concatenate([by_columns[0], attention_terms[1], by_columns[1]], axis=0)
        every_slot = jnp.arange(slot_count * lax.axis_size("grp"), dtype=jnp.int32)
        hits = (block_owner * slot_count + slots)[None, :GATE_AT] == every_slot[:, None]
        which = jnp.sum(jnp.where(hits, block_order[None, :GATE_AT], 0), axis=1)
        spread = jnp.where(
            jnp.any(hits, axis=1)[:, None, None],
            jnp.take(found, which, axis=0, mode="clip"),
            jnp.zeros((), LOW),
        )
        extra = lax.psum_scatter(spread, "grp", scatter_dimension=0, tiled=True)
        return extra[early_slots:]

    late_extra = lax.cond(
        after(spills, late_sums, early_terms[0]), sums_spilled, nothing_spilled
    )

    spilled = spills & my_attention[early_slots:]
    late_sums = jnp.where(spilled[:, None, None], late_extra, late_sums)
    late_half = late_slots // 2
    states = (weight_master, weight_first, weight_second)

    def query_gradient(share):
        return contract_rows(share, query_share) + plain_dot(grad_kv_share, kv_rows)

    def finish_input(grad_hone):
        scaled_one = grad_hone * gain_one
        spread = jnp.mean(scaled_one * normed_one, axis=-1, keepdims=True)
        input_grad = grad_resid + root_one * (scaled_one - normed_one * spread)
        gain_terms = [
            jnp.sum(grad_hone * normed_one, axis=0), jnp.sum(grad_htwo * normed_two, axis=0)
        ]
        return (
            input_grad.astype(LOW).reshape(sequence_count, segment_rows, D),
            jnp.stack(gain_terms),
        )

    def finish_output(sent):
        output = residual + add_up(sent[0], sent[1:])
        return (
            jnp.where(valid_rows, output, 0.0)
            .astype(LOW)
            .reshape(sequence_count, segment_rows, D)
        )

    def update(parts, low, updated):
        return adamw_slots(kinds, *states, parts, low, updated)

    if is_line() and team == 4:
        tie = lax.optimization_barrier

        def as_slots(rows):
            return rows.reshape(-1, piece, D)

        def join(*pieces):
            return jnp.concatenate([as_slots(rows) for rows in pieces], axis=0)

        kept, given = early_terms
        given, late_sums, grad_query_share = tie((given, late_sums, grad_query_share))
        swapped = core_swap(given)
        first, second = late_sums[:late_half], late_sums[late_half:]
        first_near = near_far(first)
        grad_hone = query_gradient(grad_query_share)
        swapped, grad_hone = tie((swapped, grad_hone))
        sums = (kept.astype(FULL) + swapped.astype(FULL)).astype(LOW)
        sums = sums.reshape(4, early_slots, piece, D)
        up, down = line_terms(sums, 1, None, None)
        upward, downward = line_step(up, down, 1)
        own, near, far, cross = split_parts(grad_hone)
        near, far, cross = near.astype(LOW), far.astype(LOW), cross.astype(LOW)
        rows = token_count // 2
        step = late_half // 2
        first_near, near, far, cross, _, _ = tie((first_near, near, far, cross, up, down))
        by_near = swap_dp(join(first_near[1][:step], near[:rows], cross[:rows]), 1)
        by_far = swap_dp(join(first_near[0][step:], far[rows:], cross[rows:]), 2)
        upward, downward, near, far = tie((upward, downward, near, far))
        up, down = line_terms(sums, 2, upward, downward)
        upward, downward = line_step(up, down, 2)
        by_near, by_far, near, far, _, _ = tie((by_near, by_far, near, far, up, down))
        first_cross = join(by_near[:step], by_far[: late_half - step])
        near_first, by_way_near = split_rows(by_near[step:].reshape(-1, D), rows)
        far_second, by_way_far = split_rows(by_far[late_half - step :].reshape(-1, D), rows)
        far_first = (far[:rows].astype(FULL) + by_way_near.astype(FULL)).astype(LOW)
        near_second = (near[rows:].astype(FULL) + by_way_far.astype(FULL)).astype(LOW)
        by_near = swap_dp(join(second, near_second), 1)
        by_far = swap_dp(join(second, far_first), 2)
        upward, downward, near_second, far_first = tie(
            (upward, downward, near_second, far_first)
        )
        up, down = line_terms(sums, 3, upward, downward)
        upward, downward = line_step(up, down, 3)
        by_near, by_far, _, _ = tie((by_near, by_far, up, down))
        second_near = [by_near[:late_half], by_far[:late_half]]
        second_cross = cross_of(*second_near)
        parts, second_near = tie(([first, *first_near, first_cross], second_near))
        updated = update(parts, early_slots, None)
        upward, downward, updated = tie((upward, downward, updated))
        early_sums = of_chip(sums, member // 2).astype(FULL)
        early_sums = (early_sums + upward.astype(FULL) + downward.astype(FULL)).astype(LOW)
        early_near = near_far(early_sums)
        parts = [second, *second_near, jnp.concatenate(second_cross, axis=0)]
        parts, updated, early_sums = tie((parts, updated, early_sums))
        updated = update(parts, early_slots + late_half, updated)
        near_first, by_far, updated = tie((near_first, by_far, updated))
        grad_hone = own + jnp.concatenate(
            [
                near_first.astype(FULL) + by_far[late_half:].reshape(rows, D).astype(FULL),
                by_near[late_half:].reshape(rows, D).astype(FULL) + far_second.astype(FULL),
            ]
        )
        input_grad, gain_terms = finish_input(grad_hone)
        others = [swap_dp(gain_terms, distance) for distance in range(1, team)]
        early_near, gain_terms = tie((early_near, gain_terms))
        early_cross = cross_of(*early_near)
        down_sent, early_near = tie((down_sent, early_near))
        layer_output = finish_output(down_sent)
        gain_terms, others, layer_output = tie((gain_terms, others, layer_output))
        gain_terms = add_up(gain_terms, others)
        other = core_swap(gain_terms)
        gain_terms, other, early_cross = tie((gain_terms, other, early_cross))
        gain_terms = gain_terms + other
        around = [
            lax.ppermute(gain_terms, "grp", [(a, (a + 2 * turn_by) % 8) for a in range(8)])
            for turn_by in range(1, 4)
        ]
        parts = [early_sums, *early_near, jnp.concatenate(early_cross, axis=0)]
        parts, gain_terms, updated = tie((parts, gain_terms, updated))
        updated = update(parts, 0, updated)
        gain_grad = add_up(gain_terms, around)
    else:
        updated = update(gather_parts(late_sums), early_slots, None)
        early_sums = lax.psum_scatter(early_terms[0], "grp", scatter_dimension=0, tiled=True)
        updated = update(gather_parts(early_sums), 0, updated)
        input_grad, gain_terms = finish_input(scatter_dp(query_gradient(grad_query_share)))
        gain_grad = lax.psum(gain_terms, ("dp", "grp"))
        layer_output = finish_output(down_sent)
    new_master, new_first, new_second, weight_copy = updated

    share_width = gain_master.shape[1]
    gain_share = lax.dynamic_slice_in_dim(gain_grad, member * share_width, share_width, 1)
    new_gain, new_gain_first, new_gain_second = adamw(
        gain_master, gain_first, gain_second, gain_share, GAIN_RATE, 0.0
    )
    return (
        layer_output,
        input_grad,
        new_master,
        new_first,
        new_second,
        weight_copy,
        new_gain,
        new_gain_first,
        new_gain_second,
    )


def solution(mesh):
    return jax.shard_map(
        per_device,
        mesh=mesh,
        in_specs=(
            P("dp", "grp", None),
            P("dp", "grp", None),
            P("dp"),
            P(),
            P("grp", None, None),
            P("grp", None, None),
            P("grp", None, None),
            P(None, "grp"),
            P(None, "grp"),
            P(None, "grp"),
        ),
        out_specs=(
            P("dp", "grp", None),
            P("dp", "grp", None),
            P("grp", None, None),
            P("grp", None, None),
            P("grp", None, None),
            P("grp", None, None),
            P(None, "grp"),
            P(None, "grp"),
            P(None, "grp"),
        ),
        check_vma=False,
    )
```

```python
import functools
import math

import jax
import jax.numpy as jnp
from jax import lax
from jax.experimental import pallas as pl
from jax.experimental.pallas import tpu as pltpu
from jax.sharding import PartitionSpec as P

D = 2048
QUERY_HEADS = 32
KEY_VALUE_HEADS = 4
HEAD_WIDTH = 64
FF = 5632
ROW_LENGTH = 2048
R = 128
STEP = 7
KEY_VALUE_WIDTH = 256
MODEL_BLOCKS = D // R
KV_BLOCKS = KEY_VALUE_WIDTH // R
FF_BLOCKS = FF // R
KEY_AT = MODEL_BLOCKS
OUT_AT = MODEL_BLOCKS + 2 * KV_BLOCKS
GATE_AT = OUT_AT + MODEL_BLOCKS
UP_AT = GATE_AT + FF_BLOCKS
DOWN_AT = UP_AT + FF_BLOCKS
BLOCKS = DOWN_AT + FF_BLOCKS

NORM_EPS = 1e-05
BETA_ONE = 0.9
BETA_TWO = 0.95
ADAM_EPS = 1e-08
WEIGHT_RATE = 0.1
GAIN_RATE = 0.5
WEIGHT_DECAY = 0.1
MASKED = -1e30
LOW = jnp.bfloat16
FULL = jnp.float32


def rotary_tables(positions, head_size):
    halfway = head_size // 2
    spacing = jnp.arange(halfway, dtype=FULL) * (-2.0 * math.log(10000.0) / head_size)
    angles = positions.astype(FULL)[:, None] * jnp.exp(spacing)[None, :]
    return (jnp.cos(angles), jnp.sin(angles))


def apply_rotation(values, cosine_rows, sine_rows):
    halfway = values.shape[-1] // 2
    leading = values[..., :halfway]
    trailing = values[..., halfway:]
    cos_rows = cosine_rows[:, None, :]
    sin_rows = sine_rows[:, None, :]
    return jnp.concatenate(
        [leading * cos_rows - trailing * sin_rows, trailing * cos_rows + leading * sin_rows],
        axis=-1,
    )


def contract_rows(left, right):
    return lax.dot_general(left, right, (((1,), (1,)), ((), ())), preferred_element_type=FULL)


def contract_first(left, right):
    return lax.dot_general(left, right, (((0,), (0,)), ((), ())), preferred_element_type=FULL)


def plain_dot(left, right):
    return jnp.dot(left, right, preferred_element_type=FULL)


def adamw(master, first, second, gradient, rate, decay):
    first_new = BETA_ONE * first + (1.0 - BETA_ONE) * gradient
    second_new = BETA_TWO * second + (1.0 - BETA_TWO) * gradient * gradient
    first_fix = 1.0 - BETA_ONE**STEP
    second_fix = 1.0 - BETA_TWO**STEP
    stepped = first_new / first_fix / (jnp.sqrt(second_new / second_fix) + ADAM_EPS)
    return (master - rate * (stepped + decay * master), first_new, second_new)


KEY_CHUNK = 256
GROUP_WIDTH = D // KEY_VALUE_HEADS
PAIRS = GROUP_WIDTH // 128
EXP_SCALE = math.log2(math.e) / math.sqrt(HEAD_WIDTH)


def lanes_of(shape):
    return lax.broadcasted_iota(jnp.int32, shape, len(shape) - 1)


def swap_halves(values):
    first = (lanes_of(values.shape) % HEAD_WIDTH) < HEAD_WIDTH // 2
    return jnp.where(first, pltpu.roll(values, 96, 1), pltpu.roll(values, 32, 1))


def turn(values, cosine, sine):
    return values * cosine + swap_halves(values) * sine


def chunk_bounds(where_ref):
    start, rows, length = where_ref[0], where_ref[1], where_ref[2 + pl.program_id(0)]
    free = jnp.minimum(start // KEY_CHUNK, length // KEY_CHUNK)
    last = jnp.minimum(start + rows, length)
    return free, (last + KEY_CHUNK - 1) // KEY_CHUNK, start, length


def chunk_rows(spots_ref, chunk):
    return pl.ds(pl.multiple_of(spots_ref[chunk] * KEY_CHUNK, KEY_CHUNK), KEY_CHUNK)


def stacked(block, odd):
    wide = block.astype(FULL)
    wide = jnp.where(odd, pltpu.roll(wide, 64, 1), wide)
    low = jnp.where(lanes_of(wide.shape) < HEAD_WIDTH, wide, 0.0)
    return jnp.concatenate([low, pltpu.roll(low, 64, 1)], axis=0)


def mask_of(chunk, start, length, queries):
    keys = chunk * KEY_CHUNK + lax.broadcasted_iota(jnp.int32, (KEY_CHUNK, queries), 0)
    places = start + lax.broadcasted_iota(jnp.int32, (KEY_CHUNK, queries), 1)
    allowed = (keys <= places) & (keys < length)
    return jnp.concatenate([allowed, allowed], axis=0)


def across(left, right):
    return lax.dot_general(left, right, (((1,), (1,)), ((), ())), preferred_element_type=FULL)


def attend_forward_kernel(
    where_ref, spots_ref, cos_ref, sin_ref, q_ref, k_ref, v_ref, out_ref, log_ref, turned, peaks, sums, totals
):
    queries = q_ref.shape[1]
    odd = (pl.program_id(1) % 2) == 1
    free, end, start, length = chunk_bounds(where_ref)
    for pair in range(PAIRS):
        lanes = slice(128 * pair, 128 * pair + 128)
        turned[:, lanes] = turn(q_ref[0, :, lanes].astype(FULL), cos_ref[...], sin_ref[...]).astype(LOW)
    peaks[...] = jnp.full(peaks.shape, MASKED, FULL)
    sums[...] = jnp.zeros(sums.shape, FULL)
    totals[...] = jnp.zeros(totals.shape, FULL)

    def step(chunk, masked):
        rows = chunk_rows(spots_ref, chunk)
        keys = stacked(k_ref[0, rows, :], odd).astype(LOW)
        values = stacked(v_ref[0, rows, :], odd).T.astype(LOW)
        allowed = mask_of(chunk, start, length, queries) if masked else None
        for pair in range(PAIRS):
            scores = across(keys, turned[:, 128 * pair : 128 * pair + 128]) * EXP_SCALE
            if masked:
                scores = jnp.where(allowed, scores, MASKED)
            weights, fades = [], []
            for side in range(2):
                head = slice(2 * pair + side, 2 * pair + side + 1)
                part = scores[side * KEY_CHUNK : (side + 1) * KEY_CHUNK]
                old = peaks[head, :]
                new = jnp.maximum(old, jnp.max(part, axis=0, keepdims=True))
                weight = jnp.exp2(part - new)
                fade = jnp.exp2(old - new)
                peaks[head, :] = new
                sums[head, :] = sums[head, :] * fade + jnp.sum(weight, axis=0, keepdims=True)
                weights.append(weight.astype(LOW))
                fades.append(jnp.broadcast_to(fade, (HEAD_WIDTH, queries)))
            mixed = jnp.dot(values, jnp.concatenate(weights, axis=0), preferred_element_type=FULL)
            totals[pair] = totals[pair] * jnp.concatenate(fades, axis=0) + mixed

    @pl.loop(0, free)
    def _(chunk):
        step(chunk, False)

    @pl.loop(free, end)
    def _(chunk):
        step(chunk, True)

    for pair in range(PAIRS):
        shares = [
            jnp.broadcast_to(1.0 / sums[2 * pair + side : 2 * pair + side + 1, :], (HEAD_WIDTH, queries))
            for side in range(2)
        ]
        mixed = totals[pair] * jnp.concatenate(shares, axis=0)
        out_ref[0, :, 128 * pair : 128 * pair + 128] = mixed.T.astype(LOW)
    log_ref[0] = peaks[...] + jnp.log2(sums[...])


def attend_backward_kernel(
    where_ref, spots_ref, cos_ref, sin_ref, q_ref, k_ref, v_ref, out_ref, grad_ref, log_ref,
    dq_ref, dkv_ref, turned, dots, turning, key_sums, value_sums,
):
    queries = q_ref.shape[1]
    group = pl.program_id(1)
    odd = (group % 2) == 1
    free, end, start, length = chunk_bounds(where_ref)
    for pair in range(PAIRS):
        lanes = slice(128 * pair, 128 * pair + 128)
        turned[:, lanes] = turn(q_ref[0, :, lanes].astype(FULL), cos_ref[...], sin_ref[...]).astype(LOW)
        products = (out_ref[0, :, lanes].astype(FULL) * grad_ref[0, :, lanes].astype(FULL)).T
        dots[2 * pair : 2 * pair + 1, :] = jnp.sum(products[:HEAD_WIDTH], axis=0, keepdims=True)
        dots[2 * pair + 1 : 2 * pair + 2, :] = jnp.sum(products[HEAD_WIDTH:], axis=0, keepdims=True)
    turning[...] = jnp.zeros(turning.shape, FULL)

    @pl.when(group == 0)
    def _():
        dkv_ref[...] = jnp.zeros(dkv_ref.shape, LOW)

    key_lanes = pl.ds(pl.multiple_of((group // 2) * 128, 128), 128)
    value_lanes = pl.ds(pl.multiple_of(KEY_VALUE_WIDTH + (group // 2) * 128, 128), 128)

    def step(chunk, masked):
        rows = chunk_rows(spots_ref, chunk)
        wide_keys = stacked(k_ref[0, rows, :], odd)
        keys = wide_keys.astype(LOW)
        keys_down = wide_keys.T.astype(LOW)
        values = stacked(v_ref[0, rows, :], odd).astype(LOW)
        allowed = mask_of(chunk, start, length, queries) if masked else None
        for pair in range(PAIRS):
            lanes = slice(128 * pair, 128 * pair + 128)
            asked = turned[:, lanes]
            given = grad_ref[0, :, lanes]
            scores = across(keys, asked) * EXP_SCALE
            if masked:
                scores = jnp.where(allowed, scores, MASKED)
            slopes = across(values, given)
            weights, moves = [], []
            for side in range(2):
                head = slice(2 * pair + side, 2 * pair + side + 1)
                part = slice(side * KEY_CHUNK, (side + 1) * KEY_CHUNK)
                weight = jnp.exp2(scores[part] - log_ref[0, head, :])
                weights.append(weight.astype(LOW))
                moves.append((weight * (slopes[part] - dots[head, :])).astype(LOW))
            weights = jnp.concatenate(weights, axis=0)
            moves = jnp.concatenate(moves, axis=0)
            value_part = jnp.dot(weights, given, preferred_element_type=FULL)
            key_part = jnp.dot(moves, asked, preferred_element_type=FULL)
            if pair == 0:
                value_sums[...] = value_part
                key_sums[...] = key_part
            else:
                value_sums[...] += value_part
                key_sums[...] += key_part
            turning[pair] += jnp.dot(keys_down, moves, preferred_element_type=FULL)
        for sums, lanes, scale in (
            (key_sums, key_lanes, 1.0 / math.sqrt(HEAD_WIDTH)),
            (value_sums, value_lanes, 1.0),
        ):
            both = (sums[:KEY_CHUNK] + pltpu.roll(sums[KEY_CHUNK:], 64, 1)) * scale
            low_side = lanes_of(both.shape) < HEAD_WIDTH
            kept = dkv_ref[0, rows, lanes].astype(FULL)
            mine = jnp.where(odd, pltpu.roll(both, 64, 1), both)
            dkv_ref[0, rows, lanes] = jnp.where(low_side != odd, mine, kept).astype(LOW)

    @pl.loop(0, free)
    def _(chunk):
        step(chunk, False)

    @pl.loop(free, end)
    def _(chunk):
        step(chunk, True)

    for pair in range(PAIRS):
        back = turning[pair].T * (1.0 / math.sqrt(HEAD_WIDTH))
        dq_ref[0, :, 128 * pair : 128 * pair + 128] = turn(back, cos_ref[...], -sin_ref[...]).astype(LOW)


def attention_specs(sequences, rows, row_length):
    q_spec = pl.BlockSpec((1, rows, GROUP_WIDTH), lambda s, g, w, t: (s, 0, g))
    k_spec = pl.BlockSpec((1, row_length, 128), lambda s, g, w, t: (s, 0, g // 2))
    v_spec = pl.BlockSpec((1, row_length, 128), lambda s, g, w, t: (s, 0, 2 + g // 2))
    table_spec = pl.BlockSpec((rows, 128), lambda s, g, w, t: (0, 0))
    log_spec = pl.BlockSpec((1, 2 * PAIRS, rows), lambda s, g, w, t: (s, g, 0))
    return q_spec, k_spec, v_spec, table_spec, log_spec


def attend_forward(places, spots, cosine, sine, query_proj, kv_all):
    sequences, rows, _ = query_proj.shape
    row_length = kv_all.shape[1]
    q_spec, k_spec, v_spec, table_spec, log_spec = attention_specs(sequences, rows, row_length)
    pairs = sequences * QUERY_HEADS * rows * row_length
    return pl.pallas_call(
        attend_forward_kernel,
        grid_spec=pltpu.PrefetchScalarGridSpec(
            num_scalar_prefetch=2,
            grid=(sequences, KEY_VALUE_HEADS),
            in_specs=[table_spec, table_spec, q_spec, k_spec, v_spec],
            out_specs=[q_spec, log_spec],
            scratch_shapes=[
                pltpu.VMEM((rows, GROUP_WIDTH), LOW),
                pltpu.VMEM((2 * PAIRS, rows), FULL),
                pltpu.VMEM((2 * PAIRS, rows), FULL),
                pltpu.VMEM((PAIRS, 128, rows), FULL),
            ],
        ),
        out_shape=[
            jax.ShapeDtypeStruct(query_proj.shape, LOW),
            jax.ShapeDtypeStruct((sequences, QUERY_HEADS, rows), FULL),
        ],
        compiler_params=pltpu.CompilerParams(vmem_limit_bytes=40 * 1024 * 1024),
        cost_estimate=pl.CostEstimate(
            flops=4 * HEAD_WIDTH * pairs, bytes_accessed=8 * 1024 * 1024, transcendentals=pairs
        ),
        name="attend_forward",
    )(places, spots, cosine, sine, query_proj, kv_all, kv_all)


def attend_backward(places, spots, cosine, sine, query_proj, kv_all, attended, grad_attended, logs):
    sequences, rows, _ = query_proj.shape
    row_length = kv_all.shape[1]
    q_spec, k_spec, v_spec, table_spec, log_spec = attention_specs(sequences, rows, row_length)
    pairs = sequences * QUERY_HEADS * rows * row_length
    return pl.pallas_call(
        attend_backward_kernel,
        grid_spec=pltpu.PrefetchScalarGridSpec(
            num_scalar_prefetch=2,
            grid=(sequences, KEY_VALUE_HEADS),
            in_specs=[table_spec, table_spec, q_spec, k_spec, v_spec, q_spec, q_spec, log_spec],
            out_specs=[
                q_spec,
                pl.BlockSpec((1, row_length, 2 * KEY_VALUE_WIDTH), lambda s, g, w, t: (s, 0, 0)),
            ],
            scratch_shapes=[
                pltpu.VMEM((rows, GROUP_WIDTH), LOW),
                pltpu.VMEM((2 * PAIRS, rows), FULL),
                pltpu.VMEM((PAIRS, 128, rows), FULL),
                pltpu.VMEM((2 * KEY_CHUNK, 128), FULL),
                pltpu.VMEM((2 * KEY_CHUNK, 128), FULL),
            ],
        ),
        out_shape=[
            jax.ShapeDtypeStruct(query_proj.shape, LOW),
            jax.ShapeDtypeStruct((sequences, row_length, 2 * KEY_VALUE_WIDTH), LOW),
        ],
        compiler_params=pltpu.CompilerParams(vmem_limit_bytes=40 * 1024 * 1024),
        cost_estimate=pl.CostEstimate(
            flops=10 * HEAD_WIDTH * pairs, bytes_accessed=12 * 1024 * 1024, transcendentals=pairs
        ),
        name="attend_backward",
    )(places, spots, cosine, sine, query_proj, kv_all, kv_all, attended, grad_attended, logs)


def swap_dp(value, distance):
    size = lax.axis_size("dp")
    return lax.ppermute(value, "dp", [(a, a ^ distance) for a in range(size)])


def part_members():
    size = lax.axis_size("dp")
    rank = lax.axis_index("dp")
    return [rank ^ d if size == 4 else jnp.int32(d) for d in range(size)]


def near_far(value):
    return [swap_dp(value, 1), swap_dp(value, 2)]


def cross_of(near, far):
    half = near.shape[0] // 2
    return [swap_dp(far[:half], 1), swap_dp(near[half:], 2)]


def gather_parts(value):
    size = lax.axis_size("dp")
    if size != 4:
        whole = lax.all_gather(value, "dp", axis=0)
        return [whole[d] for d in range(size)]
    beside = near_far(value)
    return [value, *beside, jnp.concatenate(cross_of(*beside), axis=0)]


def gather_dp(value):
    return jnp.concatenate(gather_parts(value), axis=0)


def gather_direct(value):
    size = lax.axis_size("dp")
    if size != 4:
        return gather_parts(value)
    near, far = swap_dp(value, 1), swap_dp(value, 2)
    return [value, near, far, swap_dp(value, 3)]


def send_parts(parts):
    size = lax.axis_size("dp")
    if size != 4:
        stack = jnp.concatenate([part.astype(LOW) for part in parts], axis=0)
        total = lax.psum_scatter(stack, "dp", scatter_dimension=0, tiled=True)
        return [jnp.zeros_like(total), total]
    return [parts[0]] + [swap_dp(parts[distance], distance) for distance in range(1, size)]


def add_up(own, received):
    total = own.astype(FULL)
    for part in received:
        total = total + part.astype(FULL)
    return total


def exchange_parts(parts):
    size = lax.axis_size("dp")
    if size != 4:
        whole = lax.all_to_all(jnp.stack(parts), "dp", 0, 0)
        return [whole[d] for d in range(size)]
    return [parts[0]] + [swap_dp(parts[d], d) for d in range(1, size)]


def split_parts(value):
    size = lax.axis_size("dp")
    rows = value.shape[0] // size
    return [value[d * rows : (d + 1) * rows] for d in range(size)]


def scatter_dp(value):
    size = lax.axis_size("dp")
    if size != 4:
        return lax.psum_scatter(
            value.astype(LOW), "dp", scatter_dimension=0, tiled=True
        ).astype(FULL)
    own, near, far, cross = split_parts(value)
    half = own.shape[0] // 2
    near, far, cross = near.astype(LOW), far.astype(LOW), cross.astype(LOW)
    by_near = swap_dp(cross[:half], 1)
    by_far = swap_dp(cross[half:], 2)
    near_first = swap_dp(near[:half], 1)
    far_second = swap_dp(far[half:], 2)
    far_first = swap_dp((far[:half].astype(FULL) + by_near.astype(FULL)).astype(LOW), 2)
    near_second = swap_dp((near[half:].astype(FULL) + by_far.astype(FULL)).astype(LOW), 1)
    return own + jnp.concatenate(
        [
            near_first.astype(FULL) + far_first.astype(FULL),
            near_second.astype(FULL) + far_second.astype(FULL),
        ]
    )


def split_rows(value, rows):
    return value[:rows], value[rows:]


def line_up(parts, width):
    rows = parts[0].shape[0]
    whole = jnp.zeros((rows, len(parts) * width), parts[0].dtype)
    for part, who in zip(parts, part_members()):
        whole = lax.dynamic_update_slice_in_dim(whole, part, who * width, 1)
    return whole


def cut_up(value, width):
    return [lax.dynamic_slice_in_dim(value, who * width, width, 1) for who in part_members()]


def is_line():
    return lax.axis_size("grp") == 8


def chip_shift(value, steps):
    pairs = []
    for chip in range(4):
        if 0 <= chip + steps < 4:
            pairs += [(2 * chip + core, 2 * (chip + steps) + core) for core in range(2)]
    return lax.ppermute(value, "grp", pairs)


def core_swap(value):
    return lax.ppermute(value, "grp", [(a, a ^ 1) for a in range(8)])


def gather_earlier(value):
    sequences, rows, width = value.shape
    member = lax.axis_index("grp")
    chunks = ROW_LENGTH // KEY_CHUNK
    if not is_line() or rows != KEY_CHUNK:
        whole = lax.all_gather(value, "grp", axis=1, tiled=True)
        return whole, jnp.arange(chunks, dtype=jnp.int32)
    pieces = [value] + [chip_shift(value, steps) for steps in range(1, 4)]
    pieces += [core_swap(piece) for piece in pieces]
    order = jnp.arange(chunks, dtype=jnp.int32)
    other_core = (order % 2 != member % 2).astype(jnp.int32)
    spots = 4 * other_core + jnp.maximum(member // 2 - order // 2, 0)
    return jnp.concatenate(pieces, axis=1), spots


def scatter_earlier(terms):
    sequences, row_length, width = terms.shape
    if not is_line() or ROW_LENGTH // 8 != KEY_CHUNK:
        total = lax.psum_scatter(terms, "grp", scatter_dimension=1, tiled=True)
        return [total], [total]
    kept, given = terms[:, : row_length // 2], terms[:, row_length // 2 :]
    chip_sums = kept.astype(FULL) + core_swap(given).astype(FULL)
    sent = [chip_sums[:, k * KEY_CHUNK : (k + 1) * KEY_CHUNK].astype(LOW) for k in range(1, 4)]
    own = chip_sums[:, :KEY_CHUNK]
    return [own] + [chip_shift(part, -k) for k, part in enumerate(sent, 1)], sent


def finish_earlier(sums, *meanwhile):
    *sums, _ = lax.optimization_barrier((*sums, meanwhile))
    return add_up(sums[0], sums[1:])


def line_terms(sums, step, upward, downward):
    chip = lax.axis_index("grp") // 2
    up, down = of_chip(sums, chip + 4 - step), of_chip(sums, chip - 4 + step)
    if step > 1:
        up = (up.astype(FULL) + upward.astype(FULL)).astype(LOW)
        down = (down.astype(FULL) + downward.astype(FULL)).astype(LOW)
    return up, down


def line_step(up, down, step):
    up_pairs = [(2 * c + k, 2 * c + 2 + k) for c in range(step) for k in range(2)]
    down_pairs = [(2 * c + k, 2 * c - 2 + k) for c in range(4 - step, 4) for k in range(2)]
    return lax.ppermute(up, "grp", up_pairs), lax.ppermute(down, "grp", down_pairs)


def of_chip(sums, index):
    return lax.dynamic_index_in_dim(sums, jnp.clip(index, 0, 3), 0, keepdims=False)


ANY_SPEC = pl.BlockSpec(memory_space=pltpu.HBM)
READ_GROUPS = 8


def move(source, target, sem, start):
    copy = pltpu.make_async_copy(source, target, sem)
    if start:
        copy.start()
    else:
        copy.wait()


def block_call(kernel, name, table, inputs, outputs, count, piece, aliases=None, spare=4):
    hold = pltpu.VMEM((count, piece, D), LOW)
    return pl.pallas_call(
        kernel,
        grid_spec=pltpu.PrefetchScalarGridSpec(
            num_scalar_prefetch=1,
            grid=(1,),
            in_specs=[ANY_SPEC] * len(inputs),
            out_specs=[ANY_SPEC] * len(outputs),
            scratch_shapes=[hold, pltpu.SemaphoreType.DMA((READ_GROUPS,)), pltpu.SemaphoreType.DMA],
        ),
        out_shape=outputs,
        input_output_aliases=aliases or {},
        compiler_params=pltpu.CompilerParams(
            vmem_limit_bytes=2 * count * piece * D + spare * 1024 * 1024
        ),
        cost_estimate=pl.CostEstimate(
            flops=0, bytes_accessed=4 * count * piece * D, transcendentals=0
        ),
        name=name,
    )(table, *inputs)


def pick_kernel(at_ref, early_ref, late_ref, *refs):
    outs, hold, read_sems, write_sem = refs[:2], refs[2], refs[3], refs[4]
    count = 3 * FF_BLOCKS
    half = FF_BLOCKS // 2
    early_slots, late_slots = at_ref[2 * count], at_ref[2 * count + 1]
    stages = [(0, 0, low) for low in range(0, 2 * FF_BLOCKS, half)]
    stages += [(1, 2 * FF_BLOCKS, low) for low in (0, half)]
    for group, (_, first, low) in enumerate(stages):

        @pl.loop(first + low, first + low + half)
        def _(block):
            owner, slot = at_ref[block], at_ref[count + block]

            @pl.when(slot < early_slots)
            def _():
                source = early_ref.at[owner * early_slots + slot]
                move(source, hold.at[block], read_sems.at[group], True)

            @pl.when(slot >= early_slots)
            def _():
                source = late_ref.at[owner * late_slots + slot - early_slots]
                move(source, hold.at[block], read_sems.at[group], True)

    for start in (True, False):
        for group, (index, first, low) in enumerate(stages):
            some = hold.at[pl.ds(first + low, half)]
            if start:
                move(some, some, read_sems.at[group], False)
            move(some, outs[index].at[pl.ds(low, half)], write_sem, start)


def pick_blocks(owners, slots, early, late, early_slots, late_slots):
    table = jnp.concatenate([owners, slots, jnp.array([early_slots, late_slots], jnp.int32)])
    piece = early.shape[1]
    outs = [jax.ShapeDtypeStruct((count * FF_BLOCKS, piece, D), LOW) for count in (2, 1)]
    return block_call(
        pick_kernel, "pick_blocks", table, (early, late), outs, 3 * FF_BLOCKS, piece, spare=16
    )


def pick_early_kernel(
    team, at_ref, early_ref, query_ref, kv_ref, out_ref, hold, read_sems, write_sem
):
    early_slots = at_ref[2 * GATE_AT]
    share = D // team
    stages = (
        (0, KEY_AT, query_ref, True),
        (KEY_AT, OUT_AT, kv_ref, False),
        (OUT_AT, GATE_AT, out_ref, True),
    )
    for group, (low, high, _, _) in enumerate(stages):

        @pl.loop(low, high)
        def _(block):
            source = early_ref.at[at_ref[block] * early_slots + at_ref[GATE_AT + block]]
            move(source, hold.at[block], read_sems.at[group], True)

    for start in (True, False):
        for group, (low, high, target, by_columns) in enumerate(stages):
            some = pl.ds(low, high - low)
            if start:
                move(hold.at[some], hold.at[some], read_sems.at[group], False)
            if by_columns:
                for band in range(team):
                    lanes = pl.ds(band * share, share)
                    move(hold.at[some, :, lanes], target.at[:, band], write_sem, start)
            else:
                move(hold.at[some], target, write_sem, start)


def pick_early(owners, slots, early, early_slots, team):
    piece = early.shape[1]
    columns = jax.ShapeDtypeStruct((MODEL_BLOCKS, team, piece, D // team), LOW)
    rows = jax.ShapeDtypeStruct((2 * KV_BLOCKS, piece, D), LOW)
    return block_call(
        functools.partial(pick_early_kernel, team),
        "pick_early",
        jnp.concatenate([owners, slots, jnp.array([early_slots], jnp.int32)]),
        (early,),
        [columns, rows, columns],
        GATE_AT,
        piece,
    )


def assemble_kernel(order_ref, *refs):
    count = len(refs) - 4
    parts, whole, hold, read_sems, write_sem = refs[:count], refs[-4], refs[-3], refs[-2], refs[-1]
    rows, width = parts[0].shape
    band = rows // 4
    for start in (True, False):
        for group in range(4):
            some = pl.ds(group * band, band)
            for index, part in enumerate(parts):
                lanes = pl.ds(pl.multiple_of(order_ref[index] * width, width), width)
                move(part.at[some], hold.at[some, lanes], read_sems.at[group], start)
            if not start:
                move(hold.at[some], whole.at[some], write_sem, True)
    move(hold, whole, write_sem, False)


def assemble_columns(parts):
    rows, width = parts[0].shape
    wide = width * len(parts)
    return pl.pallas_call(
        assemble_kernel,
        grid_spec=pltpu.PrefetchScalarGridSpec(
            num_scalar_prefetch=1,
            grid=(1,),
            in_specs=[ANY_SPEC] * len(parts),
            out_specs=ANY_SPEC,
            scratch_shapes=[
                pltpu.VMEM((rows, wide), LOW),
                pltpu.SemaphoreType.DMA((4,)),
                pltpu.SemaphoreType.DMA,
            ],
        ),
        out_shape=jax.ShapeDtypeStruct((rows, wide), LOW),
        compiler_params=pltpu.CompilerParams(vmem_limit_bytes=2 * rows * wide + 4 * 1024 * 1024),
        cost_estimate=pl.CostEstimate(
            flops=0, bytes_accessed=4 * rows * wide, transcendentals=0
        ),
        name="assemble_columns",
    )(jnp.stack(part_members()), *parts)


def in_cut(targets, core, outs, owner, slot, act):
    for (low, high, side), out_ref in zip(targets, outs):
        here = (slot >= low) & (slot < high)
        row = owner
        if side is not None:
            here = here & ((owner % 2 == core) if side == 0 else (owner % 2 != core))
            row = owner // 2

        @pl.when(here)
        def _():
            act(out_ref.at[row * (high - low) + slot - low])


def target_shape(target, piece):
    low, high, side = target
    owners = lax.axis_size("grp") // (1 if side is None else 2)
    return jax.ShapeDtypeStruct((owners * (high - low), piece, D), LOW)


def place_ff_kernel(targets, at_ref, *refs):
    terms, outs = refs[:2], refs[2:-3]
    hold, read_sems, write_sem = refs[-3:]
    count = 3 * FF_BLOCKS
    half = FF_BLOCKS // 2
    stages = [(0, 0, low) for low in range(0, 2 * FF_BLOCKS, half)]
    stages += [(1, 2 * FF_BLOCKS, low) for low in (0, half)]
    for start in (True, False):
        for group, (index, first, low) in enumerate(stages):
            target = hold.at[pl.ds(first + low, half)]
            move(terms[index].at[pl.ds(low, half)], target, read_sems.at[group], start)
            if start:
                continue

            @pl.loop(first + low, first + low + half)
            def _(block):
                in_cut(
                    targets,
                    at_ref[2 * count],
                    outs,
                    at_ref[block],
                    at_ref[count + block],
                    lambda target: move(hold.at[block], target, write_sem, True),
                )

    move(hold, hold, write_sem, False)


def place_ff(owners, slots, terms, targets):
    piece = terms[0].shape[1]
    return block_call(
        functools.partial(place_ff_kernel, targets),
        "place_ff",
        jnp.concatenate([owners, slots, lax.axis_index("grp")[None] % 2]),
        terms,
        [target_shape(target, piece) for target in targets],
        3 * FF_BLOCKS,
        piece,
    )


def place_more_kernel(team, targets, kinds, at_ref, *refs):
    sources, outs = refs[: len(kinds)], refs[-3 - len(targets) : -3]
    hold, read_sems, write_sem = refs[-3:]
    share = D // team
    total = sum(count for count, _ in kinds)

    def write(block, start):
        in_cut(
            targets,
            at_ref[2 * total],
            outs,
            at_ref[block],
            at_ref[total + block],
            lambda target: move(hold.at[block], target, write_sem, start),
        )

    for start in (True, False):
        low = 0
        for group, ((count, by_columns), source) in enumerate(zip(kinds, sources)):
            some = pl.ds(low, count)
            if by_columns:
                for band in range(team):
                    lanes = pl.ds(band * share, share)
                    move(source.at[:, band], hold.at[some, :, lanes], read_sems.at[group], start)
            else:
                move(source, hold.at[some], read_sems.at[group], start)
            if not start:

                @pl.loop(low, low + count)
                def _(block):
                    write(block, True)

            low += count

    @pl.loop(0, total)
    def _(block):
        write(block, False)


def place_more(name, owners, slots, terms, kinds, placed, targets, team):
    piece = placed[0].shape[1]
    return block_call(
        functools.partial(place_more_kernel, team, targets, kinds),
        name,
        jnp.concatenate([owners, slots, lax.axis_index("grp")[None] % 2]),
        (*terms, *placed),
        [jax.ShapeDtypeStruct(part.shape, LOW) for part in placed],
        sum(count for count, _ in kinds),
        piece,
        {1 + len(terms) + index: index for index in range(len(placed))},
    )


def adamw_by_products(master, first, second, gradient):
    first_new = BETA_ONE * first + (1.0 - BETA_ONE) * gradient
    second_new = BETA_TWO * second + (1.0 - BETA_TWO) * (gradient * gradient)
    root = jnp.sqrt(second_new * (1.0 / (1.0 - BETA_TWO**STEP))) + ADAM_EPS
    stepped = (first_new * (WEIGHT_RATE / (1.0 - BETA_ONE**STEP))) / root
    return ((1.0 - WEIGHT_RATE * WEIGHT_DECAY) * master - stepped, first_new, second_new)


STRIPS = 1


def adamw_kernel(team, first_slot, at_ref, master, first, second, *refs):
    parts = refs[:team]
    new_master, new_first, new_second, copy, shares = refs[-5:]
    kind = at_ref[team + first_slot + pl.program_id(0)]
    strip = pl.program_id(1)
    piece, share = R // team, D // team

    @pl.when(strip == 0)
    def _():
        for index in range(team):
            shares[at_ref[index]] = parts[index][0]

    def update(rows, lanes, gradient):
        results = adamw_by_products(
            master[0, rows, lanes], first[0, rows, lanes], second[0, rows, lanes], gradient
        )
        for target, value in zip((new_master, new_first, new_second), results):
            target[0, rows, lanes] = value
        copy[0, rows, lanes] = results[0].astype(LOW)

    bands = team // STRIPS
    for turn_of in range(STRIPS):
        for band in range(bands):
            rows = slice(band * piece, (band + 1) * piece)
            source = turn_of * bands + band
            here = strip == turn_of

            @pl.when(here & (kind == 1))
            def _():
                update(rows, slice(0, D), shares[source].astype(FULL))

            @pl.when(here & (kind == 2))
            def _():
                for index in range(team):
                    lanes = slice(index * share, (index + 1) * share)
                    gradient = shares[index, :, source * share : (source + 1) * share]
                    update(rows, lanes, gradient.astype(FULL))

            @pl.when(here & (kind == 0))
            def _():
                update(rows, slice(0, D), jnp.zeros((piece, D), FULL))


def adamw_slots(kinds, master, first, second, parts, first_slot, so_far):
    team = len(parts)
    count = parts[0].shape[0]
    slot_spec = pl.BlockSpec((1, R // STRIPS, D), lambda i, j, a: (first_slot + i, j, 0))
    part_spec = pl.BlockSpec((1, R // team, D), lambda i, j, a: (i, 0, 0))
    whole = jax.ShapeDtypeStruct(master.shape, FULL)
    extra = [] if so_far is None else list(so_far)
    return pl.pallas_call(
        functools.partial(adamw_kernel, team, first_slot),
        grid_spec=pltpu.PrefetchScalarGridSpec(
            num_scalar_prefetch=1,
            grid=(count, STRIPS),
            in_specs=[slot_spec] * 3 + [part_spec] * team + [ANY_SPEC] * len(extra),
            out_specs=[slot_spec] * 4,
            scratch_shapes=[pltpu.VMEM((team, R // team, D), LOW)],
        ),
        out_shape=[whole, whole, whole, jax.ShapeDtypeStruct(master.shape, LOW)],
        input_output_aliases={4 + team + k: k for k in range(len(extra))},
        compiler_params=pltpu.CompilerParams(vmem_limit_bytes=52 * 1024 * 1024),
        cost_estimate=pl.CostEstimate(
            flops=20 * count * R * D, bytes_accessed=28 * count * R * D, transcendentals=0
        ),
        name="adamw_slots",
    )(jnp.concatenate([jnp.stack(part_members()), kinds]), master, first, second, *parts, *extra)


def after(value, *others):
    return lax.optimization_barrier((value,) + others)[0]


def per_device(
    layer_input,
    out_cotangent,
    seq_lengths,
    block_owner,
    weight_master,
    weight_first,
    weight_second,
    gain_master,
    gain_first,
    gain_second,
):
    slot_count = weight_master.shape[0]
    team = lax.axis_size("dp")
    rank = lax.axis_index("dp")
    member = lax.axis_index("grp")
    piece = R // team
    sequence_count = layer_input.shape[0]
    segment_rows = layer_input.shape[1]
    token_count = sequence_count * segment_rows
    model_share = D // team
    kv_share = KEY_VALUE_WIDTH // team
    ff_share = FF // team
    early_slots = slot_count * 5 // 12
    late_slots = slot_count - early_slots
    sides = (0, 1) if is_line() and team == 4 else (None,)
    targets = tuple((0, early_slots, side) for side in sides) + ((early_slots, slot_count, None),)

    block_order = jnp.arange(BLOCKS, dtype=jnp.int32)
    same_owner = block_owner[:, None] == block_owner[None, :]
    earlier = block_order[None, :] < block_order[:, None]
    slots = jnp.sum((same_owner & earlier).astype(jnp.int32), axis=1)
    whole_columns = (block_order < KEY_AT) | ((block_order >= OUT_AT) & (block_order < GATE_AT))
    block_kind = jnp.where(whole_columns, 2, 1)
    mine = (block_owner == member)[None, :] & (
        slots[None, :] == jnp.arange(slot_count, dtype=jnp.int32)[:, None]
    )
    kinds = jnp.sum(jnp.where(mine, block_kind[None, :], 0), axis=1)
    my_attention = jnp.any(mine & (block_order < GATE_AT)[None, :], axis=1)
    spills = jnp.any(slots[:GATE_AT] >= early_slots)

    def shares_of(low, high):
        count = high - low
        by_rows = lax.dynamic_slice(weight_master, (low, rank * piece, 0), (count, piece, D))
        by_columns = lax.dynamic_slice(
            weight_master, (low, 0, rank * model_share), (count, R, model_share)
        ).astype(LOW)
        by_columns = jnp.concatenate(
            [by_columns[:, j * piece : (j + 1) * piece] for j in range(team)], axis=-1
        )
        return jnp.where((kinds[low:high] == 2)[:, None, None], by_columns, by_rows.astype(LOW))

    shares_early = shares_of(0, early_slots)
    shares_late = shares_of(early_slots, slot_count)
    gathered_early = lax.all_gather(shares_early, "grp", axis=0, tiled=True)
    gathered_late = lax.all_gather(shares_late, "grp", axis=0, tiled=True)
    gains_all = lax.all_gather(gain_master.astype(LOW), "grp", axis=1, tiled=True)

    positions = member * segment_rows + jnp.arange(segment_rows, dtype=jnp.int32)
    valid_rows = (positions[None, :] < seq_lengths[:, None]).reshape(token_count, 1)
    cosine_rows, sine_rows = rotary_tables(positions, HEAD_WIDTH)
    wide_cosine = jnp.concatenate([cosine_rows] * 4, axis=1)
    wide_sine = jnp.concatenate([-sine_rows, sine_rows] * 2, axis=1)
    places = jnp.concatenate(
        [jnp.stack([member * segment_rows, jnp.int32(segment_rows)]), seq_lengths]
    ).astype(jnp.int32)
    inputs = layer_input.reshape(token_count, D).astype(FULL)
    root_one = lax.rsqrt(jnp.mean(inputs * inputs, axis=-1, keepdims=True) + NORM_EPS)
    normed_one = inputs * root_one
    gain_one = gains_all[0].astype(FULL)
    gain_two = gains_all[1].astype(FULL)
    hidden_one = (normed_one * gain_one).astype(LOW)
    hidden_one_all = gather_dp(hidden_one)
    grad_out = jnp.where(valid_rows, out_cotangent.reshape(token_count, D), jnp.zeros((), LOW))
    grad_out_all = gather_dp(after(grad_out, hidden_one_all))
    gathered_early = after(gathered_early, hidden_one_all, grad_out_all)

    def attention_early():
        return tuple(
            pick_early(block_owner[:GATE_AT], slots[:GATE_AT], gathered_early, early_slots, team)
        )

    def attention_spilled():
        everything = lax.all_gather(
            jnp.concatenate([shares_early, shares_late]), "grp", axis=0, tiled=True
        )
        found = jnp.take(
            everything, (block_owner * slot_count + slots)[:GATE_AT], axis=0, mode="clip"
        )

        def columns(first):
            chosen = found[first : first + MODEL_BLOCKS]
            return chosen.reshape(MODEL_BLOCKS, piece, team, model_share).transpose(0, 2, 1, 3)

        return columns(0), found[KEY_AT:OUT_AT], columns(OUT_AT)

    query_share, kv_rows, out_share = lax.cond(spills, attention_spilled, attention_early)
    query_share = query_share.reshape(D, model_share)
    kv_rows = kv_rows.reshape(2 * kv_share, D)
    out_share = out_share.reshape(D, model_share)


    kv_shares = contract_rows(hidden_one_all, kv_rows).astype(LOW)
    kv_parts = exchange_parts(split_parts(kv_shares))
    query_shares = plain_dot(after(hidden_one_all, kv_shares), query_share).astype(LOW)
    query_parts = exchange_parts(split_parts(query_shares))
    kv_proj = (
        line_up(kv_parts, 2 * kv_share)
        .reshape(token_count, team, 2 * KV_BLOCKS, piece)
        .transpose(0, 2, 1, 3)
        .reshape(token_count, 2 * KEY_VALUE_WIDTH)
    )
    keys_local = apply_rotation(
        kv_proj[:, :KEY_VALUE_WIDTH]
        .astype(FULL)
        .reshape(sequence_count, segment_rows, KEY_VALUE_HEADS, HEAD_WIDTH),
        cosine_rows,
        sine_rows,
    ).astype(LOW)
    kv_local = jnp.concatenate(
        [
            keys_local.reshape(sequence_count, segment_rows, KEY_VALUE_WIDTH),
            kv_proj[:, KEY_VALUE_WIDTH:].reshape(sequence_count, segment_rows, KEY_VALUE_WIDTH),
        ],
        axis=-1,
    )
    kv_all, spots = gather_earlier(kv_local)
    query_proj = line_up(query_parts, model_share).reshape(sequence_count, segment_rows, D)
    w_out = assemble_columns(gather_parts(after(out_share, query_proj, kv_local)))

    attended, logs = attend_forward(places, spots, wide_cosine, wide_sine, query_proj, kv_all)
    attended_flat = attended.reshape(token_count, D)
    residual = inputs + plain_dot(attended_flat, w_out)
    root_two = lax.rsqrt(jnp.mean(residual * residual, axis=-1, keepdims=True) + NORM_EPS)
    normed_two = residual * root_two
    hidden_two = (normed_two * gain_two).astype(LOW)

    hidden_two_parts = gather_direct(hidden_two)
    ff_blocks = pick_blocks(
        block_owner[GATE_AT:],
        slots[GATE_AT:],
        gathered_early,
        after(gathered_late, hidden_two),
        early_slots,
        late_slots,
    )
    w_both, w_down = ff_blocks[0].reshape(2 * ff_share, D), ff_blocks[1].reshape(ff_share, D)
    grad_out_parts = split_parts(grad_out_all)
    inner = jnp.zeros((team * token_count, ff_share), LOW)
    grad_both = jnp.zeros((team * token_count, 2 * ff_share), LOW)
    inner_parts, grad_htwo_parts = [], []
    for index, (hidden, given) in enumerate(zip(hidden_two_parts, grad_out_parts)):
        if index > 0:
            hidden = after(hidden, grad_htwo_parts[-1])
        both = contract_rows(hidden, w_both)
        gate_pre, up_pre = both[:, :ff_share], both[:, ff_share:]
        sigmoid_gate = jax.nn.sigmoid(gate_pre)
        activated = gate_pre * sigmoid_gate
        inner_parts.append((activated * up_pre).astype(LOW))
        grad_inner = contract_rows(given, w_down)
        grad_gate = grad_inner * up_pre * (sigmoid_gate * (1.0 + gate_pre * (1.0 - sigmoid_gate)))
        grad_up = grad_inner * activated
        grad_part = jnp.concatenate([grad_gate.astype(LOW), grad_up.astype(LOW)], axis=1)
        part = plain_dot(grad_part, w_both)
        grad_htwo_parts.append(part if index == 0 else part.astype(LOW))
        first = index * token_count
        inner = lax.dynamic_update_slice(inner, inner_parts[-1], (first, 0))
        grad_both = lax.dynamic_update_slice(grad_both, grad_part, (first, 0))
    grad_htwo_sent = send_parts(grad_htwo_parts)
    grad_htwo = add_up(grad_htwo_sent[0], grad_htwo_sent[1:])
    hidden_two_all = jnp.concatenate(hidden_two_parts, axis=0)
    grad_both = after(grad_both, grad_htwo_sent[1])
    both_terms = contract_first(grad_both, hidden_two_all).astype(LOW)
    inner = after(inner, both_terms, *grad_htwo_sent[1:])
    ff_terms = [
        both_terms.reshape(-1, piece, D),
        contract_first(inner, grad_out_all).astype(LOW).reshape(-1, piece, D),
    ]
    cut_terms = place_ff(block_owner[GATE_AT:], slots[GATE_AT:], ff_terms, targets)
    late_terms = cut_terms[-1]
    late_sums = lax.psum_scatter(late_terms, "grp", scatter_dimension=0, tiled=True)

    grad_htwo = after(grad_htwo, late_terms)
    scaled_two = grad_htwo * gain_two
    grad_resid = grad_out.astype(FULL) + root_two * (
        scaled_two - normed_two * jnp.mean(scaled_two * normed_two, axis=-1, keepdims=True)
    )
    resid_low = grad_resid.astype(LOW)
    grad_attended = contract_rows(resid_low, w_out).astype(LOW)
    down_parts = [plain_dot(part, after(w_down, grad_attended)) for part in inner_parts]
    down_parts = down_parts[:1] + [part.astype(LOW) for part in down_parts[1:]]
    down_sent = send_parts(down_parts)
    crossing = [
        jnp.concatenate([after(attended_flat, grad_attended), share], axis=1)
        for share in cut_up(resid_low, model_share)
    ]
    if team == 4:
        farthest = crossing[3]
        crossing = [crossing[0], swap_dp(crossing[1], 1), swap_dp(crossing[2], 2)]
    else:
        crossing = exchange_parts(crossing)
    grad_query, kv_terms = attend_backward(
        places,
        spots,
        wide_cosine,
        wide_sine,
        query_proj,
        kv_all,
        attended,
        grad_attended.reshape(sequence_count, segment_rows, D),
        logs,
    )
    grad_query, kv_terms, crossing, down_sent = lax.optimization_barrier(
        (grad_query, kv_terms, crossing, down_sent)
    )
    query_share_parts = exchange_parts(cut_up(grad_query.reshape(token_count, D), model_share))
    key_value_sums, kv_terms = scatter_earlier(kv_terms)
    query_share_parts = lax.optimization_barrier((query_share_parts, kv_terms))[0]
    grad_query_share = jnp.concatenate(query_share_parts, axis=0)
    if team == 4:
        crossing = crossing + [swap_dp(after(farthest, *kv_terms), 3)]
    attended_all = jnp.concatenate([part[:, :D] for part in crossing], axis=0)
    resid_share = jnp.concatenate([part[:, D:] for part in crossing], axis=0)
    column_shape = (MODEL_BLOCKS, team, piece, model_share)
    out_terms = contract_first(attended_all, resid_share).astype(LOW).reshape(column_shape)
    early_terms = place_more(
        "place_out",
        block_owner[OUT_AT:GATE_AT],
        slots[OUT_AT:GATE_AT],
        (out_terms,),
        ((MODEL_BLOCKS, True),),
        cut_terms[:-1],
        targets[:-1],
        team,
    )
    query_terms = contract_first(hidden_one_all, grad_query_share).astype(LOW)
    key_value_sums = finish_earlier(key_value_sums, early_terms, query_terms)
    grad_keys = apply_rotation(
        key_value_sums[:, :, :KEY_VALUE_WIDTH].reshape(
            sequence_count, segment_rows, KEY_VALUE_HEADS, HEAD_WIDTH
        ),
        cosine_rows,
        -sine_rows,
    ).reshape(token_count, KEY_VALUE_WIDTH)
    grad_values = key_value_sums[:, :, KEY_VALUE_WIDTH:].reshape(token_count, KEY_VALUE_WIDTH)
    grad_kv = (
        jnp.concatenate([grad_keys, grad_values], axis=1)
        .astype(LOW)
        .reshape(token_count, 2 * KV_BLOCKS, team, piece)
        .transpose(0, 2, 1, 3)
        .reshape(token_count, 2 * KEY_VALUE_WIDTH)
    )
    grad_kv_share = jnp.concatenate(exchange_parts(cut_up(grad_kv, 2 * kv_share)), axis=0)

    kv_weight_terms = contract_first(grad_kv_share, hidden_one_all).astype(LOW)
    attention_terms = [
        query_terms.reshape(column_shape),
        kv_weight_terms.reshape(2 * KV_BLOCKS, piece, D),
        out_terms,
    ]
    early_terms = place_more(
        "place_query",
        block_owner[:OUT_AT],
        slots[:OUT_AT],
        attention_terms[:2],
        ((MODEL_BLOCKS, True), (2 * KV_BLOCKS, False)),
        early_terms,
        targets[:-1],
        team,
    )

    def nothing_spilled():
        return jnp.zeros((late_slots, piece, D), LOW)

    def sums_spilled():
        by_columns = [
            attention_terms[k].transpose(0, 2, 1, 3).reshape(MODEL_BLOCKS, piece, D) for k in (0, 2)
        ]
        found = jnp.concatenate([by_columns[0], attention_terms[1], by_columns[1]], axis=0)
        every_slot = jnp.arange(slot_count * lax.axis_size("grp"), dtype=jnp.int32)
        hits = (block_owner * slot_count + slots)[None, :GATE_AT] == every_slot[:, None]
        which = jnp.sum(jnp.where(hits, block_order[None, :GATE_AT], 0), axis=1)
        spread = jnp.where(
            jnp.any(hits, axis=1)[:, None, None],
            jnp.take(found, which, axis=0, mode="clip"),
            jnp.zeros((), LOW),
        )
        extra = lax.psum_scatter(spread, "grp", scatter_dimension=0, tiled=True)
        return extra[early_slots:]

    late_extra = lax.cond(
        after(spills, late_sums, early_terms[0]), sums_spilled, nothing_spilled
    )

    spilled = spills & my_attention[early_slots:]
    late_sums = jnp.where(spilled[:, None, None], late_extra, late_sums)
    late_half = late_slots // 2
    states = (weight_master, weight_first, weight_second)

    def query_gradient(share):
        return contract_rows(share, query_share) + plain_dot(grad_kv_share, kv_rows)

    def finish_input(grad_hone):
        scaled_one = grad_hone * gain_one
        spread = jnp.mean(scaled_one * normed_one, axis=-1, keepdims=True)
        input_grad = grad_resid + root_one * (scaled_one - normed_one * spread)
        gain_terms = [
            jnp.sum(grad_hone * normed_one, axis=0), jnp.sum(grad_htwo * normed_two, axis=0)
        ]
        return (
            input_grad.astype(LOW).reshape(sequence_count, segment_rows, D),
            jnp.stack(gain_terms),
        )

    def finish_output(sent):
        output = residual + add_up(sent[0], sent[1:])
        return (
            jnp.where(valid_rows, output, 0.0)
            .astype(LOW)
            .reshape(sequence_count, segment_rows, D)
        )

    def update(parts, low, updated):
        return adamw_slots(kinds, *states, parts, low, updated)

    if is_line() and team == 4:
        tie = lax.optimization_barrier

        def as_slots(rows):
            return rows.reshape(-1, piece, D)

        def join(*pieces):
            return jnp.concatenate([as_slots(rows) for rows in pieces], axis=0)

        kept, given = early_terms
        given, late_sums, grad_query_share = tie((given, late_sums, grad_query_share))
        swapped = core_swap(given)
        first, second = late_sums[:late_half], late_sums[late_half:]
        first_near = near_far(first)
        grad_hone = query_gradient(grad_query_share)
        swapped, grad_hone = tie((swapped, grad_hone))
        sums = (kept.astype(FULL) + swapped.astype(FULL)).astype(LOW)
        sums = sums.reshape(4, early_slots, piece, D)
        up, down = line_terms(sums, 1, None, None)
        upward, downward = line_step(up, down, 1)
        own, near, far, cross = split_parts(grad_hone)
        near, far, cross = near.astype(LOW), far.astype(LOW), cross.astype(LOW)
        rows = token_count // 2
        step = late_half // 2
        first_near, near, far, cross, _, _ = tie((first_near, near, far, cross, up, down))
        by_near = swap_dp(join(first_near[1][:step], near[:rows], cross[:rows]), 1)
        by_far = swap_dp(join(first_near[0][step:], far[rows:], cross[rows:]), 2)
        down_sent, near, far = tie((down_sent, near, far))
        layer_output = finish_output(down_sent)
        upward, downward, near, far, layer_output = tie(
            (upward, downward, near, far, layer_output)
        )
        up, down = line_terms(sums, 2, upward, downward)
        upward, downward = line_step(up, down, 2)
        by_near, by_far, near, far, _, _ = tie((by_near, by_far, near, far, up, down))
        first_cross = join(by_near[:step], by_far[: late_half - step])
        near_first, by_way_near = split_rows(by_near[step:].reshape(-1, D), rows)
        far_second, by_way_far = split_rows(by_far[late_half - step :].reshape(-1, D), rows)
        far_first = (far[:rows].astype(FULL) + by_way_near.astype(FULL)).astype(LOW)
        near_second = (near[rows:].astype(FULL) + by_way_far.astype(FULL)).astype(LOW)
        by_near = swap_dp(join(second, near_second), 1)
        by_far = swap_dp(join(second, far_first), 2)
        upward, downward, near_second, far_first = tie(
            (upward, downward, near_second, far_first)
        )
        up, down = line_terms(sums, 3, upward, downward)
        upward, downward = line_step(up, down, 3)
        by_near, by_far, _, _ = tie((by_near, by_far, up, down))
        second_near = [by_near[:late_half], by_far[:late_half]]
        second_cross = cross_of(*second_near)
        parts, second_near = tie(([first, *first_near, first_cross], second_near))
        updated = update(parts, early_slots, None)
        upward, downward, updated = tie((upward, downward, updated))
        early_sums = of_chip(sums, member // 2).astype(FULL)
        early_sums = (early_sums + upward.astype(FULL) + downward.astype(FULL)).astype(LOW)
        cut = early_slots // 2
        halves = [early_sums[:cut], early_sums[cut:]]
        near_front, near_back = [near_far(half) for half in halves]
        parts = [second, *second_near, jnp.concatenate(second_cross, axis=0)]
        parts, updated, halves = tie((parts, updated, halves))
        updated = update(parts, early_slots + late_half, updated)
        near_front, near_back, updated = tie((near_front, near_back, updated))
        cross_front, cross_back = cross_of(*near_front), cross_of(*near_back)
        near_first, by_far, near_front, near_back = tie((near_first, by_far, near_front, near_back))
        grad_hone = own + jnp.concatenate(
            [
                near_first.astype(FULL) + by_far[late_half:].reshape(rows, D).astype(FULL),
                by_near[late_half:].reshape(rows, D).astype(FULL) + far_second.astype(FULL),
            ]
        )
        input_grad, gain_terms = finish_input(grad_hone)
        cross_front, gain_terms, input_grad, updated = tie(
            (cross_front, gain_terms, input_grad, updated)
        )
        others = [swap_dp(gain_terms, distance) for distance in range(1, team)]
        parts = [halves[0], *near_front, jnp.concatenate(cross_front, axis=0)]
        updated = update(parts, 0, updated)
        gain_terms, others, cross_back, updated = tie((gain_terms, others, cross_back, updated))
        gain_terms = add_up(gain_terms, others)
        other = core_swap(gain_terms)
        gain_terms, other, cross_back = tie((gain_terms, other, cross_back))
        gain_terms = gain_terms + other
        around = [
            lax.ppermute(gain_terms, "grp", [(a, (a + 2 * turn_by) % 8) for a in range(8)])
            for turn_by in range(1, 4)
        ]
        parts = [halves[1], *near_back, jnp.concatenate(cross_back, axis=0)]
        parts, gain_terms, updated = tie((parts, gain_terms, updated))
        updated = update(parts, cut, updated)
        gain_grad = add_up(gain_terms, around)
    else:
        updated = update(gather_parts(late_sums), early_slots, None)
        early_sums = lax.psum_scatter(early_terms[0], "grp", scatter_dimension=0, tiled=True)
        updated = update(gather_parts(early_sums), 0, updated)
        input_grad, gain_terms = finish_input(scatter_dp(query_gradient(grad_query_share)))
        gain_grad = lax.psum(gain_terms, ("dp", "grp"))
        layer_output = finish_output(down_sent)
    new_master, new_first, new_second, weight_copy = updated

    share_width = gain_master.shape[1]
    gain_share = lax.dynamic_slice_in_dim(gain_grad, member * share_width, share_width, 1)
    new_gain, new_gain_first, new_gain_second = adamw(
        gain_master, gain_first, gain_second, gain_share, GAIN_RATE, 0.0
    )
    return (
        layer_output,
        input_grad,
        new_master,
        new_first,
        new_second,
        weight_copy,
        new_gain,
        new_gain_first,
        new_gain_second,
    )


def solution(mesh):
    return jax.shard_map(
        per_device,
        mesh=mesh,
        in_specs=(
            P("dp", "grp", None),
            P("dp", "grp", None),
            P("dp"),
            P(),
            P("grp", None, None),
            P("grp", None, None),
            P("grp", None, None),
            P(None, "grp"),
            P(None, "grp"),
            P(None, "grp"),
        ),
        out_specs=(
            P("dp", "grp", None),
            P("dp", "grp", None),
            P("grp", None, None),
            P("grp", None, None),
            P("grp", None, None),
            P("grp", None, None),
            P(None, "grp"),
            P(None, "grp"),
            P(None, "grp"),
        ),
        check_vma=False,
    )
```
